32 devices in a mesh: dp: 16 (over z, y, x), rep: 2 (over core).
Axes of the slice: x: 2, y: 2, z: 4, core: 2. Of those that a mesh axis runs over, the one named last changes fastest.
Arguments:
- image_in: bfloat16 [4096, 50, 384], P(('dp', 'rep')), may hold values from -6 to 6
- img_gains: float32 [2, 384], replicated, may hold values from 0.5 to 1.5
- img_shifts: float32 [2, 384], replicated, may hold values from -1 to 1
- img_qkv: bfloat16 [384, 1152], replicated, may hold values from -0.3125 to 0.3125
- img_out: bfloat16 [384, 384], replicated, may hold values from -0.875 to 0.875
- img_up: bfloat16 [384, 1536], replicated, may hold values from -0.3125 to 0.3125
- img_down: bfloat16 [1536, 384], replicated, may hold values from -0.15625 to 0.15625
- text_in: bfloat16 [4096, 16, 384], P(('dp', 'rep')), may hold values from -6 to 6
- lengths: int32 [4096], P(('dp', 'rep')), may hold values from 2 to 16
- valid: int32 [4096], P(('dp', 'rep')), may hold values from 0 to 1, as said below
- txt_gains: float32 [2, 384], replicated, may hold values from 0.5 to 1.5
- txt_shifts: float32 [2, 384], replicated, may hold values from -1 to 1
- txt_qkv: bfloat16 [384, 1152], replicated, may hold values from -0.3125 to 0.3125
- txt_out: bfloat16 [384, 384], replicated, may hold values from -0.625 to 0.625
- txt_up: bfloat16 [384, 1536], replicated, may hold values from -0.3125 to 0.3125
- txt_down: bfloat16 [1536, 384], replicated, may hold values from -0.15625 to 0.15625
- log_scale: float32 [], replicated, may hold values from 4.2 to 4.6
Outputs:
- loss: float32 [], replicated
- grad_txt_gains: float32 [2, 384], replicated
- grad_txt_shifts: float32 [2, 384], replicated
- grad_txt_qkv: float32 [384, 1152], replicated
- grad_txt_out: float32 [384, 384], replicated
- grad_txt_up: float32 [384, 1536], replicated
- grad_txt_down: float32 [1536, 384], replicated
- grad_log_scale: float32 [], replicated
- grad_text_in: float32 [4096, 16, 384], P(('dp', 'rep'))
The draws below stay inside these ranges and needn't reach their ends.
Inputs may be any that keep to these rules, and one draw needn't show every extreme that they name: In each aligned block of 128 slots (the slots of one device) the valid pairs come first, and there are 128, 64 or 32 of them.
All inputs are finite; a program needn't handle non-finite values.
Results may differ from the reference program's by a relative error of at most 0.012.
The reference program's roundings to bfloat16 on the way count: a program that leaves them out, or rounds other values in their place, can miss the bound.
Values may be sent and summed in bfloat16 or wider, within the bound.
No kernel may reach another device: no remote copies, remote signals or barrier semaphores. Data moves between devices by JAX's collectives and lax.ppermute only.
A program may use at most 320 MiB of HBM per device.

```python
import math
import jax
import jax.numpy as jnp
from jax import lax

D = 384
HEAD = 64
FF = 1536
IMG = 50
TXT = 16
PAIR_DEV = 128
PAIRS = 4096


def draw_valid(key, part):
    key = jax.random.fold_in(key, 11)
    block_count = PAIRS // PAIR_DEV
    chosen_kind = jax.random.randint(key, (block_count,), 0, 4)
    divisor = jnp.where(chosen_kind == 3, 4, jnp.where(chosen_kind == 2, 2, 1))
    counts = PAIR_DEV // divisor
    slot_ids = jnp.arange(PAIR_DEV)
    return (slot_ids[None, :] < counts[:, None]).astype(jnp.int32).reshape(PAIRS)


def plant(entries, rng, low, top_value):
    extent = entries.shape
    spot = [jax.random.randint(jax.random.fold_in(rng, axis), (), 0, extent[axis]) for axis in range(len(extent))]
    entries = entries.at[tuple(spot)].set(low)
    longest = extent.index(max(extent))
    spot[longest] = (spot[longest] + 1) % extent[longest]
    return entries.at[tuple(spot)].set(top_value)


def block_scale(stream_key, extent, split, least, largest):
    level, own = 1.0, jax.random.fold_in(stream_key, 6)
    for dim, blocks in split:
        heights = jnp.exp(jax.random.uniform(jax.random.fold_in(own, dim), (blocks,), jnp.float32, least / len(split), largest / len(split)))
        level = level * jnp.repeat(heights, extent[dim] // blocks).reshape([-1 if axis == dim else 1 for axis in range(len(extent))])
    return level


def bell_draw(stream_key, dims, scale, reach, split=(), held_as=jnp.bfloat16):
    loudness = block_scale(stream_key, dims, split, -0.22, 0.18) if split else 1.0
    entries = jax.random.normal(stream_key, dims, jnp.float32) * scale * loudness
    return jnp.minimum(jnp.maximum(entries, -reach), reach).astype(held_as)


def setup_inputs(seed: int = 0) -> dict:
    key_of = jax.random.split(jax.random.key(seed), 18)
    return {
        "image_in": bell_draw(key_of[0], (PAIRS, IMG, D), 1.0, 6.0, ((0, 32),)),
        "img_gains": jnp.clip(1.0 + 0.1 * jax.random.normal(key_of[1], (2, D), jnp.float32), 0.5, 1.5),
        "img_shifts": bell_draw(key_of[2], (2, D), 0.2, 1.0, (), jnp.float32),
        "img_qkv": bell_draw(key_of[3], (D, 3 * D), D ** -0.5, 0.3125),
        "img_out": bell_draw(key_of[4], (D, D), (D // 8) ** -0.5, 0.875),
        "img_up": bell_draw(key_of[5], (D, FF), D ** -0.5, 0.3125),
        "img_down": bell_draw(key_of[6], (FF, D), FF ** -0.5, 0.15625),
        "text_in": bell_draw(key_of[7], (PAIRS, TXT, D), 1.0, 6.0, ((0, 32),)),
        "lengths": plant(jax.random.randint(key_of[8], (PAIRS,), 2, TXT + 1), jax.random.fold_in(key_of[8], 1), 2, TXT).astype(jnp.int32),
        "valid": draw_valid(jax.random.fold_in(key_of[17], 71), 0),
        "txt_gains": jnp.clip(1.0 + 0.1 * jax.random.normal(key_of[10], (2, D), jnp.float32), 0.5, 1.5),
        "txt_shifts": bell_draw(key_of[11], (2, D), 0.2, 1.0, (), jnp.float32),
        "txt_qkv": bell_draw(key_of[12], (D, 3 * D), D ** -0.5, 0.3125),
        "txt_out": bell_draw(key_of[13], (D, D), (D // 4) ** -0.5, 0.625),
        "txt_up": bell_draw(key_of[14], (D, FF), D ** -0.5, 0.3125),
        "txt_down": bell_draw(key_of[15], (FF, D), FF ** -0.5, 0.15625),
        "log_scale": jnp.clip(jax.random.uniform(key_of[16], (), jnp.float32, 4.2, 4.6), 4.2, 4.6),
    }


@jax.custom_vjp
def low(v):
    return lax.optimization_barrier(v.astype(jnp.bfloat16)).astype(jnp.float32)

@jax.custom_vjp
def low_back(v):
    return v

def low_keep(v):
    return (low(v), None)

def low_pass(kept, grad):
    return (grad,)

def back_keep(v):
    return (v, None)

def back_low(kept, grad):
    return (low(grad),)
low.defvjp(low_keep, low_pass)
low_back.defvjp(back_keep, back_low)

def product(form, left_arr, right_arr):
    return jnp.einsum(form, left_arr, right_arr, precision=lax.Precision.HIGHEST)

def layer_norm(inputs, gain, shift):
    averaged = lax.optimization_barrier(jnp.mean(inputs, -1, keepdims=True))
    centred = inputs - averaged
    variance = lax.optimization_barrier(jnp.mean(centred * centred, -1, keepdims=True))
    return centred * lax.rsqrt(variance + 1e-06) * gain + shift

def softmax_rows(scores):
    top_val = lax.optimization_barrier(jnp.max(scores, -1, keepdims=True))
    expsum = jnp.exp(scores - top_val)
    return expsum / lax.optimization_barrier(jnp.sum(expsum, -1, keepdims=True))

def gelu_fn(inputs):
    return jax.nn.gelu(inputs, approximate=True)

def block_forward(inputs, gain_rows, shift_rows, w_qkv, w_out, w_up, w_down, key_ok):
    sequences, positions, features = inputs.shape
    heads_count = features // HEAD
    normed_one = low(layer_norm(inputs, gain_rows[0], shift_rows[0]))
    project = low(low_back(product('spd,de->spe', normed_one, w_qkv)))
    project = project.reshape(sequences, positions, 3, heads_count, HEAD)
    queries = project[:, :, 0]
    key_rows = project[:, :, 1]
    values = project[:, :, 2]
    scores = low_back(HEAD ** (-0.5) * product('sqhc,skhc->shqk', queries, key_rows))
    if key_ok is not None:
        scores = jnp.where(key_ok[:, None, None, :], scores, -1000000000.0)
    weights_low = low(softmax_rows(scores))
    attended = low(low_back(product('shqk,skhc->sqhc', weights_low, values)))
    attended = attended.reshape(sequences, positions, features)
    middle = inputs + low_back(product('spd,de->spe', attended, w_out))
    normed_two = low(layer_norm(middle, gain_rows[1], shift_rows[1]))
    before = low_back(product('spd,df->spf', normed_two, w_up))
    hidden = low(gelu_fn(before))
    return middle + low_back(product('spf,fd->spd', hidden, w_down))

def embed_rows(output, tok_weights):
    pooled = lax.optimization_barrier(jnp.sum(output * tok_weights[:, :, None], 1))
    return pooled * lax.rsqrt(lax.optimization_barrier(jnp.sum(pooled * pooled, -1, keepdims=True)) + 1e-06)

def masked_lse(scores, pair_mask):
    masked = jnp.where(pair_mask[None, :] > 0, scores, -1e+30)
    top_val = lax.optimization_barrier(jnp.max(masked, -1, keepdims=True))
    return top_val[:, 0] + jnp.log(lax.optimization_barrier(jnp.sum(jnp.exp(masked - top_val), -1)))

def reference(image_in, img_gains, img_shifts, img_qkv, img_out, img_up, img_down, text_in, lengths, valid, txt_gains, txt_shifts, txt_qkv, txt_out, txt_up, txt_down, log_scale):
    image_group = math.gcd(PAIRS, 64)
    text_group = math.gcd(PAIRS, 256)
    row_block = math.gcd(PAIRS, 1024)
    image_qkv = img_qkv.astype(jnp.float32)
    image_out = img_out.astype(jnp.float32)
    image_up = img_up.astype(jnp.float32)
    image_down = img_down.astype(jnp.float32)

    def image_block(pieces):
        output = block_forward(pieces.astype(jnp.float32), img_gains, img_shifts, image_qkv, image_out, image_up, image_down, None)
        flat_weights = jnp.full(output.shape[:2], 1.0 / IMG, jnp.float32)
        return low(embed_rows(output, flat_weights))
    image_emb = lax.map(image_block, image_in.reshape(PAIRS // image_group, image_group, IMG, D)).reshape(PAIRS, D)
    slot_ids = jnp.arange(TXT)
    key_ok = slot_ids[None, :] < lengths[:, None]
    tok_weights = key_ok.astype(jnp.float32) / lengths[:, None].astype(jnp.float32)
    pair_mask = valid.astype(jnp.float32)

    def forward(params, text_x):
        gain_rows, shift_rows, w_qkv, w_out, w_up, w_down, log_value = params

        def text_block(pieces):
            text_part, ok_part, weight_part = pieces
            output = block_forward(text_part, gain_rows, shift_rows, w_qkv, w_out, w_up, w_down, ok_part)
            return low(embed_rows(output, weight_part))
        groups = PAIRS // text_group
        text_emb = lax.map(jax.checkpoint(text_block), (text_x.reshape(groups, text_group, TXT, D), key_ok.reshape(groups, text_group, TXT), tok_weights.reshape(groups, text_group, TXT))).reshape(PAIRS, D)
        logit_scale = jnp.exp(log_value)

        def lse_rows(left_all, right_all):

            def one_block(left_part):
                return masked_lse(low_back(logit_scale * product('id,jd->ij', left_part, right_all)), pair_mask)
            return lax.map(jax.checkpoint(one_block), left_all.reshape(PAIRS // row_block, row_block, D)).reshape(PAIRS)
        row_lse = lse_rows(text_emb, image_emb)
        col_lse = lse_rows(image_emb, text_emb)
        diagonal = logit_scale * lax.optimization_barrier(jnp.sum(text_emb * image_emb, -1))
        pair_total = jnp.sum(pair_mask)
        return jnp.sum(pair_mask * (row_lse + col_lse - 2.0 * diagonal)) / (2.0 * pair_total)
    params = (txt_gains, txt_shifts, txt_qkv.astype(jnp.float32), txt_out.astype(jnp.float32), txt_up.astype(jnp.float32), txt_down.astype(jnp.float32), log_scale)
    loss, pull = jax.vjp(forward, params, text_in.astype(jnp.float32))
    param_grads, input_grad = pull(jnp.ones((), jnp.float32))
    return (loss, param_grads[0], param_grads[1], param_grads[2], param_grads[3], param_grads[4], param_grads[5], param_grads[6], input_grad)
```

```python
import functools
import jax
import jax.numpy as jnp
from jax import lax
from jax.experimental import pallas as pl
from jax.experimental.pallas import tpu as pltpu
from jax.sharding import PartitionSpec as P

HEAD = 64
LANES = 128
f32 = jnp.float32
bf16 = jnp.bfloat16
GELU_C = 0.7978845608028654
GELU_A = 0.044715
SHIFT = 50.0
SAFE = 80.0
VMEM = 48 * 1024 * 1024


def dot(a, b):
    return jnp.dot(a, b, preferred_element_type=f32)


def dot_nt(a, b):
    return lax.dot_general(a, b, (((1,), (1,)), ((), ())), preferred_element_type=f32)


def dot_tn(a, b):
    return lax.dot_general(a, b, (((0,), (0,)), ((), ())), preferred_element_type=f32)


def norm_parts(x):
    mu = jnp.mean(x, -1, keepdims=True)
    c = x - mu
    rstd = lax.rsqrt(jnp.mean(c * c, -1, keepdims=True) + 1e-6)
    return c * rstd, rstd


def whole(a):
    return pl.BlockSpec(a.shape, lambda *_: (0,) * a.ndim)


def params():
    return pltpu.CompilerParams(vmem_limit_bytes=VMEM)


def split_bf16(v):
    hi = v.astype(bf16)
    return hi, (v - hi.astype(f32)).astype(bf16)


def image_kernel(
    seqs, tokens, x_ref, gains_ref, shifts_ref, wqkv_ref, wo_ref, wup_ref, wdown_ref, out_ref,
    xs, qkv, att, sc, ec, hs, ms,
):
    pad = -(-tokens // 8) * 8
    rows, pair = seqs * pad, 2 * pad
    step = pl.program_id(0)
    d, ff = x_ref.shape[2], wup_ref.shape[1]
    hp = d // LANES

    @pl.when(step == 0)
    def _():
        xs[...] = jnp.zeros_like(xs)

    for b in range(seqs):
        xs[b * pad : b * pad + tokens, :] = x_ref[b].astype(f32)
    x = xs[...]
    n1 = (norm_parts(x)[0] * gains_ref[0:1, :] + shifts_ref[0:1, :]).astype(bf16)
    qkv[:, :d] = (dot(n1, wqkv_ref[:, :d]) * HEAD**-0.5).astype(bf16)
    qkv[:, d:] = dot(n1, wqkv_ref[:, d:]).astype(bf16)

    low = lax.broadcasted_iota(jnp.int32, (pair, LANES), 1) < HEAD
    key_lane = lax.broadcasted_iota(jnp.int32, (pair, 2 * pair), 1)
    query_row = lax.broadcasted_iota(jnp.int32, (pair, 2 * pair), 0)
    first_head = key_lane < pair
    key_row = jnp.where(first_head, key_lane, key_lane - pair)
    second_image = key_row >= pad
    key_pos = jnp.where(second_image, key_row - pad, key_row)
    bias = jnp.where((key_pos < tokens) & (second_image == (query_row >= pad)), 0.0, -1e30)
    zero, one = jnp.zeros((pair, LANES), bf16), jnp.ones((pair, LANES), bf16)
    ones = jnp.concatenate([jnp.where(low, one, zero), jnp.where(low, zero, one)], 0)
    big = jnp.zeros((pair, 2 * pair), f32)
    for b in range(seqs // 2):
        r = slice(b * pair, (b + 1) * pair)
        for p in range(hp):
            q = qkv[r, p * LANES : (p + 1) * LANES]
            k = qkv[r, d + p * LANES : d + (p + 1) * LANES]
            stacked = jnp.concatenate([jnp.where(low, k, zero), jnp.where(low, zero, k)], 0)
            s = dot_nt(q, stacked)
            big = jnp.maximum(big, jnp.abs(s))
            sc[b * hp + p] = s
    safe = jnp.max(big) < SAFE

    @pl.when(safe)
    def _():
        for i in range(seqs // 2 * hp):
            ec[i] = jnp.exp(sc[i] + bias).astype(bf16)

    @pl.when(jnp.logical_not(safe))
    def _():
        @pl.loop(0, seqs // 2 * hp)
        def _(i):
            s = sc[i] + bias
            top0 = jnp.max(jnp.where(first_head, s, -2e30), -1, keepdims=True)
            top1 = jnp.max(jnp.where(first_head, -2e30, s), -1, keepdims=True)
            ec[i] = jnp.exp(s - jnp.where(first_head, top0, top1)).astype(bf16)

    for b in range(seqs // 2):
        r = slice(b * pair, (b + 1) * pair)
        for p in range(hp):
            v = qkv[r, 2 * d + p * LANES : 2 * d + (p + 1) * LANES]
            stacked = jnp.concatenate([jnp.where(low, v, zero), jnp.where(low, zero, v)], 0)
            o = dot(ec[b * hp + p], jnp.concatenate([stacked, ones], 1))
            att[r, p * LANES : (p + 1) * LANES] = (o[:, :LANES] / o[:, LANES:]).astype(bf16)
    mid = x + dot(att[...], wo_ref[...])
    keep = lax.broadcasted_iota(jnp.int32, (seqs, pad, 1), 1) < tokens
    keep = jnp.where(keep, 1.0, 0.0).reshape(rows, 1)
    at = pl.ds(pl.multiple_of(step * seqs, seqs), seqs)
    ms[at, :] = jnp.sum((mid * keep).reshape(seqs, pad, d), 1)
    n2 = ((norm_parts(mid)[0] * gains_ref[1:2, :] + shifts_ref[1:2, :]) * keep).astype(bf16)
    chunk = 512
    for c in range(0, ff, chunk):
        v = dot(n2, wup_ref[:, c : c + chunk])
        t = jnp.tanh(v * (GELU_C + (GELU_C * GELU_A) * (v * v)))
        h = (0.5 * v) * (1.0 + t)
        hs[at, c : c + chunk] = jnp.sum(h.reshape(seqs, pad, chunk), 1)

    @pl.when(step == pl.num_programs(0) - 1)
    def _():
        hi, lo = split_bf16(hs[...] * (1.0 / tokens))
        u = ms[...] * (1.0 / tokens) + dot(hi, wdown_ref[...]) + dot(lo, wdown_ref[...])
        out_ref[...] = (u * lax.rsqrt(jnp.sum(u * u, -1, keepdims=True) + 1e-6)).astype(bf16)


def image_embed(x, gains, shifts, wqkv, wo, wup, wdown, start, count, seqs=16):
    tokens, d = x.shape[1:]
    ff = wup.shape[1]
    pad = -(-tokens // 8) * 8
    tiles = seqs // 2 * (d // LANES)
    first = start // seqs
    return pl.pallas_call(
        functools.partial(image_kernel, seqs, tokens),
        grid=(count // seqs,),
        in_specs=[pl.BlockSpec((seqs, tokens, d), lambda i: (i + first, 0, 0))]
        + [whole(a) for a in (gains, shifts, wqkv, wo, wup, wdown)],
        out_specs=pl.BlockSpec((count, d), lambda i: (0, 0)),
        out_shape=jax.ShapeDtypeStruct((count, d), bf16),
        scratch_shapes=[
            pltpu.VMEM((seqs * pad, d), f32),
            pltpu.VMEM((seqs * pad, 3 * d), bf16),
            pltpu.VMEM((seqs * pad, d), bf16),
            pltpu.VMEM((tiles, 2 * pad, 4 * pad), f32),
            pltpu.VMEM((tiles, 2 * pad, 4 * pad), bf16),
            pltpu.VMEM((count, ff), f32),
            pltpu.VMEM((count, d), f32),
        ],
        compiler_params=params(),
        cost_estimate=pl.CostEstimate(
            flops=2 * count * pad * d * (4 * d + ff), bytes_accessed=2 * count * tokens * d, transcendentals=0
        ),
        name="image_block",
    )(x, gains, shifts, wqkv, wo, wup, wdown)


def stack_heads(a, low, zero):
    return jnp.concatenate([jnp.where(low, a, zero), jnp.where(low, zero, a)], 0)


def text_forward_kernel(
    txt, x_ref, len_ref, key_ref, gains_ref, shifts_ref, wqkv_ref, wo_ref, wup_ref, wdown_ref,
    xhat1_ref, rstd1_ref, n1_ref, qkv_ref, probs_ref, att_ref, xhat2_ref, rstd2_ref, n2_ref, slope_ref,
    hpool_ref, u_ref, ms,
):
    step = pl.program_id(0)
    rows, d = x_ref.shape
    ff = wup_ref.shape[1]
    seqs = rows // txt
    x = x_ref[...].astype(f32)
    xhat1, rstd1 = norm_parts(x)
    xhat1_ref[...] = xhat1.astype(bf16)
    rstd1_ref[...] = rstd1
    n1 = (xhat1 * gains_ref[0:1, :] + shifts_ref[0:1, :]).astype(bf16)
    n1_ref[...] = n1
    qkv_ref[:, :d] = (dot(n1, wqkv_ref[:, :d]) * HEAD**-0.5).astype(bf16)
    qkv_ref[:, d:] = dot(n1, wqkv_ref[:, d:]).astype(bf16)
    low = lax.broadcasted_iota(jnp.int32, (LANES, LANES), 1) < HEAD
    same = (
        lax.broadcasted_iota(jnp.int32, (LANES, LANES), 0) // txt
        == lax.broadcasted_iota(jnp.int32, (LANES, LANES), 1) // txt
    )
    zero = jnp.zeros((LANES, LANES), bf16)
    for g in range(rows // LANES):
        r = slice(g * LANES, (g + 1) * LANES)
        bias = jnp.where(same & (key_ref[0, g : g + 1, :] > 0), 0.0, -1e30)
        for p in range(d // LANES):
            c = slice(p * LANES, (p + 1) * LANES)
            q = qkv_ref[r, p * LANES : (p + 1) * LANES]
            k = qkv_ref[r, d + p * LANES : d + (p + 1) * LANES]
            v = qkv_ref[r, 2 * d + p * LANES : 2 * d + (p + 1) * LANES]
            s = dot_nt(q, stack_heads(k, low, zero))
            halves = []
            for h in range(2):
                sh = s[:, h * LANES : (h + 1) * LANES] + bias
                e = jnp.exp(sh - jnp.max(sh, -1, keepdims=True))
                halves.append(e / jnp.sum(e, -1, keepdims=True))
            probs = jnp.concatenate(halves, 1).astype(bf16)
            probs_ref[g * (d // LANES) + p] = probs
            att_ref[r, c] = dot(probs, stack_heads(v, low, zero)).astype(bf16)
    mid = x + dot(att_ref[...], wo_ref[...])
    xhat2, rstd2 = norm_parts(mid)
    xhat2_ref[...] = xhat2.astype(bf16)
    rstd2_ref[...] = rstd2
    pos = lax.broadcasted_iota(jnp.int32, (rows, 1), 0) % txt
    keep = jnp.where(pos.astype(f32) < len_ref[...], 1.0, 0.0)
    n2 = ((xhat2 * gains_ref[1:2, :] + shifts_ref[1:2, :]) * keep).astype(bf16)
    n2_ref[...] = n2
    at = pl.ds(pl.multiple_of(step * seqs, seqs), seqs)
    ms[at, :] = jnp.sum((mid * keep).reshape(seqs, txt, d), 1)
    chunk = 512
    for c in range(0, ff, chunk):
        v = dot(n2, wup_ref[:, c : c + chunk])
        v2 = v * v
        t = jnp.tanh(v * (GELU_C + (GELU_C * GELU_A) * v2))
        half = 0.5 + 0.5 * t
        h = v * half
        slope = half + h * (1.0 - t) * (GELU_C + (3.0 * GELU_C * GELU_A) * v2)
        slope_ref[:, c : c + chunk] = (slope * keep).astype(bf16)
        hpool_ref[at, c : c + chunk] = jnp.sum(h.reshape(seqs, txt, chunk), 1)

    @pl.when(step == pl.num_programs(0) - 1)
    def _():
        hi, lo = split_bf16(hpool_ref[...])
        pooled = ms[...] + dot(hi, wdown_ref[...]) + dot(lo, wdown_ref[...])
        u_ref[...] = pooled


def text_forward(x, row_len, key_ok, gains, shifts, wqkv, wo, wup, wdown, txt, rows=256):
    total, d = x.shape
    ff = wup.shape[1]
    pairs = total // txt
    hp = d // LANES
    block = lambda *tail: pl.BlockSpec((rows,) + tail, lambda i: (i,) + (0,) * len(tail))
    shape = jax.ShapeDtypeStruct
    key3 = key_ok.reshape(total // rows, rows // LANES, LANES)
    return pl.pallas_call(
        functools.partial(text_forward_kernel, txt),
        grid=(total // rows,),
        in_specs=[block(d), block(1), pl.BlockSpec((1, rows // LANES, LANES), lambda i: (i, 0, 0))]
        + [whole(a) for a in (gains, shifts, wqkv, wo, wup, wdown)],
        out_specs=[
            block(d), block(1), block(d), block(3 * d),
            pl.BlockSpec((rows // LANES * hp, LANES, 2 * LANES), lambda i: (i, 0, 0)),
            block(d), block(d), block(1), block(d), block(ff),
            pl.BlockSpec((pairs, ff), lambda i: (0, 0)), pl.BlockSpec((pairs, d), lambda i: (0, 0)),
        ],
        out_shape=[
            shape((total, d), bf16), shape((total, 1), f32), shape((total, d), bf16), shape((total, 3 * d), bf16),
            shape((total // LANES * hp, LANES, 2 * LANES), bf16),
            shape((total, d), bf16), shape((total, d), bf16), shape((total, 1), f32), shape((total, d), bf16),
            shape((total, ff), bf16), shape((pairs, ff), f32), shape((pairs, d), f32),
        ],
        scratch_shapes=[pltpu.VMEM((pairs, d), f32)],
        compiler_params=params(),
        cost_estimate=pl.CostEstimate(
            flops=2 * total * d * (4 * d + ff), bytes_accessed=2 * total * (12 * d + ff), transcendentals=0
        ),
        name="text_forward",
    )(x, row_len, key3, gains, shifts, wqkv, wo, wup, wdown)


def scores_kernel(place_ref, text_ref, mask_ref, a_ref, b_ref, col_ref, scale_ref, s_ref, all_ref, col_out, row_out):
    step = pl.program_id(0)
    group = a_ref.shape[0]
    half = a_ref.shape[1]
    inner = place_ref[1]
    scale = scale_ref[0]
    mask = mask_ref[...]

    @pl.when(step == 0)
    def _():
        row_out[...] = jnp.zeros_like(row_out)

    for k in range(group):
        at = lax.bitwise_xor(k, inner)
        cols = slice(k * 2 * half, (k + 1) * 2 * half)
        images = jnp.concatenate([a_ref[at], b_ref[at]], 0)
        all_ref[cols, :] = images
        s = scale * dot_nt(text_ref[...], images)
        s_ref[:, cols] = s
        up = jnp.exp(s - SHIFT)
        down = jnp.exp(jnp.minimum(s, 0.0) + SHIFT)
        col_out[0:1, cols] = jnp.sum(up * mask, 0, keepdims=True)
        col_out[1:2, cols] = jnp.sum(down * mask, 0, keepdims=True)
        okay = col_ref[0:1, cols]
        row_out[:, :1] += jnp.sum(up * okay, 1, keepdims=True)
        row_out[:, 1:2] += jnp.sum(down * okay, 1, keepdims=True)


def log_sum(up, down):
    fine = up >= 1.9287498479639178e-22
    return jnp.where(
        fine, jnp.log(jnp.where(fine, up, 1.0)) + SHIFT, jnp.log(jnp.where(fine, 1.0, down)) - SHIFT
    )


def gradient_kernel(
    dp, own, s_ref, all_ref, colstat_ref, rowstat_ref, mask_ref, col_ref, text_ref, image_ref, scale_ref,
    grad_ref, loss_ref,
):
    step = pl.program_id(0)
    factor = scale_ref[1]
    mask = mask_ref[...]
    okay = col_ref[...]
    row_lse = log_sum(rowstat_ref[:, :1], rowstat_ref[:, 1:2])
    col_lse = log_sum(colstat_ref[0:1, :], colstat_ref[1:2, :])

    @pl.when(step == 0)
    def _():
        grad_ref[...] = jnp.zeros_like(grad_ref)
        loss_ref[...] = jnp.zeros_like(loss_ref)
        t = text_ref[...].astype(f32) * image_ref[...].astype(f32)
        diag = scale_ref[0] * jnp.sum(t, -1, keepdims=True)
        m = mask[:own]
        rows = factor * jnp.sum(m * (row_lse[:own] - 2.0 * diag), 0, keepdims=True)
        loss_ref[0:1, 0:1] = rows
        loss_ref[1:2, 0:1] = -2.0 * factor * jnp.sum(m * diag, 0, keepdims=True)

    s = s_ref[...]
    g = (jnp.exp(jnp.minimum(s - row_lse, 1.0)) + jnp.exp(jnp.minimum(s - col_lse, 1.0))) * ((factor * mask) * okay)
    grad_ref[...] += dot(g.astype(bf16), all_ref[...])
    cols = (factor / dp) * jnp.sum(jnp.where(okay > 0, col_lse, 0.0), 1, keepdims=True)
    loss_ref[0:1, 0:1] += cols
    logs = jnp.sum(jnp.sum(g * s, 0, keepdims=True), 1, keepdims=True)
    loss_ref[1:2, 0:1] += logs


def backward_ffn_kernel(
    txt, part_ref, back_ref, image_ref, u_ref, len_ref, mask_ref, scale_ref, rowlen_ref, hpool_ref,
    n2_ref, slope_ref, xhat2_ref, rstd2_ref, att_ref, gains_ref, wdown_ref, wup_ref, wo_ref,
    dffn_ref, dwo_ref, gmid_ref, datt_ref, gain_ref, dh, gd, acc_up, acc_o,
):
    step = pl.program_id(0)
    last = step == pl.num_programs(0) - 1
    rows, d = n2_ref.shape
    ff = wup_ref.shape[1]
    seqs = rows // txt

    @pl.when(step == 0)
    def _():
        scale, factor = scale_ref[0], scale_ref[1]
        u = u_ref[...] / len_ref[...]
        r = lax.rsqrt(jnp.sum(u * u, -1, keepdims=True) + 1e-6)
        g = scale * (part_ref[...] + back_ref[...])
        g = g - (2.0 * factor * scale) * mask_ref[...] * image_ref[...].astype(f32)
        du = r * g - (r * r * r) * u * jnp.sum(u * g, -1, keepdims=True)
        du = du / len_ref[...]
        gd[...] = du
        low = du.astype(bf16)
        dh[...] = dot_nt(low, wdown_ref[...])
        hi, lo = split_bf16(hpool_ref[...])
        dffn_ref[:ff, :] = (dot_tn(hi, low) + dot_tn(lo, low)).astype(bf16)
        acc_up[...] = jnp.zeros_like(acc_up)
        acc_o[...] = jnp.zeros_like(acc_o)
        gain_ref[...] = jnp.zeros_like(gain_ref)

    at = pl.ds(pl.multiple_of(step * seqs, seqs), seqs)
    n2 = n2_ref[...]
    dn2 = jnp.zeros((rows, d), f32)
    chunk = 512
    for c in range(0, ff, chunk):
        cs = slice(c, c + chunk)
        spread = jnp.broadcast_to(dh[at, cs][:, None, :], (seqs, txt, chunk)).reshape(rows, chunk)
        grad_before = (spread * slope_ref[:, cs].astype(f32)).astype(bf16)
        acc_up[:, cs] += dot_tn(n2, grad_before)
        dn2 += dot_nt(grad_before, wup_ref[:, cs])
    xhat = xhat2_ref[...].astype(f32)
    gain_ref[0:1, :] += jnp.sum(dn2 * xhat, 0, keepdims=True)
    gain_ref[1:2, :] += jnp.sum(dn2, 0, keepdims=True)
    gn = dn2 * gains_ref[1:2, :]
    dmid = rstd2_ref[...] * (
        gn - jnp.mean(gn, -1, keepdims=True) - xhat * jnp.mean(gn * xhat, -1, keepdims=True)
    )
    pos = lax.broadcasted_iota(jnp.int32, (rows, 1), 0) % txt
    keep = jnp.where(pos.astype(f32) < rowlen_ref[...], 1.0, 0.0)
    direct = jnp.broadcast_to(gd[at, :][:, None, :], (seqs, txt, d)).reshape(rows, d)
    gmid = direct * keep + dmid
    gmid_ref[...] = gmid
    branch = gmid.astype(bf16)
    acc_o[...] += dot_tn(att_ref[...], branch)
    datt_ref[...] = dot_nt(branch, wo_ref[...]).astype(bf16)

    @pl.when(last)
    def _():
        for b in range(ff // d):
            dffn_ref[ff + b * d : ff + (b + 1) * d, :] = acc_up[:, b * d : (b + 1) * d].astype(bf16)
        dwo_ref[...] = acc_o[...].astype(bf16)


def backward_attention_kernel(
    gmid_ref, datt_ref, qkv_ref, probs_ref, n1_ref, xhat1_ref, rstd1_ref, gains_ref, wqkv_ref,
    dx_ref, dqkv_ref, gain_ref, gq, acc,
):
    step = pl.program_id(0)
    rows, d = gmid_ref.shape
    low = lax.broadcasted_iota(jnp.int32, (LANES, LANES), 1) < HEAD
    zero = jnp.zeros((LANES, LANES), bf16)

    @pl.when(step == 0)
    def _():
        acc[...] = jnp.zeros_like(acc)
        gain_ref[...] = jnp.zeros_like(gain_ref)

    for g in range(rows // LANES):
        r = slice(g * LANES, (g + 1) * LANES)
        for p in range(d // LANES):
            cq = slice(p * LANES, (p + 1) * LANES)
            ck = slice(d + p * LANES, d + (p + 1) * LANES)
            cv = slice(2 * d + p * LANES, 2 * d + (p + 1) * LANES)
            q, k, v, da = qkv_ref[r, cq], qkv_ref[r, ck], qkv_ref[r, cv], datt_ref[r, cq]
            low_probs = probs_ref[g * (d // LANES) + p]
            probs = low_probs.astype(f32)
            dprobs = dot_nt(da, stack_heads(v, low, zero))
            dv = dot_tn(low_probs, da)
            halves = []
            for h in range(2):
                hs = slice(h * LANES, (h + 1) * LANES)
                ph, dh = probs[:, hs], dprobs[:, hs]
                halves.append(ph * (dh - jnp.sum(ph * dh, -1, keepdims=True)))
            ds = jnp.concatenate(halves, 1).astype(bf16)
            gq[r, cq] = (dot(ds, stack_heads(k, low, zero)) * HEAD**-0.5).astype(bf16)
            dk = dot_tn(ds, q)
            gq[r, ck] = jnp.where(low, dk[:LANES], dk[LANES:]).astype(bf16)
            gq[r, cv] = jnp.where(low, dv[:LANES], dv[LANES:]).astype(bf16)
    gp = gq[...]
    acc[...] += dot_tn(n1_ref[...], gp)
    dn1 = dot_nt(gp, wqkv_ref[...])
    xhat = xhat1_ref[...].astype(f32)
    gain_ref[0:1, :] += jnp.sum(dn1 * xhat, 0, keepdims=True)
    gain_ref[1:2, :] += jnp.sum(dn1, 0, keepdims=True)
    gn = dn1 * gains_ref[0:1, :]
    dx_ref[...] = gmid_ref[...] + rstd1_ref[...] * (
        gn - jnp.mean(gn, -1, keepdims=True) - xhat * jnp.mean(gn * xhat, -1, keepdims=True)
    )

    @pl.when(step == pl.num_programs(0) - 1)
    def _():
        for b in range(3):
            dqkv_ref[b * d : (b + 1) * d, :] = acc[:, b * d : (b + 1) * d].astype(bf16)


class Links:
    def __init__(self, mesh):
        self.dp, self.rep = mesh.shape["dp"], mesh.shape["rep"]
        self.bits = (self.dp - 1).bit_length()

    def bit(self, b):
        return (lax.axis_index("dp") >> b) & 1

    def across(self, x, b):
        return lax.ppermute(x, "dp", [(i, i ^ (1 << b)) for i in range(self.dp)])

    def core(self, x):
        return lax.ppermute(x, "rep", [(0, 1), (1, 0)])

    def gather(self, x, order):
        slots = {0: x}
        x = x[None]
        done = []
        for b in order:
            got = self.across(x, b)
            x = jnp.concatenate([x, got], 0)
            done.append(b)
        slots = [0]
        for b in done:
            slots = slots + [s | (1 << b) for s in slots]
        return x, slots

    def scatter_sum(self, x, order):
        n = x.shape[0] // 2
        v = lax.axis_index("rep")
        got = self.core(lax.dynamic_slice_in_dim(x, (1 - v) * n, n))
        x = (lax.dynamic_slice_in_dim(x, v * n, n).astype(f32) + got.astype(f32)).astype(bf16)
        for b in order:
            n, v = n // 2, self.bit(b)
            got = self.across(lax.dynamic_slice_in_dim(x, (1 - v) * n, n), b)
            x = (lax.dynamic_slice_in_dim(x, v * n, n).astype(f32) + got.astype(f32)).astype(bf16)
        return x

    def spread(self, x, order):
        for b in reversed(order):
            got = self.across(x, b)
            x = jnp.where(self.bit(b) == 0, jnp.concatenate([x, got], 0), jnp.concatenate([got, x], 0))
        got = self.core(x)
        return jnp.where(
            lax.axis_index("rep") == 0, jnp.concatenate([x, got], 0), jnp.concatenate([got, x], 0)
        )

    def total(self, x):
        x = x + self.core(x)
        for b in range(self.bits):
            x = x + self.across(x, b)
        return x


def body(
    links, image_in, img_gains, img_shifts, img_qkv, img_out, img_up, img_down, text_in, lengths, valid,
    txt_gains, txt_shifts, txt_qkv, txt_out, txt_up, txt_down, log_scale,
):
    dp, bits = links.dp, links.bits
    pairs, txt, d = text_in.shape
    ff = txt_up.shape[1]
    tokens = pairs * txt
    half = pairs // 2
    scale = jnp.exp(log_scale)

    own_mask = valid.astype(f32)
    col_mask = own_mask[None, :]
    for b in range(bits):
        got = links.across(col_mask, b)
        col_mask = jnp.where(
            links.bit(b) == 0, jnp.concatenate([col_mask, got], 0), jnp.concatenate([got, col_mask], 0)
        )
    col_mask = col_mask.reshape(1, dp * pairs)
    other_mask = links.core(own_mask)
    nvalid = jnp.sum(col_mask)
    nvalid = nvalid + links.core(nvalid.reshape(1, 1))[0, 0]
    factor = 0.5 / nvalid
    row_mask = jnp.concatenate([own_mask, other_mask])[:, None]
    scalars = jnp.stack([scale, factor])

    order = list(range(bits))[::-1]
    image_args = (image_in, img_gains, img_shifts, img_qkv, img_out, img_up, img_down)
    emb_a = image_embed(*image_args, 0, half)
    all_a, slots = links.gather(emb_a, order)
    emb_b = image_embed(*image_args, half, half)
    all_b, slots = links.gather(emb_b, order)
    place_of = [slots.index(k) for k in range(dp)]
    assert all(place_of[i] ^ place_of[j] == place_of[i ^ j] for i in range(dp) for j in range(dp))

    flen = lengths.astype(f32)[:, None]
    row_len = jnp.broadcast_to(flen, (pairs, txt)).reshape(tokens, 1)
    key_ok = (jnp.arange(txt)[None, :] < lengths[:, None]).astype(f32).reshape(tokens // LANES, LANES)
    (xhat1, rstd1, n1, qkv, probs, att, xhat2, rstd2, n2, slope, hpool, pooled) = text_forward(
        text_in.reshape(tokens, d), row_len, key_ok, txt_gains, txt_shifts, txt_qkv, txt_out, txt_up, txt_down, txt
    )
    u = pooled / flen
    text_emb = (u * lax.rsqrt(jnp.sum(u * u, -1, keepdims=True) + 1e-6)).astype(bf16)
    texts = jnp.concatenate([text_emb, links.core(text_emb)], 0)
    rows = 2 * pairs

    all_a, all_b = bit_order(all_a, order, bits), bit_order(all_b, order, bits)
    group = min(8, dp)
    me = lax.axis_index("dp")
    place = jnp.stack([me // group, me % group]).astype(jnp.int32)
    cols = group * pairs
    smem = pl.BlockSpec(memory_space=pltpu.SMEM)
    keep = lambda *_: (0, 0)
    scores, images, col_sum, row_sum = pl.pallas_call(
        scores_kernel,
        grid_spec=pltpu.PrefetchScalarGridSpec(
            num_scalar_prefetch=1,
            grid=(dp // group,),
            in_specs=[
                pl.BlockSpec((rows, d), keep),
                pl.BlockSpec((rows, 1), keep),
                pl.BlockSpec((group, half, d), lambda i, s: (lax.bitwise_xor(i, s[0]), 0, 0)),
                pl.BlockSpec((group, half, d), lambda i, s: (lax.bitwise_xor(i, s[0]), 0, 0)),
                pl.BlockSpec((1, cols), lambda i, s: (0, i)),
                smem,
            ],
            out_specs=[
                pl.BlockSpec((rows, cols), lambda i, s: (0, i)),
                pl.BlockSpec((cols, d), lambda i, s: (i, 0)),
                pl.BlockSpec((2, cols), lambda i, s: (0, i)),
                pl.BlockSpec((rows, 2), keep),
            ],
        ),
        out_shape=[
            jax.ShapeDtypeStruct((rows, dp * pairs), f32),
            jax.ShapeDtypeStruct((dp * pairs, d), bf16),
            jax.ShapeDtypeStruct((2, dp * pairs), f32),
            jax.ShapeDtypeStruct((rows, 2), f32),
        ],
        compiler_params=params(),
        name="pair_scores",
    )(place, texts, row_mask, all_a, all_b, col_mask, scalars)
    swapped = links.core(row_sum)
    row_sum = row_sum + jnp.concatenate([swapped[pairs:], swapped[:pairs]], 0)
    for b in range(bits):
        col_sum = col_sum + links.across(col_sum, b)

    own_images = jnp.concatenate([emb_a, emb_b], 0)
    partial, sums = pl.pallas_call(
        functools.partial(gradient_kernel, dp, pairs),
        grid=(dp // group,),
        in_specs=[
            pl.BlockSpec((rows, cols), lambda i: (0, i)),
            pl.BlockSpec((cols, d), lambda i: (i, 0)),
            pl.BlockSpec((2, cols), lambda i: (0, i)),
            whole(row_sum),
            whole(row_mask),
            pl.BlockSpec((1, cols), lambda i: (0, i)),
            whole(text_emb),
            whole(own_images),
            smem,
        ],
        out_specs=[pl.BlockSpec((rows, d), lambda i: (0, 0)), pl.BlockSpec((8, LANES), lambda i: (0, 0))],
        out_shape=[jax.ShapeDtypeStruct((rows, d), f32), jax.ShapeDtypeStruct((8, LANES), f32)],
        compiler_params=params(),
        name="pair_gradients",
    )(scores, images, col_sum, row_sum, row_mask, col_mask, text_emb, own_images, scalars)
    back = links.core(partial[pairs:])

    block_rows = 256
    steps = tokens // block_rows
    block = lambda w: pl.BlockSpec((block_rows, w), lambda i: (i, 0))
    dffn, dwo, gmid, datt, gain2 = pl.pallas_call(
        functools.partial(backward_ffn_kernel, txt),
        grid=(steps,),
        in_specs=[
            pl.BlockSpec((pairs, d), lambda i: (0, 0)), whole(back), whole(own_images), whole(pooled), whole(flen),
            pl.BlockSpec((pairs, 1), lambda i: (0, 0)), smem, block(1), whole(hpool),
            block(d), block(ff), block(d), block(1), block(d),
            whole(txt_gains), whole(txt_down), whole(txt_up), whole(txt_out),
        ],
        out_specs=[
            pl.BlockSpec((2 * ff, d), lambda i: (0, 0)), pl.BlockSpec((d, d), lambda i: (0, 0)),
            block(d), block(d), pl.BlockSpec((8, d), lambda i: (0, 0)),
        ],
        out_shape=[
            jax.ShapeDtypeStruct((2 * ff, d), bf16), jax.ShapeDtypeStruct((d, d), bf16),
            jax.ShapeDtypeStruct((tokens, d), f32), jax.ShapeDtypeStruct((tokens, d), bf16),
            jax.ShapeDtypeStruct((8, d), f32),
        ],
        scratch_shapes=[
            pltpu.VMEM((pairs, ff), f32), pltpu.VMEM((pairs, d), f32), pltpu.VMEM((d, ff), f32), pltpu.VMEM((d, d), f32),
        ],
        compiler_params=params(),
        cost_estimate=pl.CostEstimate(flops=4 * tokens * d * (ff + d), bytes_accessed=2 * tokens * (ff + 6 * d), transcendentals=0),
        name="backward_ffn",
    )(
        partial, back, own_images, pooled, flen, row_mask, scalars, row_len, hpool, n2, slope, xhat2, rstd2, att,
        txt_gains, txt_down, txt_up, txt_out,
    )
    orders = (list(range(bits)), [1, 0] + list(range(2, bits)) if bits > 1 else list(range(bits)))
    part_ffn = links.scatter_sum(dffn, orders[0])

    dx, dqkv, gain1 = pl.pallas_call(
        backward_attention_kernel,
        grid=(steps,),
        in_specs=[
            block(d), block(d), block(3 * d),
            pl.BlockSpec((block_rows // LANES * (d // LANES), LANES, 2 * LANES), lambda i: (i, 0, 0)),
            block(d), block(d), block(1), whole(txt_gains), whole(txt_qkv),
        ],
        out_specs=[block(d), pl.BlockSpec((3 * d, d), lambda i: (0, 0)), pl.BlockSpec((8, d), lambda i: (0, 0))],
        out_shape=[
            jax.ShapeDtypeStruct((tokens, d), f32), jax.ShapeDtypeStruct((3 * d, d), bf16), jax.ShapeDtypeStruct((8, d), f32),
        ],
        scratch_shapes=[pltpu.VMEM((block_rows, 3 * d), bf16), pltpu.VMEM((d, 3 * d), f32)],
        compiler_params=params(),
        cost_estimate=pl.CostEstimate(flops=4 * tokens * d * 4 * d, bytes_accessed=2 * tokens * 12 * d, transcendentals=0),
        name="backward_attention",
    )(gmid, datt, qkv, probs, n1, xhat1, rstd1, txt_gains, txt_qkv)
    part_att = links.scatter_sum(jnp.concatenate([dqkv, dwo], 0), orders[1])

    small = jnp.concatenate(
        [gain1[0:1], gain2[0:1], gain1[1:2], gain2[1:2], jnp.broadcast_to(sums[0:2, 0:1], (2, d)), jnp.zeros((2, d), f32)], 0
    )
    small = links.total(small)
    full_ffn = links.spread(part_ffn, orders[0])
    full_att = links.spread(part_att, orders[1])
    side = lambda a, n: a.astype(f32).reshape(n, d, d).transpose(1, 0, 2).reshape(d, n * d)
    return (
        small[4, 0],
        small[0:2],
        small[2:4],
        side(full_att[: 3 * d], 3),
        full_att[3 * d :].astype(f32),
        side(full_ffn[ff:], ff // d),
        full_ffn[:ff].astype(f32),
        small[5, 0],
        dx.reshape(pairs, txt, d),
    )


def bit_order(x, order, bits):
    if order == list(range(bits)):
        return x
    tail = x.shape[1:]
    x = x.reshape((2,) * bits + tail)
    have = [order[bits - 1 - a] for a in range(bits)]
    want = [have.index(b) for b in reversed(range(bits))]
    return x.transpose(want + [bits + i for i in range(len(tail))]).reshape((1 << bits,) + tail)


def solution(mesh):
    both = ("dp", "rep")
    deep = P(both, None, None)
    in_specs = (deep,) + (P(),) * 6 + (deep, P(both), P(both)) + (P(),) * 7
    out_specs = (P(),) * 8 + (deep,)
    return jax.shard_map(
        functools.partial(body, Links(mesh)), mesh=mesh, in_specs=in_specs, out_specs=out_specs, check_vma=False
    )
```

```python
import functools
import jax
import jax.numpy as jnp
from jax import lax
from jax.experimental import pallas as pl
from jax.experimental.pallas import tpu as pltpu
from jax.sharding import PartitionSpec as P

HEAD = 64
LANES = 128
f32 = jnp.float32
bf16 = jnp.bfloat16
GELU_C = 0.7978845608028654
GELU_A = 0.044715
SHIFT = 50.0
SAFE = 80.0
NOTE = 16
VMEM = 48 * 1024 * 1024


def dot(a, b):
    return jnp.dot(a, b, preferred_element_type=f32)


def dot_nt(a, b):
    return lax.dot_general(a, b, (((1,), (1,)), ((), ())), preferred_element_type=f32)


def dot_tn(a, b):
    return lax.dot_general(a, b, (((0,), (0,)), ((), ())), preferred_element_type=f32)


def norm_parts(x):
    mu = jnp.mean(x, -1, keepdims=True)
    c = x - mu
    rstd = lax.rsqrt(jnp.mean(c * c, -1, keepdims=True) + 1e-6)
    return c * rstd, rstd


def whole(a):
    return pl.BlockSpec(a.shape, lambda *_: (0,) * a.ndim)


def params():
    return pltpu.CompilerParams(vmem_limit_bytes=VMEM)


def cost(us):
    return pl.CostEstimate(flops=int(us * 1.1e9), bytes_accessed=0, transcendentals=0)


def split_bf16(v):
    hi = v.astype(bf16)
    return hi, (v - hi.astype(f32)).astype(bf16)


def count_rows(valid_ref, d):
    count = jnp.sum(valid_ref[...].astype(f32), 1, keepdims=True)
    return jnp.broadcast_to(count, (NOTE, d)).astype(bf16)


def image_kernel(
    seqs, x_ref, valid_ref, gains_ref, shifts_ref, wqkv_ref, wo_ref, wup_ref, wdown_ref, out_ref,
    xt, xs, qkv, att, sc, ec, hs, ms,
):
    tokens, _, d = x_ref.shape
    pad = -(-tokens // 8) * 8
    rows, pair = seqs * pad, 2 * pad
    step = pl.program_id(0)
    ff = wup_ref.shape[1]
    hp = d // LANES

    @pl.when(step == 0)
    def _():
        xs[...] = jnp.zeros_like(xs)

    for p in range(hp):
        c = slice(p * LANES, (p + 1) * LANES)
        xt[p] = x_ref[:, :, c].astype(f32).reshape(tokens * seqs, LANES)
        for b in range(seqs):
            xs[b * pad : b * pad + tokens, c] = xt[p, pl.ds(b, tokens, stride=seqs), :]
    x = xs[...]
    n1 = (norm_parts(x)[0] * gains_ref[0:1, :] + shifts_ref[0:1, :]).astype(bf16)
    qkv[:, :d] = (dot(n1, wqkv_ref[:, :d]) * HEAD**-0.5).astype(bf16)
    qkv[:, d:] = dot(n1, wqkv_ref[:, d:]).astype(bf16)

    low = lax.broadcasted_iota(jnp.int32, (pair, LANES), 1) < HEAD
    key_lane = lax.broadcasted_iota(jnp.int32, (pair, 2 * pair), 1)
    query_row = lax.broadcasted_iota(jnp.int32, (pair, 2 * pair), 0)
    first_head = key_lane < pair
    key_row = jnp.where(first_head, key_lane, key_lane - pair)
    second_image = key_row >= pad
    key_pos = jnp.where(second_image, key_row - pad, key_row)
    bias = jnp.where((key_pos < tokens) & (second_image == (query_row >= pad)), 0.0, -1e30)
    zero, one = jnp.zeros((pair, LANES), bf16), jnp.ones((pair, LANES), bf16)
    ones = jnp.concatenate([jnp.where(low, one, zero), jnp.where(low, zero, one)], 0)
    big = jnp.zeros((pair, 2 * pair), f32)
    for b in range(seqs // 2):
        r = slice(b * pair, (b + 1) * pair)
        for p in range(hp):
            q = qkv[r, p * LANES : (p + 1) * LANES]
            k = qkv[r, d + p * LANES : d + (p + 1) * LANES]
            stacked = jnp.concatenate([jnp.where(low, k, zero), jnp.where(low, zero, k)], 0)
            s = dot_nt(q, stacked)
            big = jnp.maximum(big, jnp.abs(s))
            sc[b * hp + p] = s
    safe = jnp.max(big) < SAFE

    @pl.when(safe)
    def _():
        for i in range(seqs // 2 * hp):
            ec[i] = jnp.exp(sc[i] + bias).astype(bf16)

    @pl.when(jnp.logical_not(safe))
    def _():
        @pl.loop(0, seqs // 2 * hp)
        def _(i):
            s = sc[i] + bias
            top0 = jnp.max(jnp.where(first_head, s, -2e30), -1, keepdims=True)
            top1 = jnp.max(jnp.where(first_head, -2e30, s), -1, keepdims=True)
            ec[i] = jnp.exp(s - jnp.where(first_head, top0, top1)).astype(bf16)

    for b in range(seqs // 2):
        r = slice(b * pair, (b + 1) * pair)
        for p in range(hp):
            v = qkv[r, 2 * d + p * LANES : 2 * d + (p + 1) * LANES]
            stacked = jnp.concatenate([jnp.where(low, v, zero), jnp.where(low, zero, v)], 0)
            o = dot(ec[b * hp + p], jnp.concatenate([stacked, ones], 1))
            att[r, p * LANES : (p + 1) * LANES] = (o[:, :LANES] / o[:, LANES:]).astype(bf16)
    mid = x + dot(att[...], wo_ref[...])
    keep = lax.broadcasted_iota(jnp.int32, (seqs, pad, 1), 1) < tokens
    keep = jnp.where(keep, 1.0, 0.0).reshape(rows, 1)
    at = pl.ds(pl.multiple_of(step * seqs, seqs), seqs)
    ms[at, :] = jnp.sum((mid * keep).reshape(seqs, pad, d), 1)
    n2 = ((norm_parts(mid)[0] * gains_ref[1:2, :] + shifts_ref[1:2, :]) * keep).astype(bf16)
    chunk = 512
    for c in range(0, ff, chunk):
        v = dot(n2, wup_ref[:, c : c + chunk])
        t = jnp.tanh(v * (GELU_C + (GELU_C * GELU_A) * (v * v)))
        h = (0.5 * v) * (1.0 + t)
        hs[at, c : c + chunk] = jnp.sum(h.reshape(seqs, pad, chunk), 1)

    @pl.when(step == pl.num_programs(0) - 1)
    def _():
        hi, lo = split_bf16(hs[...] * (1.0 / tokens))
        u = ms[...] * (1.0 / tokens) + dot(hi, wdown_ref[...]) + dot(lo, wdown_ref[...])
        n = u.shape[0]
        out_ref[:n] = (u * lax.rsqrt(jnp.sum(u * u, -1, keepdims=True) + 1e-6)).astype(bf16)
        if out_ref.shape[0] > n:
            out_ref[n:] = count_rows(valid_ref, d)


def image_embed(xt, valid, gains, shifts, wqkv, wo, wup, wdown, start, count, note, seqs=16):
    tokens, _, d = xt.shape
    ff = wup.shape[1]
    pad = -(-tokens // 8) * 8
    tiles = seqs // 2 * (d // LANES)
    first = start // seqs
    rows = count + (NOTE if note else 0)
    return pl.pallas_call(
        functools.partial(image_kernel, seqs),
        grid=(count // seqs,),
        in_specs=[pl.BlockSpec((tokens, seqs, d), lambda i: (0, i + first, 0))]
        + [whole(a) for a in (valid, gains, shifts, wqkv, wo, wup, wdown)],
        out_specs=pl.BlockSpec((rows, d), lambda i: (0, 0)),
        out_shape=jax.ShapeDtypeStruct((rows, d), bf16),
        scratch_shapes=[
            pltpu.VMEM((d // LANES, seqs * tokens, LANES), f32),
            pltpu.VMEM((seqs * pad, d), f32),
            pltpu.VMEM((seqs * pad, 3 * d), bf16),
            pltpu.VMEM((seqs * pad, d), bf16),
            pltpu.VMEM((tiles, 2 * pad, 4 * pad), f32),
            pltpu.VMEM((tiles, 2 * pad, 4 * pad), bf16),
            pltpu.VMEM((count, ff), f32),
            pltpu.VMEM((count, d), f32),
        ],
        compiler_params=params(),
        cost_estimate=cost(0.45 * count),
        name="image_block",
    )(xt, valid, gains, shifts, wqkv, wo, wup, wdown)


def stack_heads(a, low, zero):
    return jnp.concatenate([jnp.where(low, a, zero), jnp.where(low, zero, a)], 0)


def text_forward_kernel(
    txt, held, x_ref, len_ref, key_ref, flen_ref, gains_ref, shifts_ref, wqkv_ref, wo_ref, wup_ref, wdown_ref, *refs,
):
    (xhat1_ref, rstd1_ref, n1_ref, qkv_ref, probs_ref, att_ref, xhat2_ref, rstd2_ref, n2_ref, slope_ref,
     hpool_ref, u_ref, emb_ref, ms) = refs[held:]
    step = pl.program_id(0)
    rows, d = x_ref.shape
    ff = wup_ref.shape[1]
    seqs = rows // txt
    x = x_ref[...].astype(f32)
    xhat1, rstd1 = norm_parts(x)
    xhat1_ref[...] = xhat1.astype(bf16)
    rstd1_ref[...] = rstd1
    n1 = (xhat1 * gains_ref[0:1, :] + shifts_ref[0:1, :]).astype(bf16)
    n1_ref[...] = n1
    qkv_ref[:, :d] = (dot(n1, wqkv_ref[:, :d]) * HEAD**-0.5).astype(bf16)
    qkv_ref[:, d:] = dot(n1, wqkv_ref[:, d:]).astype(bf16)
    low = lax.broadcasted_iota(jnp.int32, (LANES, LANES), 1) < HEAD
    same = (
        lax.broadcasted_iota(jnp.int32, (LANES, LANES), 0) // txt
        == lax.broadcasted_iota(jnp.int32, (LANES, LANES), 1) // txt
    )
    zero = jnp.zeros((LANES, LANES), bf16)
    for g in range(rows // LANES):
        r = slice(g * LANES, (g + 1) * LANES)
        bias = jnp.where(same & (key_ref[0, g : g + 1, :] > 0), 0.0, -1e30)
        for p in range(d // LANES):
            c = slice(p * LANES, (p + 1) * LANES)
            q = qkv_ref[r, p * LANES : (p + 1) * LANES]
            k = qkv_ref[r, d + p * LANES : d + (p + 1) * LANES]
            v = qkv_ref[r, 2 * d + p * LANES : 2 * d + (p + 1) * LANES]
            s = dot_nt(q, stack_heads(k, low, zero))
            halves = []
            for h in range(2):
                sh = s[:, h * LANES : (h + 1) * LANES] + bias
                e = jnp.exp(sh - jnp.max(sh, -1, keepdims=True))
                halves.append(e / jnp.sum(e, -1, keepdims=True))
            probs = jnp.concatenate(halves, 1).astype(bf16)
            probs_ref[g * (d // LANES) + p] = probs
            att_ref[r, c] = dot(probs, stack_heads(v, low, zero)).astype(bf16)
    mid = x + dot(att_ref[...], wo_ref[...])
    xhat2, rstd2 = norm_parts(mid)
    xhat2_ref[...] = xhat2.astype(bf16)
    rstd2_ref[...] = rstd2
    pos = lax.broadcasted_iota(jnp.int32, (rows, 1), 0) % txt
    keep = jnp.where(pos.astype(f32) < len_ref[...], 1.0, 0.0)
    n2 = ((xhat2 * gains_ref[1:2, :] + shifts_ref[1:2, :]) * keep).astype(bf16)
    n2_ref[...] = n2
    at = pl.ds(pl.multiple_of(step * seqs, seqs), seqs)
    ms[at, :] = jnp.sum((mid * keep).reshape(seqs, txt, d), 1)
    chunk = 512
    for c in range(0, ff, chunk):
        v = dot(n2, wup_ref[:, c : c + chunk])
        v2 = v * v
        t = jnp.tanh(v * (GELU_C + (GELU_C * GELU_A) * v2))
        half = 0.5 + 0.5 * t
        h = v * half
        slope = half + h * (1.0 - t) * (GELU_C + (3.0 * GELU_C * GELU_A) * v2)
        slope_ref[:, c : c + chunk] = (slope * keep).astype(bf16)
        hpool_ref[at, c : c + chunk] = jnp.sum(h.reshape(seqs, txt, chunk), 1)

    @pl.when(step == pl.num_programs(0) - 1)
    def _():
        hi, lo = split_bf16(hpool_ref[...])
        pooled = ms[...] + dot(hi, wdown_ref[...]) + dot(lo, wdown_ref[...])
        u = pooled / flen_ref[...]
        u_ref[...] = u
        emb_ref[...] = (u * lax.rsqrt(jnp.sum(u * u, -1, keepdims=True) + 1e-6)).astype(bf16)


def text_forward(piece, pieces, held, x, row_len, key_ok, flen, gains, shifts, wqkv, wo, wup, wdown, txt, rows=256):
    total, d = x.shape
    ff = wup.shape[1]
    pairs = total // txt
    hp = d // LANES
    part = pairs // pieces
    steps = total // pieces // rows
    first = piece * steps
    block = lambda *tail: pl.BlockSpec((rows,) + tail, lambda i: (i + first,) + (0,) * len(tail))
    still = lambda *shape: pl.BlockSpec(shape, lambda i: (piece, 0))
    shape = jax.ShapeDtypeStruct
    key3 = key_ok.reshape(total // rows, rows // LANES, LANES)
    args = (x, row_len, key3, flen, gains, shifts, wqkv, wo, wup, wdown)
    return pl.pallas_call(
        functools.partial(text_forward_kernel, txt, len(held)),
        grid=(steps,),
        in_specs=[
            block(d), block(1), pl.BlockSpec((1, rows // LANES, LANES), lambda i: (i + first, 0, 0)), still(part, 1)
        ]
        + [whole(a) for a in args[4:]]
        + [pl.BlockSpec(memory_space=pl.ANY)] * len(held),
        out_specs=[
            block(d), block(1), block(d), block(3 * d),
            pl.BlockSpec((rows // LANES * hp, LANES, 2 * LANES), lambda i: (i + first, 0, 0)),
            block(d), block(d), block(1), block(d), block(ff),
            still(part, ff), still(part, d), still(part, d),
        ],
        out_shape=[
            shape((total, d), bf16), shape((total, 1), f32), shape((total, d), bf16), shape((total, 3 * d), bf16),
            shape((total // LANES * hp, LANES, 2 * LANES), bf16),
            shape((total, d), bf16), shape((total, d), bf16), shape((total, 1), f32), shape((total, d), bf16),
            shape((total, ff), bf16), shape((pairs, ff), f32), shape((pairs, d), f32), shape((pairs, d), bf16),
        ],
        input_output_aliases={len(args) + i: i for i in range(len(held))},
        scratch_shapes=[pltpu.VMEM((part, d), f32)],
        compiler_params=params(),
        cost_estimate=cost(0.013 * total / pieces),
        name="text_forward",
    )(*args, *held)


def scores_kernel(
    group, place_ref, own_ref, other_ref, mask_ref, scale_ref, a0_ref, a1_ref, b0_ref, b1_ref,
    s_ref, all_ref, col_out, okay_out, row_out,
):
    step = pl.program_id(0)
    pairs = own_ref.shape[0]
    half = b0_ref.shape[1]
    scale = scale_ref[0]
    mask = mask_ref[...]
    inner = lax.rem(place_ref[0], group)
    late = lax.bitwise_xor(step, lax.div(place_ref[0], group)) >= pl.num_programs(0) // 2
    texts = jnp.concatenate([own_ref[...], other_ref[...]], 0)

    @pl.when(step == 0)
    def _():
        row_out[...] = jnp.zeros_like(row_out)
        row_out[:, 3:4] = mask

    lane = lax.broadcasted_iota(jnp.int32, (1, pairs), 1).astype(f32)
    for k in range(group):
        at = lax.bitwise_xor(k, inner)
        cols = slice(k * pairs, (k + 1) * pairs)
        a = jnp.where(late, a1_ref[at], a0_ref[at])
        images = jnp.concatenate([a[:half], jnp.where(late, b1_ref[at], b0_ref[at])], 0)
        count = a[half : half + 1, 0:1].astype(f32)
        okay = jnp.where(lane < count, 1.0, 0.0)
        okay_out[0:1, cols] = okay
        all_ref[cols, :] = images
        s = scale * dot_nt(texts, images)
        s_ref[:, cols] = s
        up = jnp.exp(s - SHIFT)
        down = jnp.exp(jnp.minimum(s, 0.0) + SHIFT)
        col_out[0:1, cols] = jnp.sum(up * mask, 0, keepdims=True)
        col_out[1:2, cols] = jnp.sum(down * mask, 0, keepdims=True)
        row_out[:, 0:1] += jnp.sum(up * okay, 1, keepdims=True)
        row_out[:, 1:2] += jnp.sum(down * okay, 1, keepdims=True)
        row_out[:, 2:3] += jnp.broadcast_to(count, (2 * pairs, 1))


def pair_scores(place, own, other, mask, scale, a0, a1, b0, b1):
    slots, half, d = b0.shape
    pairs = own.shape[0]
    group = min(8, slots)
    groups = slots // group
    cols = group * pairs
    keep = lambda *_: (0, 0)
    turn = lambda i, s: (lax.rem(lax.bitwise_xor(i, lax.div(s[0], group)), groups), 0, 0)
    still = lambda a: pl.BlockSpec(a.shape, keep)
    shape = jax.ShapeDtypeStruct
    return pl.pallas_call(
        functools.partial(scores_kernel, group),
        grid_spec=pltpu.PrefetchScalarGridSpec(
            num_scalar_prefetch=1,
            grid=(2 * groups,),
            in_specs=[still(own), still(other), still(mask), pl.BlockSpec(memory_space=pltpu.SMEM)]
            + [pl.BlockSpec((group,) + a.shape[1:], turn) for a in (a0, a1, b0, b1)],
            out_specs=[
                pl.BlockSpec((2 * pairs, cols), lambda i, s: (0, i)),
                pl.BlockSpec((cols, d), lambda i, s: (i, 0)),
                pl.BlockSpec((2, cols), lambda i, s: (0, i)),
                pl.BlockSpec((1, cols), lambda i, s: (0, i)),
                pl.BlockSpec((2 * pairs, 4), keep),
            ],
        ),
        out_shape=[
            shape((2 * pairs, 2 * groups * cols), f32), shape((2 * groups * cols, d), bf16),
            shape((2, 2 * groups * cols), f32), shape((1, 2 * groups * cols), f32), shape((2 * pairs, 4), f32),
        ],
        compiler_params=params(),
        cost_estimate=cost(4.0),
        name="pair_scores",
    )(place, own, other, mask, scale, a0, a1, b0, b1)


def log_sum(up, down):
    fine = up >= 1.9287498479639178e-22
    return jnp.where(
        fine, jnp.log(jnp.where(fine, up, 1.0)) + SHIFT, jnp.log(jnp.where(fine, 1.0, down)) - SHIFT
    )


def gradient_kernel(
    dp, scale_ref, s_ref, all_ref, col_ref, got_ref, okay_ref, row_ref, swap_ref, text_ref, a_ref, b_ref,
    grad_ref, back_ref, loss_ref,
):
    step = pl.program_id(0)
    pairs = text_ref.shape[0]
    half = b_ref.shape[0]
    row = row_ref[...] + jnp.concatenate([swap_ref[pairs:], swap_ref[:pairs]], 0)
    factor = 0.5 / row[0:1, 2:3]
    mask = row_ref[:, 3:4]
    okay = okay_ref[...]
    row_lse = log_sum(row[:, 0:1], row[:, 1:2])
    col = col_ref[...] + got_ref[...]
    col_lse = log_sum(col[0:1, :], col[1:2, :])

    @pl.when(step == 0)
    def _():
        grad_ref[...] = jnp.zeros_like(grad_ref)
        back_ref[...] = jnp.zeros_like(back_ref)
        loss_ref[...] = jnp.zeros_like(loss_ref)
        images = jnp.concatenate([a_ref[:half], b_ref[...]], 0)
        t = text_ref[...].astype(f32) * images.astype(f32)
        diag = scale_ref[0] * jnp.sum(t, -1, keepdims=True)
        m = mask[:pairs]
        loss_ref[0:1, 0:1] = factor * jnp.sum(m * (row_lse[:pairs] - 2.0 * diag), 0, keepdims=True)
        loss_ref[1:2, 0:1] = -2.0 * factor * jnp.sum(m * diag, 0, keepdims=True)

    s = s_ref[...]
    g = jnp.exp(jnp.minimum(s - row_lse, 1.0)) + jnp.exp(jnp.minimum(s - col_lse, 1.0))
    g = g * ((factor * mask) * okay)
    grad = dot(g.astype(bf16), all_ref[...])
    grad_ref[...] += grad[:pairs]
    back_ref[...] += grad[pairs:]
    cols = jnp.sum(jnp.where(okay > 0, col_lse, 0.0), 1, keepdims=True)
    loss_ref[0:1, 0:1] += factor * (cols * (1.0 / dp))
    loss_ref[1:2, 0:1] += jnp.sum(jnp.sum(g * s, 0, keepdims=True), 1, keepdims=True)


def pair_gradients(dp, scale, scores, images, col, got, okay, row, swap, texts, a, b):
    pairs, d = texts.shape
    cols = min(8, dp) * pairs
    still = lambda *shape: pl.BlockSpec(shape, lambda i: (0, 0))
    shape = jax.ShapeDtypeStruct
    return pl.pallas_call(
        functools.partial(gradient_kernel, dp),
        grid=(dp * pairs // cols,),
        in_specs=[
            pl.BlockSpec(memory_space=pltpu.SMEM),
            pl.BlockSpec((2 * pairs, cols), lambda i: (0, i)),
            pl.BlockSpec((cols, d), lambda i: (i, 0)),
            pl.BlockSpec((2, cols), lambda i: (0, i)),
            pl.BlockSpec((2, cols), lambda i: (0, i)),
            pl.BlockSpec((1, cols), lambda i: (0, i)),
        ]
        + [whole(x) for x in (row, swap, texts, a, b)],
        out_specs=[still(pairs, d), still(pairs, d), still(8, LANES)],
        out_shape=[shape((pairs, d), f32), shape((pairs, d), f32), shape((8, LANES), f32)],
        compiler_params=params(),
        cost_estimate=cost(3.0),
        name="pair_gradients",
    )(scale, scores, images, col, got, okay, row, swap, texts, a, b)


def backward_ffn_kernel(
    txt, layout, scale_ref, part_ref, back_ref, row_ref, swap_ref, a_ref, b_ref, u_ref, len_ref, hpool_ref,
    rowlen_ref, n2_ref, slope_ref, xhat2_ref, rstd2_ref, att_ref, gains_ref, wdown_ref, wup_ref, wo_ref,
    sum_ref, gmid_ref, datt_ref, gain_ref, dh, gd, acc_up, acc_o,
):
    step = pl.program_id(0)
    rows, d = n2_ref.shape
    ff = wup_ref.shape[1]
    seqs = rows // txt
    down_at, up_at, out_at = layout

    @pl.when(step == 0)
    def _():
        pairs = part_ref.shape[0]
        half = b_ref.shape[0]
        scale = scale_ref[0]
        factor = 0.5 / (row_ref[0:1, 2:3] + swap_ref[0:1, 2:3])
        images = jnp.concatenate([a_ref[:half], b_ref[...]], 0).astype(f32)
        u = u_ref[...]
        r = lax.rsqrt(jnp.sum(u * u, -1, keepdims=True) + 1e-6)
        g = scale * (part_ref[...] + back_ref[...]) - (2.0 * scale) * (factor * row_ref[:pairs, 3:4]) * images
        du = (r * g - (r * r * r) * u * jnp.sum(u * g, -1, keepdims=True)) / len_ref[...]
        gd[...] = du
        low = du.astype(bf16)
        dh[...] = dot_nt(low, wdown_ref[...])
        hi, lo = split_bf16(hpool_ref[...])
        sum_ref[down_at : down_at + ff] = (dot_tn(hi, low) + dot_tn(lo, low)).astype(bf16)
        acc_up[...] = jnp.zeros_like(acc_up)
        acc_o[...] = jnp.zeros_like(acc_o)
        gain_ref[...] = jnp.zeros_like(gain_ref)

    at = pl.ds(pl.multiple_of(step * seqs, seqs), seqs)
    n2 = n2_ref[...]
    dn2 = jnp.zeros((rows, d), f32)
    chunk = 512
    for c in range(0, ff, chunk):
        cs = slice(c, c + chunk)
        spread = jnp.broadcast_to(dh[at, cs][:, None, :], (seqs, txt, chunk)).reshape(rows, chunk)
        grad_before = (spread * slope_ref[:, cs].astype(f32)).astype(bf16)
        acc_up[:, cs] += dot_tn(n2, grad_before)
        dn2 += dot_nt(grad_before, wup_ref[:, cs])
    xhat = xhat2_ref[...].astype(f32)
    gain_ref[0:1, :] += jnp.sum(dn2 * xhat, 0, keepdims=True)
    gain_ref[1:2, :] += jnp.sum(dn2, 0, keepdims=True)
    gn = dn2 * gains_ref[1:2, :]
    dmid = rstd2_ref[...] * (
        gn - jnp.mean(gn, -1, keepdims=True) - xhat * jnp.mean(gn * xhat, -1, keepdims=True)
    )
    pos = lax.broadcasted_iota(jnp.int32, (rows, 1), 0) % txt
    keep = jnp.where(pos.astype(f32) < rowlen_ref[...], 1.0, 0.0)
    direct = jnp.broadcast_to(gd[at, :][:, None, :], (seqs, txt, d)).reshape(rows, d)
    gmid = direct * keep + dmid
    gmid_ref[...] = gmid
    branch = gmid.astype(bf16)
    acc_o[...] += dot_tn(att_ref[...], branch)
    datt_ref[...] = dot_nt(branch, wo_ref[...]).astype(bf16)

    @pl.when(step == pl.num_programs(0) - 1)
    def _():
        for b in range(ff // d):
            sum_ref[up_at + b * d : up_at + (b + 1) * d, :] = acc_up[:, b * d : (b + 1) * d].astype(bf16)
        for b in range(2):
            sum_ref[out_at[b] : out_at[b] + d // 2, :] = acc_o[b * d // 2 : (b + 1) * d // 2, :].astype(bf16)
        clear_tail(sum_ref, out_at[1] + d // 2)


def clear_tail(ref, n):
    if ref.shape[0] > n:
        ref[n:] = jnp.zeros((ref.shape[0] - n,) + ref.shape[1:], ref.dtype)


def backward_ffn(
    total, layout, scale, part, back, row, swap, a, b, u, flen, hpool, row_len, n2, slope, xhat2, rstd2, att,
    gains, wdown, wup, wo, txt, rows=256,
):
    tokens, d = n2.shape
    pairs, ff = hpool.shape
    block = lambda w: pl.BlockSpec((rows, w), lambda i: (i, 0))
    still = lambda *shape: pl.BlockSpec(shape, lambda i: (0, 0))
    shape = jax.ShapeDtypeStruct
    return pl.pallas_call(
        functools.partial(backward_ffn_kernel, txt, layout),
        grid=(tokens // rows,),
        in_specs=[pl.BlockSpec(memory_space=pltpu.SMEM)]
        + [whole(x) for x in (part, back, row, swap, a, b, u, flen, hpool)]
        + [block(1), block(d), block(ff), block(d), block(1), block(d)]
        + [whole(x) for x in (gains, wdown, wup, wo)],
        out_specs=[still(total, d), block(d), block(d), still(8, d)],
        out_shape=[shape((total, d), bf16), shape((tokens, d), f32), shape((tokens, d), bf16), shape((8, d), f32)],
        scratch_shapes=[
            pltpu.VMEM((pairs, ff), f32), pltpu.VMEM((pairs, d), f32), pltpu.VMEM((d, ff), f32), pltpu.VMEM((d, d), f32)
        ],
        compiler_params=params(),
        cost_estimate=cost(0.008 * tokens),
        name="backward_ffn",
    )(scale, part, back, row, swap, a, b, u, flen, hpool, row_len, n2, slope, xhat2, rstd2, att, gains, wdown, wup, wo)


def backward_attention_kernel(
    held, last, datt_ref, qkv_ref, probs_ref, n1_ref, cols_ref, wqkv_ref, *refs
):
    old_acc, old_flat = refs[1:3] if held else (None, None)
    gq_ref, sum_ref, flat_ref, acc, flat = refs[held:]
    step = pl.program_id(0)
    rows, d = n1_ref.shape
    low = lax.broadcasted_iota(jnp.int32, (LANES, LANES), 1) < HEAD
    zero = jnp.zeros((LANES, LANES), bf16)

    @pl.when(step == 0)
    def _():
        acc[...] = old_acc[...] if held else jnp.zeros_like(acc)
        flat[...] = old_flat[...] if held else jnp.zeros_like(flat)

    for g in range(rows // LANES):
        r = slice(g * LANES, (g + 1) * LANES)
        for p in range(d // LANES):
            cq = slice(p * LANES, (p + 1) * LANES)
            ck = slice(d + p * LANES, d + (p + 1) * LANES)
            cv = slice(2 * d + p * LANES, 2 * d + (p + 1) * LANES)
            q, k, v, da = qkv_ref[r, cq], qkv_ref[r, ck], qkv_ref[r, cv], datt_ref[r, cq]
            low_probs = probs_ref[g * (d // LANES) + p]
            probs = low_probs.astype(f32)
            dprobs = dot_nt(da, stack_heads(v, low, zero))
            dv = dot_tn(low_probs, da)
            halves = []
            for h in range(2):
                hs = slice(h * LANES, (h + 1) * LANES)
                ph, dh = probs[:, hs], dprobs[:, hs]
                halves.append(ph * (dh - jnp.sum(ph * dh, -1, keepdims=True)))
            ds = jnp.concatenate(halves, 1).astype(bf16)
            gq_ref[r, cq] = (dot(ds, stack_heads(k, low, zero)) * HEAD**-0.5).astype(bf16)
            dk = dot_tn(ds, q)
            gq_ref[r, ck] = jnp.where(low, dk[:LANES], dk[LANES:]).astype(bf16)
            gq_ref[r, cv] = jnp.where(low, dv[:LANES], dv[LANES:]).astype(bf16)
    gq = gq_ref[...]
    acc[...] += dot_tn(n1_ref[...], gq)
    flat[0:1, :] += jnp.sum(gq.astype(f32), 0, keepdims=True)

    @pl.when(step == pl.num_programs(0) - 1)
    def _():
        if not last:
            sum_ref[...] = acc[...]
            flat_ref[...] = flat[...]
            return
        for b in range(3):
            sum_ref[b * d : (b + 1) * d, :] = acc[:, b * d : (b + 1) * d].astype(bf16)
        clear_tail(sum_ref, 3 * d)
        w = wqkv_ref[...].astype(f32)
        total = flat[0:1, :]
        spread = jnp.sum((acc[...] - cols_ref[:, 1:2] * total) * w, 1, keepdims=True)
        flat_ref[:, 0:1] = spread / cols_ref[:, 0:1]
        flat_ref[:, 1:2] = jnp.sum(total * w, 1, keepdims=True)


def backward_attention(piece, pieces, held, total, datt, qkv, probs, n1, cols, wqkv, rows=256):
    tokens, d = n1.shape
    steps = tokens // pieces // rows
    first = piece * steps
    last = piece == pieces - 1
    block = lambda w: pl.BlockSpec((rows, w), lambda i: (i + first, 0))
    shape = jax.ShapeDtypeStruct
    outs = (
        [shape((total, d), bf16), shape((d, 2), f32)] if last else [shape((d, 3 * d), f32), shape((8, 3 * d), f32)]
    )
    args = (datt, qkv, probs, n1, cols, wqkv)
    return pl.pallas_call(
        functools.partial(backward_attention_kernel, len(held), last),
        grid=(steps,),
        in_specs=[
            block(d), block(3 * d),
            pl.BlockSpec((rows // LANES * (d // LANES), LANES, 2 * LANES), lambda i: (i + first, 0, 0)),
            block(d), whole(cols), whole(wqkv),
        ]
        + ([pl.BlockSpec(memory_space=pl.ANY)] + [whole(x) for x in held[1:]] if held else []),
        out_specs=[block(3 * d)] + [whole(x) for x in outs],
        out_shape=[shape((tokens, 3 * d), bf16)] + outs,
        input_output_aliases={len(args): 0} if held else {},
        scratch_shapes=[pltpu.VMEM((d, 3 * d), f32), pltpu.VMEM((8, 3 * d), f32)],
        compiler_params=params(),
        cost_estimate=cost(0.009 * tokens / pieces),
        name="backward_attention",
    )(*args, *held)


def backward_input_kernel(gq_ref, gmid_ref, xhat1_ref, rstd1_ref, gains_ref, wqkv_ref, dx_ref):
    gn = dot_nt(gq_ref[...], wqkv_ref[...]) * gains_ref[0:1, :]
    xhat = xhat1_ref[...].astype(f32)
    dx_ref[...] = gmid_ref[...] + rstd1_ref[...] * (
        gn - jnp.mean(gn, -1, keepdims=True) - xhat * jnp.mean(gn * xhat, -1, keepdims=True)
    )


def backward_input(gq, gmid, xhat1, rstd1, gains, wqkv, rows=256):
    tokens, d = gmid.shape
    block = lambda w: pl.BlockSpec((rows, w), lambda i: (i, 0))
    return pl.pallas_call(
        backward_input_kernel,
        grid=(tokens // rows,),
        in_specs=[block(3 * d), block(d), block(d), block(1), whole(gains), whole(wqkv)],
        out_specs=block(d),
        out_shape=jax.ShapeDtypeStruct((tokens, d), f32),
        compiler_params=params(),
        cost_estimate=cost(0.004 * tokens),
        name="backward_input",
    )(gq, gmid, xhat1, rstd1, gains, wqkv)


def finish_kernel(places, rep_ref, own_ref, got_ref, *out_refs):
    first = rep_ref[0] == 0
    for out, top, left, begin, n, part in places:
        a = own_ref[begin : begin + n, :]
        b = got_ref[begin : begin + n, :]
        mine = first if part == 0 else jnp.logical_not(first)
        out_refs[out][top : top + n, left : left + a.shape[1]] = jnp.where(mine, a, b).astype(f32)


def finish(rep, own, got, shapes, segments):
    half = own.shape[0]
    places = []
    for row, count, out, top, left in segments:
        while count:
            part, begin = divmod(row, half)
            n = min(count, half - begin)
            places.append((out, top, left, begin, n, part))
            row, top, count = row + n, top + n, count - n
    outs = [jax.ShapeDtypeStruct(s, f32) for s in shapes]
    return pl.pallas_call(
        functools.partial(finish_kernel, places),
        grid=(1,),
        in_specs=[pl.BlockSpec(memory_space=pltpu.SMEM), whole(own), whole(got)],
        out_specs=[whole(x) for x in outs],
        out_shape=outs,
        compiler_params=params(),
        cost_estimate=cost(3.0),
        name="finish",
    )(rep, own, got)


class Links:
    def __init__(self, mesh):
        self.dp, self.rep = mesh.shape["dp"], mesh.shape["rep"]
        self.bits = (self.dp - 1).bit_length()
        assert self.dp == 1 << self.bits and self.rep == 2
        near, far = list(range(min(2, self.bits))), list(range(2, self.bits))
        turn = lambda bits: list(zip(bits, bits[::-1]))
        self.near, self.far = turn(near), turn(far)
        self.gather_order = [(b, b) for b in far[::-1]] + self.near

    def bit(self, pair):
        place = lax.axis_index("dp")
        return jnp.where(lax.axis_index("rep") == 0, (place >> pair[0]) & 1, (place >> pair[1]) & 1)

    def across(self, x, pair):
        moves = [(2 * i + r, 2 * (i ^ (1 << pair[r])) + r) for i in range(self.dp) for r in range(2)]
        return lax.ppermute(x, ("dp", "rep"), moves)

    def core(self, x):
        return lax.ppermute(x, "rep", [(0, 1), (1, 0)])

    def padded(self, n):
        unit = self.rep * self.dp
        return -(-n // unit) * unit


class Reduction:
    def __init__(self, links, x, small=None):
        self.links, self.x, self.small = links, x, small
        self.plan = (
            [("core", None)]
            + [("half", p) for p in links.near]
            + [("full", p) for p in links.far]
            + [("join", p) for p in links.near[::-1]]
            + [("last", None)]
        )
        self.got = None

    def start(self):
        links = self.links
        kind, pair = self.kind, self.pair = self.plan.pop(0)
        x = self.x
        if kind in ("core", "half"):
            n = x.shape[0] // 2
            self.v = lax.axis_index("rep") if kind == "core" else links.bit(pair)
            send = lax.dynamic_slice_in_dim(x, (1 - self.v) * n, n)
        else:
            send = x
        if self.small is not None and kind in ("core", "half", "full"):
            send = jnp.concatenate([send, *split_bf16(self.small)], 0)
        self.got = links.core(send) if kind in ("core", "last") else links.across(send, pair)

    def end(self):
        kind, got, x = self.kind, self.got, self.x
        if kind == "last":
            return
        if kind == "join":
            low = self.links.bit(self.pair) == 0
            self.x = jnp.where(low, jnp.concatenate([x, got], 0), jnp.concatenate([got, x], 0))
            return
        n = x.shape[0]
        if kind in ("core", "half"):
            n = n // 2
            x = lax.dynamic_slice_in_dim(x, self.v * n, n)
        self.x = (x.astype(f32) + got[:n].astype(f32)).astype(bf16)
        if self.small is not None:
            m = self.small.shape[0]
            self.small = self.small + (got[n : n + m].astype(f32) + got[n + m :].astype(f32))


def beside(*values):
    return lax.optimization_barrier(values)


def body(
    links, image_in, img_gains, img_shifts, img_qkv, img_out, img_up, img_down, text_in, lengths, valid,
    txt_gains, txt_shifts, txt_qkv, txt_out, txt_up, txt_down, log_scale,
):
    dp, bits = links.dp, links.bits
    pairs, txt, d = text_in.shape
    ff = txt_up.shape[1]
    tokens = pairs * txt
    half, quarter = pairs // 2, pairs // 4
    scale = jnp.exp(log_scale).reshape(1)
    rep = lax.axis_index("rep").astype(jnp.int32).reshape(1)
    order = links.gather_order

    own_mask = valid.astype(f32)
    row_mask = jnp.concatenate([own_mask, links.core(own_mask)])[:, None]
    flen = lengths.astype(f32)[:, None]
    row_len = jnp.broadcast_to(flen, (pairs, txt)).reshape(tokens, 1)
    key_ok = (jnp.arange(txt)[None, :] < lengths[:, None]).astype(f32).reshape(tokens // LANES, LANES)

    xt = image_in.transpose(1, 0, 2)
    image_args = (valid[None, :], img_gains, img_shifts, img_qkv, img_out, img_up, img_down)
    embed = lambda start, count, note, after: image_embed(after, *image_args, start, count, note)
    text_args = (txt_gains, txt_shifts, txt_qkv, txt_out, txt_up, txt_down)
    pieces = 4
    forward = lambda piece, held, x: text_forward(piece, pieces, held, x, row_len, key_ok, flen, *text_args, txt)

    steps_a, steps_b = list(order), list(order)
    join = lambda x, got: jnp.concatenate([x, got], 0)
    emb_a = embed(0, half, True, xt)
    a = emb_a[None]
    got = links.across(a, steps_a.pop(0))
    emb_b0 = embed(half, quarter, False, xt)
    xt, got, emb_b0 = beside(xt, got, emb_b0)
    a = join(a, got)
    got = links.across(a, steps_a.pop(0))
    emb_b1 = embed(half + quarter, quarter, False, xt)
    text_x, emb_b1, got = beside(text_in.reshape(tokens, d), emb_b1, got)
    emb_b = jnp.concatenate([emb_b0, emb_b1], 0)
    b = emb_b[None]
    held = []
    for piece in range(pieces):
        if len(steps_a):
            a = join(a, got)
            got = links.across(a, steps_a.pop(0))
        early = piece < pieces - 1 and len(steps_b) > 1
        if early:
            got_b = links.across(b, steps_b.pop(0))
        held = list(forward(piece, held, text_x))
        if early:
            text_x, got_b, held[-1] = beside(text_x, got_b, held[-1])
            b = join(b, got_b)
    while steps_a:
        a = join(a, got)
        got = links.across(a, steps_a.pop(0))
    while len(steps_b) > 1:
        b = join(b, links.across(b, steps_b.pop(0)))
    got_b = links.across(b, steps_b.pop(0))
    (xhat1, rstd1, n1, qkv, probs, att, xhat2, rstd2, n2, slope, hpool, u, text_emb) = held

    place = sum(links.bit(order[i]) << i for i in range(bits)).astype(jnp.int32).reshape(1)
    scores, images, col, okay, row = pair_scores(
        place, text_emb, links.core(text_emb), row_mask, scale, a, got, b, got_b
    )
    swap = links.core(row)
    for pair in order[:-1]:
        col = col + links.across(col, pair)
    col_got = links.across(col, order[-1])
    part, other, sums = pair_gradients(dp, scale, scores, images, col, col_got, okay, row, swap, text_emb, emb_a, emb_b)
    back = links.core(other)

    h = d // 2
    layout = (0, ff + h, (ff, 2 * ff + h))
    sum_ffn, gmid, datt, gain2 = backward_ffn(
        links.padded(2 * ff + d), layout, scale, part, back, row, swap, emb_a, emb_b, u, flen, hpool,
        row_len, n2, slope, xhat2, rstd2, att, txt_gains, txt_down, txt_up, txt_out, txt,
    )
    first = Reduction(links, sum_ffn)
    cols = jnp.stack([txt_gains[0], txt_shifts[0]], 1)
    held = []
    for piece in range(2):
        first.start()
        held = backward_attention(piece, 2, held, links.padded(3 * d), datt, qkv, probs, n1, cols, txt_qkv)
        datt, first.got, *held = beside(datt, first.got, *held)
        first.end()
    gq, sum_qkv, gain1 = held
    gain1 = gain1.T
    small = jnp.concatenate(
        [gain1[0:1], gain2[0:1], gain1[1:2], gain2[1:2], jnp.broadcast_to(sums[0:2, 0:1], (2, d)), jnp.zeros((2, d), f32)], 0
    )
    second = Reduction(links, sum_qkv, small)
    dx = None
    while first.plan or second.plan:
        if first.plan:
            first.start()
        second.start()
        if dx is None:
            dx = backward_input(gq, gmid, xhat1, rstd1, txt_gains, txt_qkv)
        if first.got is not None and first.kind != "done":
            first.got, second.got = beside(first.got, second.got)
            first.end()
            if not first.plan:
                segments = [(0, ff, 0, 0, 0), (layout[2][0], h, 1, 0, 0), (layout[2][1], h, 1, h, 0)]
                segments += [(layout[1] + i * d, d, 2, 0, i * d) for i in range(ff // d)]
                grad_down, grad_out, grad_up = finish(rep, first.x, first.got, [(ff, d), (d, d), (d, ff)], segments)
                first.kind = "done"
        second.end()
    (grad_qkv,) = finish(rep, second.x, second.got, [(d, 3 * d)], [(i * d, d, 0, 0, i * d) for i in range(3)])
    small = second.small
    return (
        small[4, 0],
        small[0:2],
        small[2:4],
        grad_qkv,
        grad_out,
        grad_up,
        grad_down,
        small[5, 0],
        dx.reshape(pairs, txt, d),
    )


def solution(mesh):
    both = ("dp", "rep")
    deep = P(both, None, None)
    in_specs = (deep,) + (P(),) * 6 + (deep, P(both), P(both)) + (P(),) * 7
    out_specs = (P(),) * 8 + (deep,)
    return jax.shard_map(
        functools.partial(body, Links(mesh)), mesh=mesh, in_specs=in_specs, out_specs=out_specs, check_vma=False
    )
```

```python
import functools
import jax
import jax.numpy as jnp
from jax import lax
from jax.experimental import pallas as pl
from jax.experimental.pallas import tpu as pltpu
from jax.sharding import PartitionSpec as P

HEAD = 64
LANES = 128
f32 = jnp.float32
bf16 = jnp.bfloat16
GELU_C = 0.7978845608028654
GELU_A = 0.044715
SHIFT = 50.0
SAFE = 80.0
NOTE = 16
PITCH = 8
VMEM = 60 * 1024 * 1024


def dot(a, b):
    return jnp.dot(a, b, preferred_element_type=f32)


def dot_nt(a, b):
    return lax.dot_general(a, b, (((1,), (1,)), ((), ())), preferred_element_type=f32)


def dot_tn(a, b):
    return lax.dot_general(a, b, (((0,), (0,)), ((), ())), preferred_element_type=f32)


def norm_parts(x):
    mu = jnp.mean(x, -1, keepdims=True)
    c = x - mu
    rstd = lax.rsqrt(jnp.mean(c * c, -1, keepdims=True) + 1e-6)
    return c * rstd, rstd


def whole(a):
    return pl.BlockSpec(a.shape, lambda *_: (0,) * a.ndim)


def params():
    return pltpu.CompilerParams(vmem_limit_bytes=VMEM)


def cost(us):
    return pl.CostEstimate(flops=int(us * 1.1e9), bytes_accessed=0, transcendentals=0)


def split_bf16(v):
    hi = v.astype(bf16)
    return hi, (v - hi.astype(f32)).astype(bf16)


def count_rows(valid_ref, d):
    count = jnp.sum(valid_ref[...].astype(f32), 1, keepdims=True)
    return jnp.broadcast_to(count, (NOTE, d)).astype(bf16)


def stack_heads(a, low, zero):
    return jnp.concatenate([jnp.where(low, a, zero), jnp.where(low, zero, a)], 0)


def image_kernel(
    seqs, x_ref, valid_ref, gains_ref, shifts_ref, wqkv_ref, wo_ref, wup_ref, wdown_ref, out_ref,
    qkv, att, sc, ec, hs, ms,
):
    tokens, _, d = x_ref.shape
    pad = -(-tokens // 8) * 8
    pitch = seqs + PITCH
    rows, pair = seqs * tokens, 2 * pad
    step = pl.program_id(0)
    ff = wup_ref.shape[1]
    hp = d // LANES

    @pl.when(step == 0)
    def _():
        qkv[:, tokens * pitch :] = jnp.zeros((3 * hp, (pad - tokens) * pitch, LANES), f32)

    x = x_ref[...].astype(f32).reshape(rows, d)
    n1 = (norm_parts(x)[0] * gains_ref[0:1, :] + shifts_ref[0:1, :]).astype(bf16)
    for c in range(3):
        r = dot(n1, wqkv_ref[:, c * d : (c + 1) * d])
        r = r * HEAD**-0.5 if c == 0 else r
        for p in range(hp):
            for t in range(tokens):
                qkv[c * hp + p, t * pitch : t * pitch + seqs] = r[t * seqs : (t + 1) * seqs, p * LANES : (p + 1) * LANES]

    low = lax.broadcasted_iota(jnp.int32, (pair, LANES), 1) < HEAD
    key_lane = lax.broadcasted_iota(jnp.int32, (pair, 2 * pair), 1)
    query_row = lax.broadcasted_iota(jnp.int32, (pair, 2 * pair), 0)
    first_head = key_lane < pair
    key_row = jnp.where(first_head, key_lane, key_lane - pair)
    second_image = key_row >= pad
    key_pos = jnp.where(second_image, key_row - pad, key_row)
    bias = jnp.where((key_pos < tokens) & (second_image == (query_row >= pad)), 0.0, -1e30)
    zero, one = jnp.zeros((pair, LANES), bf16), jnp.ones((pair, LANES), bf16)
    ones = stack_heads(one, low, zero)

    def pick(j, b):
        return jnp.concatenate([qkv[j, pl.ds(2 * b + i, pad, stride=pitch), :] for i in range(2)], 0).astype(bf16)

    def attend(b, p, e):
        v = stack_heads(pick(2 * hp + p, b), low, zero)
        o = dot(e, jnp.concatenate([v, ones], 1))
        o = o[:, :LANES] / o[:, LANES:]
        for i in range(2):
            att[p, pl.ds(2 * b + i, pad, stride=pitch), :] = o[i * pad : (i + 1) * pad]

    big = jnp.zeros((pair, 2 * pair), f32)
    for b in range(seqs // 2):
        for p in range(hp):
            s = dot_nt(pick(p, b), stack_heads(pick(hp + p, b), low, zero))
            big = jnp.maximum(big, jnp.abs(s))
            sc[b * hp + p] = s
    for i in range(seqs // 2 * hp):
        ec[i] = jnp.exp(sc[i] + bias).astype(bf16)
    for b in range(seqs // 2):
        for p in range(hp):
            attend(b, p, ec[b * hp + p])

    @pl.when(jnp.logical_not(jnp.max(big) < SAFE))
    def _():
        for b in range(seqs // 2):

            @pl.loop(0, hp)
            def _(p):
                s = sc[b * hp + p] + bias
                top0 = jnp.max(jnp.where(first_head, s, -2e30), -1, keepdims=True)
                top1 = jnp.max(jnp.where(first_head, -2e30, s), -1, keepdims=True)
                attend(b, p, jnp.exp(s - jnp.where(first_head, top0, top1)).astype(bf16))

    attended = jnp.concatenate(
        [jnp.concatenate([att[p, t * pitch : t * pitch + seqs] for p in range(hp)], 1) for t in range(tokens)], 0
    ).astype(bf16)
    mid = x_ref[...].astype(f32).reshape(rows, d) + dot(attended, wo_ref[...])
    at = pl.ds(pl.multiple_of(step * seqs, seqs), seqs)
    ms[at, :] = jnp.sum(mid.reshape(tokens, seqs, d), 0)
    n2 = (norm_parts(mid)[0] * gains_ref[1:2, :] + shifts_ref[1:2, :]).astype(bf16)
    chunk = 512
    for c in range(0, ff, chunk):
        v = dot(n2, wup_ref[:, c : c + chunk])
        t = jnp.tanh(v * (GELU_C + (GELU_C * GELU_A) * (v * v)))
        h = (0.5 * v) * (1.0 + t)
        hs[at, c : c + chunk] = jnp.sum(h.reshape(tokens, seqs, chunk), 0)

    @pl.when(step == pl.num_programs(0) - 1)
    def _():
        hi, lo = split_bf16(hs[...] * (1.0 / tokens))
        u = ms[...] * (1.0 / tokens) + dot(hi, wdown_ref[...]) + dot(lo, wdown_ref[...])
        n = u.shape[0]
        out_ref[:n] = (u * lax.rsqrt(jnp.sum(u * u, -1, keepdims=True) + 1e-6)).astype(bf16)
        if out_ref.shape[0] > n:
            out_ref[n:] = count_rows(valid_ref, d)


def image_embed(xt, valid, gains, shifts, wqkv, wo, wup, wdown, start, count, note, seqs=16):
    tokens, _, d = xt.shape
    ff = wup.shape[1]
    pad = -(-tokens // 8) * 8
    pitch = seqs + PITCH
    tiles = seqs // 2 * (d // LANES)
    first = start // seqs
    rows = count + (NOTE if note else 0)
    return pl.pallas_call(
        functools.partial(image_kernel, seqs),
        grid=(count // seqs,),
        in_specs=[pl.BlockSpec((tokens, seqs, d), lambda i: (0, i + first, 0))]
        + [whole(a) for a in (valid, gains, shifts, wqkv, wo, wup, wdown)],
        out_specs=pl.BlockSpec((rows, d), lambda i: (0, 0)),
        out_shape=jax.ShapeDtypeStruct((rows, d), bf16),
        scratch_shapes=[
            pltpu.VMEM((3 * d // LANES, pitch * pad, LANES), f32),
            pltpu.VMEM((d // LANES, pitch * pad, LANES), f32),
            pltpu.VMEM((tiles, 2 * pad, 4 * pad), f32),
            pltpu.VMEM((tiles, 2 * pad, 4 * pad), bf16),
            pltpu.VMEM((count, ff), f32),
            pltpu.VMEM((count, d), f32),
        ],
        compiler_params=params(),
        cost_estimate=cost(0.45 * count),
        name="image_block",
    )(xt, valid, gains, shifts, wqkv, wo, wup, wdown)


def real_tokens(length, txt):
    seqs = length.shape[0]
    spread = jnp.broadcast_to(length[:, None, :], (seqs, txt, 1)).reshape(seqs * txt, 1)
    pos = lax.broadcasted_iota(jnp.int32, (seqs * txt, 1), 0) % txt
    return jnp.where(pos.astype(f32) < spread, 1.0, 0.0)


def text_forward_kernel(
    txt, held, x_ref, key_ref, flen_ref, gains_ref, shifts_ref, wqkv_ref, wo_ref, wup_ref, wdown_ref, *refs,
):
    (n1_ref, qkv_ref, probs_ref, att_ref, n2_ref, slope_ref, stat_ref, hpool_ref, u_ref, emb_ref, ms, sc, ec) = refs[held:]
    step = pl.program_id(0)
    rows, d = x_ref.shape
    ff = wup_ref.shape[1]
    seqs = rows // txt
    x = x_ref[...].astype(f32)
    xhat1, rstd1 = norm_parts(x)
    n1 = (xhat1 * gains_ref[0:1, :] + shifts_ref[0:1, :]).astype(bf16)
    n1_ref[...] = n1
    qkv_ref[:, :d] = (dot(n1, wqkv_ref[:, :d]) * HEAD**-0.5).astype(bf16)
    qkv_ref[:, d:] = dot(n1, wqkv_ref[:, d:]).astype(bf16)
    low = lax.broadcasted_iota(jnp.int32, (LANES, LANES), 1) < HEAD
    same = (
        lax.broadcasted_iota(jnp.int32, (LANES, LANES), 0) // txt
        == lax.broadcasted_iota(jnp.int32, (LANES, LANES), 1) // txt
    )
    zero = jnp.zeros((LANES, LANES), bf16)
    hp = d // LANES
    tiles = [(g, p) for g in range(rows // LANES) for p in range(hp)]

    def attend(g, p, probs):
        r = slice(g * LANES, (g + 1) * LANES)
        probs_ref[g * hp + p] = probs
        v = qkv_ref[r, 2 * d + p * LANES : 2 * d + (p + 1) * LANES]
        att_ref[r, p * LANES : (p + 1) * LANES] = dot(probs, stack_heads(v, low, zero)).astype(bf16)

    def share(s, top):
        halves = []
        for h in range(2):
            sh = s[:, h * LANES : (h + 1) * LANES]
            e = jnp.exp(sh - jnp.max(sh, -1, keepdims=True)) if top else jnp.exp(sh)
            halves.append(e / jnp.sum(e, -1, keepdims=True))
        return jnp.concatenate(halves, 1).astype(bf16)

    big = jnp.zeros((LANES, 2 * LANES), f32)
    for g, p in tiles:
        r = slice(g * LANES, (g + 1) * LANES)
        bias = jnp.where(same & (key_ref[0, g : g + 1, :] > 0), 0.0, -1e30)
        q = qkv_ref[r, p * LANES : (p + 1) * LANES]
        k = qkv_ref[r, d + p * LANES : d + (p + 1) * LANES]
        s = dot_nt(q, stack_heads(k, low, zero))
        big = jnp.maximum(big, jnp.abs(s))
        sc[g * hp + p] = s + jnp.concatenate([bias, bias], 1)
    for g, p in tiles:
        ec[g * hp + p] = share(sc[g * hp + p], False)
    for g, p in tiles:
        attend(g, p, ec[g * hp + p])

    @pl.when(jnp.logical_not(jnp.max(big) < SAFE))
    def _():
        for g, p in tiles:
            attend(g, p, share(sc[g * hp + p], True))

    mid = x + dot(att_ref[...], wo_ref[...])
    xhat2, rstd2 = norm_parts(mid)
    lane = lax.broadcasted_iota(jnp.int32, (rows, LANES), 1)
    hi1, hi2 = rstd1.astype(bf16).astype(f32), rstd2.astype(bf16).astype(f32)
    stat = jnp.where(lane < 64, jnp.where(lane < 32, hi1, rstd1 - hi1), jnp.where(lane < 96, hi2, rstd2 - hi2))
    stat_ref[...] = stat.astype(bf16)
    at = pl.ds(pl.multiple_of(step * seqs, seqs), seqs)
    keep = real_tokens(flen_ref[at, :], txt)
    n2 = ((xhat2 * gains_ref[1:2, :] + shifts_ref[1:2, :]) * keep).astype(bf16)
    n2_ref[...] = n2
    ms[at, :] = jnp.sum((mid * keep).reshape(seqs, txt, d), 1)
    chunk = 512
    for c in range(0, ff, chunk):
        v = dot(n2, wup_ref[:, c : c + chunk])
        v2 = v * v
        t = jnp.tanh(v * (GELU_C + (GELU_C * GELU_A) * v2))
        half = 0.5 + 0.5 * t
        h = v * half
        slope = half + h * (1.0 - t) * (GELU_C + (3.0 * GELU_C * GELU_A) * v2)
        slope_ref[:, c : c + chunk] = (slope * keep).astype(bf16)
        hpool_ref[at, c : c + chunk] = jnp.sum(h.reshape(seqs, txt, chunk), 1)

    @pl.when(step == pl.num_programs(0) - 1)
    def _():
        hi, lo = split_bf16(hpool_ref[...])
        pooled = ms[...] + dot(hi, wdown_ref[...]) + dot(lo, wdown_ref[...])
        u = pooled / flen_ref[...]
        u_ref[...] = u
        emb_ref[...] = (u * lax.rsqrt(jnp.sum(u * u, -1, keepdims=True) + 1e-6)).astype(bf16)


def text_forward(piece, pieces, held, x, key_ok, flen, gains, shifts, wqkv, wo, wup, wdown, txt, rows=512):
    total, d = x.shape
    ff = wup.shape[1]
    pairs = total // txt
    hp = d // LANES
    part = pairs // pieces
    steps = total // pieces // rows
    first = piece * steps
    block = lambda *tail: pl.BlockSpec((rows,) + tail, lambda i: (i + first,) + (0,) * len(tail))
    still = lambda *shape: pl.BlockSpec(shape, lambda i: (piece, 0))
    shape = jax.ShapeDtypeStruct
    key3 = key_ok.reshape(total // rows, rows // LANES, LANES)
    args = (x, key3, flen, gains, shifts, wqkv, wo, wup, wdown)
    return pl.pallas_call(
        functools.partial(text_forward_kernel, txt, len(held)),
        grid=(steps,),
        in_specs=[
            block(d), pl.BlockSpec((1, rows // LANES, LANES), lambda i: (i + first, 0, 0)), still(part, 1)
        ]
        + [whole(a) for a in args[3:]]
        + [pl.BlockSpec(memory_space=pl.ANY)] * len(held),
        out_specs=[
            block(d), block(3 * d), pl.BlockSpec((rows // LANES * hp, LANES, 2 * LANES), lambda i: (i + first, 0, 0)),
            block(d), block(d), block(ff), block(LANES), still(part, ff), still(part, d), still(part, d),
        ],
        out_shape=[
            shape((total, d), bf16), shape((total, 3 * d), bf16), shape((total // LANES * hp, LANES, 2 * LANES), bf16),
            shape((total, d), bf16), shape((total, d), bf16), shape((total, ff), bf16), shape((total, LANES), bf16),
            shape((pairs, ff), f32), shape((pairs, d), f32), shape((pairs, d), bf16),
        ],
        input_output_aliases={len(args) + i: i for i in range(len(held))},
        scratch_shapes=[
            pltpu.VMEM((part, d), f32),
            pltpu.VMEM((rows // LANES * hp, LANES, 2 * LANES), f32),
            pltpu.VMEM((rows // LANES * hp, LANES, 2 * LANES), bf16),
        ],
        compiler_params=params(),
        cost_estimate=cost(0.013 * total / pieces),
        name="text_forward",
    )(*args, *held)


def scores_kernel(
    group, place_ref, own_ref, other_ref, mask_ref, scale_ref, a0_ref, a1_ref,
    s_ref, all_ref, col_out, okay_out, row_out,
):
    step = pl.program_id(0)
    pairs = own_ref.shape[0]
    scale = scale_ref[0]
    mask = mask_ref[...]
    inner = lax.rem(place_ref[0], group)
    late = lax.bitwise_xor(step, lax.div(place_ref[0], group)) >= pl.num_programs(0) // 2
    texts = jnp.concatenate([own_ref[...], other_ref[...]], 0)

    @pl.when(step == 0)
    def _():
        row_out[...] = jnp.zeros_like(row_out)
        row_out[:, 3:4] = mask

    lane = lax.broadcasted_iota(jnp.int32, (1, pairs), 1).astype(f32)
    for k in range(group):
        at = lax.bitwise_xor(k, inner)
        cols = slice(k * pairs, (k + 1) * pairs)
        a = jnp.where(late, a1_ref[at], a0_ref[at])
        images = a[:pairs]
        count = a[pairs : pairs + 1, 0:1].astype(f32)
        okay = jnp.where(lane < count, 1.0, 0.0)
        okay_out[0:1, cols] = okay
        all_ref[cols, :] = images
        s = scale * dot_nt(texts, images)
        s_ref[:, cols] = s
        up = jnp.exp(s - SHIFT)
        down = jnp.exp(jnp.minimum(s, 0.0) + SHIFT)
        col_out[0:1, cols] = jnp.sum(up * mask, 0, keepdims=True)
        col_out[1:2, cols] = jnp.sum(down * mask, 0, keepdims=True)
        row_out[:, 0:1] += jnp.sum(up * okay, 1, keepdims=True)
        row_out[:, 1:2] += jnp.sum(down * okay, 1, keepdims=True)
        row_out[:, 2:3] += jnp.broadcast_to(count, (2 * pairs, 1))


def pair_scores(place, own, other, mask, scale, a0, a1):
    slots, _, d = a0.shape
    pairs = own.shape[0]
    group = min(8, slots)
    groups = slots // group
    cols = group * pairs
    keep = lambda *_: (0, 0)
    turn = lambda i, s: (lax.rem(lax.bitwise_xor(i, lax.div(s[0], group)), groups), 0, 0)
    still = lambda a: pl.BlockSpec(a.shape, keep)
    shape = jax.ShapeDtypeStruct
    return pl.pallas_call(
        functools.partial(scores_kernel, group),
        grid_spec=pltpu.PrefetchScalarGridSpec(
            num_scalar_prefetch=1,
            grid=(2 * groups,),
            in_specs=[still(own), still(other), still(mask), pl.BlockSpec(memory_space=pltpu.SMEM)]
            + [pl.BlockSpec((group,) + a.shape[1:], turn) for a in (a0, a1)],
            out_specs=[
                pl.BlockSpec((2 * pairs, cols), lambda i, s: (0, i)),
                pl.BlockSpec((cols, d), lambda i, s: (i, 0)),
                pl.BlockSpec((2, cols), lambda i, s: (0, i)),
                pl.BlockSpec((1, cols), lambda i, s: (0, i)),
                pl.BlockSpec((2 * pairs, 4), keep),
            ],
        ),
        out_shape=[
            shape((2 * pairs, 2 * groups * cols), f32), shape((2 * groups * cols, d), bf16),
            shape((2, 2 * groups * cols), f32), shape((1, 2 * groups * cols), f32), shape((2 * pairs, 4), f32),
        ],
        compiler_params=params(),
        cost_estimate=cost(4.0),
        name="pair_scores",
    )(place, own, other, mask, scale, a0, a1)


def log_sum(up, down):
    fine = up >= 1.9287498479639178e-22
    return jnp.where(
        fine, jnp.log(jnp.where(fine, up, 1.0)) + SHIFT, jnp.log(jnp.where(fine, 1.0, down)) - SHIFT
    )


def gradient_kernel(
    dp, scale_ref, s_ref, all_ref, col_ref, got_ref, okay_ref, row_ref, swap_ref, text_ref, a_ref,
    grad_ref, back_ref, loss_ref,
):
    step = pl.program_id(0)
    pairs = text_ref.shape[0]
    row = row_ref[...] + jnp.concatenate([swap_ref[pairs:], swap_ref[:pairs]], 0)
    factor = 0.5 / row[0:1, 2:3]
    mask = row_ref[:, 3:4]
    okay = okay_ref[...]
    row_lse = log_sum(row[:, 0:1], row[:, 1:2])
    col = col_ref[...] + got_ref[...]
    col_lse = log_sum(col[0:1, :], col[1:2, :])

    @pl.when(step == 0)
    def _():
        grad_ref[...] = jnp.zeros_like(grad_ref)
        back_ref[...] = jnp.zeros_like(back_ref)
        loss_ref[...] = jnp.zeros_like(loss_ref)
        t = text_ref[...].astype(f32) * a_ref[:pairs].astype(f32)
        diag = scale_ref[0] * jnp.sum(t, -1, keepdims=True)
        m = mask[:pairs]
        loss_ref[0:1, 0:1] = factor * jnp.sum(m * (row_lse[:pairs] - 2.0 * diag), 0, keepdims=True)
        loss_ref[1:2, 0:1] = -2.0 * factor * jnp.sum(m * diag, 0, keepdims=True)

    s = s_ref[...]
    g = jnp.exp(jnp.minimum(s - row_lse, 1.0)) + jnp.exp(jnp.minimum(s - col_lse, 1.0))
    g = g * ((factor * mask) * okay)
    grad = dot(g.astype(bf16), all_ref[...])
    grad_ref[...] += grad[:pairs]
    back_ref[...] += grad[pairs:]
    cols = jnp.sum(jnp.where(okay > 0, col_lse, 0.0), 1, keepdims=True)
    loss_ref[0:1, 0:1] += factor * (cols * (1.0 / dp))
    loss_ref[1:2, 0:1] += jnp.sum(jnp.sum(g * s, 0, keepdims=True), 1, keepdims=True)


def pair_gradients(dp, scale, scores, images, col, got, okay, row, swap, texts, a):
    pairs, d = texts.shape
    cols = min(8, dp) * pairs
    still = lambda *shape: pl.BlockSpec(shape, lambda i: (0, 0))
    shape = jax.ShapeDtypeStruct
    return pl.pallas_call(
        functools.partial(gradient_kernel, dp),
        grid=(dp * pairs // cols,),
        in_specs=[
            pl.BlockSpec(memory_space=pltpu.SMEM),
            pl.BlockSpec((2 * pairs, cols), lambda i: (0, i)),
            pl.BlockSpec((cols, d), lambda i: (i, 0)),
            pl.BlockSpec((2, cols), lambda i: (0, i)),
            pl.BlockSpec((2, cols), lambda i: (0, i)),
            pl.BlockSpec((1, cols), lambda i: (0, i)),
        ]
        + [whole(x) for x in (row, swap, texts, a)],
        out_specs=[still(pairs, d), still(pairs, d), still(8, LANES)],
        out_shape=[shape((pairs, d), f32), shape((pairs, d), f32), shape((8, LANES), f32)],
        compiler_params=params(),
        cost_estimate=cost(3.0),
        name="pair_gradients",
    )(scale, scores, images, col, got, okay, row, swap, texts, a)


def backward_ffn_kernel(
    txt, layout, scale_ref, part_ref, back_ref, row_ref, swap_ref, a_ref, u_ref, len_ref, hpool_ref,
    n2_ref, slope_ref, stat_ref, att_ref, gains_ref, shifts_ref, wdown_ref, wup_ref, wo_ref,
    sum_ref, gmid_ref, datt_ref, gain_ref, dh, gd, acc_up, acc_o,
):
    step = pl.program_id(0)
    rows, d = n2_ref.shape
    ff = wup_ref.shape[1]
    seqs = rows // txt
    down_at, up_at, out_at = layout

    @pl.when(step == 0)
    def _():
        pairs = part_ref.shape[0]
        scale = scale_ref[0]
        factor = 0.5 / (row_ref[0:1, 2:3] + swap_ref[0:1, 2:3])
        images = a_ref[:pairs].astype(f32)
        u = u_ref[...]
        r = lax.rsqrt(jnp.sum(u * u, -1, keepdims=True) + 1e-6)
        g = scale * (part_ref[...] + back_ref[...]) - (2.0 * scale) * (factor * row_ref[:pairs, 3:4]) * images
        du = (r * g - (r * r * r) * u * jnp.sum(u * g, -1, keepdims=True)) / len_ref[...]
        gd[...] = du
        low = du.astype(bf16)
        dh[...] = dot_nt(low, wdown_ref[...])
        hi, lo = split_bf16(hpool_ref[...])
        sum_ref[down_at : down_at + ff] = (dot_tn(hi, low) + dot_tn(lo, low)).astype(bf16)
        acc_up[...] = jnp.zeros_like(acc_up)
        acc_o[...] = jnp.zeros_like(acc_o)
        gain_ref[...] = jnp.zeros_like(gain_ref)

    at = pl.ds(pl.multiple_of(step * seqs, seqs), seqs)
    n2 = n2_ref[...]
    dn2 = jnp.zeros((rows, d), f32)
    chunk = 512
    for c in range(0, ff, chunk):
        cs = slice(c, c + chunk)
        spread = jnp.broadcast_to(dh[at, cs][:, None, :], (seqs, txt, chunk)).reshape(rows, chunk)
        grad_before = (spread * slope_ref[:, cs].astype(f32)).astype(bf16)
        acc_up[:, cs] += dot_tn(n2, grad_before)
        dn2 += dot_nt(grad_before, wup_ref[:, cs])
    xhat = (n2.astype(f32) - shifts_ref[1:2, :]) / gains_ref[1:2, :]
    stat = stat_ref[...].astype(f32)
    gain_ref[0:1, :] += jnp.sum(dn2 * xhat, 0, keepdims=True)
    gain_ref[1:2, :] += jnp.sum(dn2, 0, keepdims=True)
    gn = dn2 * gains_ref[1:2, :]
    dmid = (stat[:, 64:65] + stat[:, 96:97]) * (
        gn - jnp.mean(gn, -1, keepdims=True) - xhat * jnp.mean(gn * xhat, -1, keepdims=True)
    )
    keep = real_tokens(len_ref[at, :], txt)
    direct = jnp.broadcast_to(gd[at, :][:, None, :], (seqs, txt, d)).reshape(rows, d)
    gmid = direct * keep + dmid
    gmid_ref[...] = gmid
    branch = gmid.astype(bf16)
    acc_o[...] += dot_tn(att_ref[...], branch)
    datt_ref[...] = dot_nt(branch, wo_ref[...]).astype(bf16)

    @pl.when(step == pl.num_programs(0) - 1)
    def _():
        for b in range(ff // d):
            sum_ref[up_at + b * d : up_at + (b + 1) * d, :] = acc_up[:, b * d : (b + 1) * d].astype(bf16)
        for b in range(2):
            sum_ref[out_at[b] : out_at[b] + d // 2, :] = acc_o[b * d // 2 : (b + 1) * d // 2, :].astype(bf16)
        clear_tail(sum_ref, out_at[1] + d // 2)


def clear_tail(ref, n):
    if ref.shape[0] > n:
        ref[n:] = jnp.zeros((ref.shape[0] - n,) + ref.shape[1:], ref.dtype)


def backward_ffn(
    total, layout, scale, part, back, row, swap, a, u, flen, hpool, n2, slope, stat, att,
    gains, shifts, wdown, wup, wo, txt, rows=512,
):
    tokens, d = n2.shape
    pairs, ff = hpool.shape
    block = lambda w: pl.BlockSpec((rows, w), lambda i: (i, 0))
    still = lambda *shape: pl.BlockSpec(shape, lambda i: (0, 0))
    shape = jax.ShapeDtypeStruct
    return pl.pallas_call(
        functools.partial(backward_ffn_kernel, txt, layout),
        grid=(tokens // rows,),
        in_specs=[pl.BlockSpec(memory_space=pltpu.SMEM)]
        + [whole(x) for x in (part, back, row, swap, a, u, flen, hpool)]
        + [block(d), block(ff), block(LANES), block(d)]
        + [whole(x) for x in (gains, shifts, wdown, wup, wo)],
        out_specs=[still(total, d), block(d), block(d), still(8, d)],
        out_shape=[shape((total, d), bf16), shape((tokens, d), f32), shape((tokens, d), bf16), shape((8, d), f32)],
        scratch_shapes=[
            pltpu.VMEM((pairs, ff), f32), pltpu.VMEM((pairs, d), f32), pltpu.VMEM((d, ff), f32), pltpu.VMEM((d, d), f32)
        ],
        compiler_params=params(),
        cost_estimate=cost(0.008 * tokens),
        name="backward_ffn",
    )(scale, part, back, row, swap, a, u, flen, hpool, n2, slope, stat, att, gains, shifts, wdown, wup, wo)


def backward_attention_kernel(
    held, last, datt_ref, qkv_ref, probs_ref, n1_ref, cols_ref, wqkv_ref, *refs
):
    old_acc, old_flat = refs[1:3] if held else (None, None)
    gq_ref, sum_ref, flat_ref, acc, flat = refs[held:]
    step = pl.program_id(0)
    rows, d = n1_ref.shape
    low = lax.broadcasted_iota(jnp.int32, (LANES, LANES), 1) < HEAD
    zero = jnp.zeros((LANES, LANES), bf16)

    @pl.when(step == 0)
    def _():
        acc[...] = old_acc[...] if held else jnp.zeros_like(acc)
        flat[...] = old_flat[...] if held else jnp.zeros_like(flat)

    for g in range(rows // LANES):
        r = slice(g * LANES, (g + 1) * LANES)
        for p in range(d // LANES):
            cq = slice(p * LANES, (p + 1) * LANES)
            ck = slice(d + p * LANES, d + (p + 1) * LANES)
            cv = slice(2 * d + p * LANES, 2 * d + (p + 1) * LANES)
            q, k, v, da = qkv_ref[r, cq], qkv_ref[r, ck], qkv_ref[r, cv], datt_ref[r, cq]
            low_probs = probs_ref[g * (d // LANES) + p]
            probs = low_probs.astype(f32)
            dprobs = dot_nt(da, stack_heads(v, low, zero))
            dv = dot_tn(low_probs, da)
            halves = []
            for h in range(2):
                hs = slice(h * LANES, (h + 1) * LANES)
                ph, dh = probs[:, hs], dprobs[:, hs]
                halves.append(ph * (dh - jnp.sum(ph * dh, -1, keepdims=True)))
            ds = jnp.concatenate(halves, 1).astype(bf16)
            gq_ref[r, cq] = (dot(ds, stack_heads(k, low, zero)) * HEAD**-0.5).astype(bf16)
            dk = dot_tn(ds, q)
            gq_ref[r, ck] = jnp.where(low, dk[:LANES], dk[LANES:]).astype(bf16)
            gq_ref[r, cv] = jnp.where(low, dv[:LANES], dv[LANES:]).astype(bf16)
    gq = gq_ref[...]
    acc[...] += dot_tn(n1_ref[...], gq)
    flat[0:1, :] += jnp.sum(gq.astype(f32), 0, keepdims=True)

    @pl.when(step == pl.num_programs(0) - 1)
    def _():
        if not last:
            sum_ref[...] = acc[...]
            flat_ref[...] = flat[...]
            return
        for b in range(3):
            sum_ref[b * d : (b + 1) * d, :] = acc[:, b * d : (b + 1) * d].astype(bf16)
        clear_tail(sum_ref, 3 * d)
        w = wqkv_ref[...].astype(f32)
        total = flat[0:1, :]
        spread = jnp.sum((acc[...] - cols_ref[:, 1:2] * total) * w, 1, keepdims=True)
        flat_ref[:, 0:1] = spread / cols_ref[:, 0:1]
        flat_ref[:, 1:2] = jnp.sum(total * w, 1, keepdims=True)


def backward_attention(piece, pieces, held, total, datt, qkv, probs, n1, cols, wqkv, rows=512):
    tokens, d = n1.shape
    steps = tokens // pieces // rows
    first = piece * steps
    last = piece == pieces - 1
    block = lambda w: pl.BlockSpec((rows, w), lambda i: (i + first, 0))
    shape = jax.ShapeDtypeStruct
    outs = (
        [shape((total, d), bf16), shape((d, 2), f32)] if last else [shape((d, 3 * d), f32), shape((8, 3 * d), f32)]
    )
    args = (datt, qkv, probs, n1, cols, wqkv)
    return pl.pallas_call(
        functools.partial(backward_attention_kernel, len(held), last),
        grid=(steps,),
        in_specs=[
            block(d), block(3 * d),
            pl.BlockSpec((rows // LANES * (d // LANES), LANES, 2 * LANES), lambda i: (i + first, 0, 0)),
            block(d), whole(cols), whole(wqkv),
        ]
        + ([pl.BlockSpec(memory_space=pl.ANY)] + [whole(x) for x in held[1:]] if held else []),
        out_specs=[block(3 * d)] + [whole(x) for x in outs],
        out_shape=[shape((tokens, 3 * d), bf16)] + outs,
        input_output_aliases={len(args): 0} if held else {},
        scratch_shapes=[pltpu.VMEM((d, 3 * d), f32), pltpu.VMEM((8, 3 * d), f32)],
        compiler_params=params(),
        cost_estimate=cost(0.009 * tokens / pieces),
        name="backward_attention",
    )(*args, *held)


def backward_input_kernel(gq_ref, gmid_ref, n1_ref, stat_ref, gains_ref, shifts_ref, wqkv_ref, dx_ref):
    gn = dot_nt(gq_ref[...], wqkv_ref[...]) * gains_ref[0:1, :]
    xhat = (n1_ref[...].astype(f32) - shifts_ref[0:1, :]) / gains_ref[0:1, :]
    stat = stat_ref[...].astype(f32)
    dx_ref[...] = gmid_ref[...] + (stat[:, 0:1] + stat[:, 32:33]) * (
        gn - jnp.mean(gn, -1, keepdims=True) - xhat * jnp.mean(gn * xhat, -1, keepdims=True)
    )


def backward_input(gq, gmid, n1, stat, gains, shifts, wqkv, rows=512):
    tokens, d = gmid.shape
    block = lambda w: pl.BlockSpec((rows, w), lambda i: (i, 0))
    return pl.pallas_call(
        backward_input_kernel,
        grid=(tokens // rows,),
        in_specs=[block(3 * d), block(d), block(d), block(LANES), whole(gains), whole(shifts), whole(wqkv)],
        out_specs=block(d),
        out_shape=jax.ShapeDtypeStruct((tokens, d), f32),
        compiler_params=params(),
        cost_estimate=cost(0.004 * tokens),
        name="backward_input",
    )(gq, gmid, n1, stat, gains, shifts, wqkv)


def finish_kernel(places, rep_ref, own_ref, got_ref, *out_refs):
    first = rep_ref[0] == 0
    for out, top, left, begin, n, part in places:
        a = own_ref[begin : begin + n, :]
        b = got_ref[begin : begin + n, :]
        mine = first if part == 0 else jnp.logical_not(first)
        out_refs[out][top : top + n, left : left + a.shape[1]] = jnp.where(mine, a, b).astype(f32)


def finish(rep, own, got, shapes, segments):
    half = own.shape[0]
    places = []
    for row, count, out, top, left in segments:
        while count:
            part, begin = divmod(row, half)
            n = min(count, half - begin)
            places.append((out, top, left, begin, n, part))
            row, top, count = row + n, top + n, count - n
    outs = [jax.ShapeDtypeStruct(s, f32) for s in shapes]
    return pl.pallas_call(
        functools.partial(finish_kernel, places),
        grid=(1,),
        in_specs=[pl.BlockSpec(memory_space=pltpu.SMEM), whole(own), whole(got)],
        out_specs=[whole(x) for x in outs],
        out_shape=outs,
        compiler_params=params(),
        cost_estimate=cost(3.0),
        name="finish",
    )(rep, own, got)


class Links:
    def __init__(self, mesh):
        self.dp, self.rep = mesh.shape["dp"], mesh.shape["rep"]
        self.bits = (self.dp - 1).bit_length()
        assert self.dp == 1 << self.bits and self.rep == 2
        near, far = list(range(min(2, self.bits))), list(range(2, self.bits))
        turn = lambda bits: list(zip(bits, bits[::-1]))
        self.near, self.far = turn(near), turn(far)
        self.gather_order = [(b, b) for b in far[::-1]] + self.near

    def bit(self, pair):
        place = lax.axis_index("dp")
        return jnp.where(lax.axis_index("rep") == 0, (place >> pair[0]) & 1, (place >> pair[1]) & 1)

    def across(self, x, pair):
        moves = [(2 * i + r, 2 * (i ^ (1 << pair[r])) + r) for i in range(self.dp) for r in range(2)]
        return lax.ppermute(x, ("dp", "rep"), moves)

    def core(self, x):
        return lax.ppermute(x, "rep", [(0, 1), (1, 0)])

    def padded(self, n):
        unit = self.rep * self.dp
        return -(-n // unit) * unit


class Reduction:
    def __init__(self, links, x, small=None):
        self.links, self.x, self.small = links, x, small
        self.plan = (
            [("core", None)]
            + [("half", p) for p in links.near]
            + [("full", p) for p in links.far]
            + [("join", p) for p in links.near[::-1]]
            + [("last", None)]
        )
        self.got = None

    def start(self):
        links = self.links
        kind, pair = self.kind, self.pair = self.plan.pop(0)
        x = self.x
        if kind in ("core", "half"):
            n = x.shape[0] // 2
            self.v = lax.axis_index("rep") if kind == "core" else links.bit(pair)
            send = lax.dynamic_slice_in_dim(x, (1 - self.v) * n, n)
        else:
            send = x
        if self.small is not None and kind in ("core", "half", "full"):
            send = jnp.concatenate([send, *split_bf16(self.small)], 0)
        self.got = links.core(send) if kind in ("core", "last") else links.across(send, pair)

    def end(self):
        kind, got, x = self.kind, self.got, self.x
        if kind == "last":
            return
        if kind == "join":
            low = self.links.bit(self.pair) == 0
            self.x = jnp.where(low, jnp.concatenate([x, got], 0), jnp.concatenate([got, x], 0))
            return
        n = x.shape[0]
        if kind in ("core", "half"):
            n = n // 2
            x = lax.dynamic_slice_in_dim(x, self.v * n, n)
        self.x = (x.astype(f32) + got[:n].astype(f32)).astype(bf16)
        if self.small is not None:
            m = self.small.shape[0]
            self.small = self.small + (got[n : n + m].astype(f32) + got[n + m :].astype(f32))


def beside(*values):
    return lax.optimization_barrier(values)


def body(
    links, image_in, img_gains, img_shifts, img_qkv, img_out, img_up, img_down, text_in, lengths, valid,
    txt_gains, txt_shifts, txt_qkv, txt_out, txt_up, txt_down, log_scale,
):
    dp, bits = links.dp, links.bits
    pairs, txt, d = text_in.shape
    ff = txt_up.shape[1]
    tokens = pairs * txt
    scale = jnp.exp(log_scale).reshape(1)
    rep = lax.axis_index("rep").astype(jnp.int32).reshape(1)
    order = links.gather_order

    own_mask = valid.astype(f32)
    row_mask = jnp.concatenate([own_mask, links.core(own_mask)])[:, None]
    flen = lengths.astype(f32)[:, None]
    key_ok = (jnp.arange(txt)[None, :] < lengths[:, None]).astype(f32).reshape(tokens // LANES, LANES)

    image_args = (valid[None, :], img_gains, img_shifts, img_qkv, img_out, img_up, img_down)
    emb = image_embed(image_in.transpose(1, 0, 2), *image_args, 0, pairs, True)
    text_args = (txt_gains, txt_shifts, txt_qkv, txt_out, txt_up, txt_down)
    text_x, emb = beside(text_in.reshape(tokens, d), emb)
    steps, pieces = list(order), 4
    a, held = emb[None], []
    for piece in range(pieces):
        if steps:
            got = links.across(a, steps.pop(0))
        held = list(text_forward(piece, pieces, held, text_x, key_ok, flen, *text_args, txt))
        if steps:
            text_x, got, held[-1] = beside(text_x, got, held[-1])
            a = jnp.concatenate([a, got], 0)
    while steps:
        got = links.across(a, steps.pop(0))
        if steps:
            a = jnp.concatenate([a, got], 0)
    n1, qkv, probs, att, n2, slope, stat, hpool, u, text_emb = held

    place = sum(links.bit(order[i]) << i for i in range(bits)).astype(jnp.int32).reshape(1)
    scores, images, col, okay, row = pair_scores(
        place, text_emb, links.core(text_emb), row_mask, scale, a, got
    )
    swap = links.core(row)
    for pair in order[:-1]:
        col = col + links.across(col, pair)
    col_got = links.across(col, order[-1])
    part, other, sums = pair_gradients(dp, scale, scores, images, col, col_got, okay, row, swap, text_emb, emb)
    back = links.core(other)

    h = d // 2
    layout = (0, ff + h, (ff, 2 * ff + h))
    sum_ffn, gmid, datt, gain2 = backward_ffn(
        links.padded(2 * ff + d), layout, scale, part, back, row, swap, emb, u, flen, hpool,
        n2, slope, stat, att, txt_gains, txt_shifts, txt_down, txt_up, txt_out, txt,
    )
    first = Reduction(links, sum_ffn)
    cols = jnp.stack([txt_gains[0], txt_shifts[0]], 1)
    held = []
    for piece in range(2):
        first.start()
        held = backward_attention(piece, 2, held, links.padded(3 * d), datt, qkv, probs, n1, cols, txt_qkv)
        datt, first.got, *held = beside(datt, first.got, *held)
        first.end()
    gq, sum_qkv, gain1 = held
    gain1 = gain1.T
    small = jnp.concatenate(
        [gain1[0:1], gain2[0:1], gain1[1:2], gain2[1:2], jnp.broadcast_to(sums[0:2, 0:1], (2, d)), jnp.zeros((2, d), f32)], 0
    )
    second = Reduction(links, sum_qkv, small)
    dx = None
    while first.plan or second.plan:
        if first.plan:
            first.start()
        second.start()
        if dx is None:
            dx = backward_input(gq, gmid, n1, stat, txt_gains, txt_shifts, txt_qkv)
        if first.got is not None and first.kind != "done":
            first.got, second.got = beside(first.got, second.got)
            first.end()
            if not first.plan:
                segments = [(0, ff, 0, 0, 0), (layout[2][0], h, 1, 0, 0), (layout[2][1], h, 1, h, 0)]
                segments += [(layout[1] + i * d, d, 2, 0, i * d) for i in range(ff // d)]
                grad_down, grad_out, grad_up = finish(rep, first.x, first.got, [(ff, d), (d, d), (d, ff)], segments)
                first.kind = "done"
        second.end()
    (grad_qkv,) = finish(rep, second.x, second.got, [(d, 3 * d)], [(i * d, d, 0, 0, i * d) for i in range(3)])
    small = second.small
    return (
        small[4, 0],
        small[0:2],
        small[2:4],
        grad_qkv,
        grad_out,
        grad_up,
        grad_down,
        small[5, 0],
        dx.reshape(pairs, txt, d),
    )


def solution(mesh):
    both = ("dp", "rep")
    deep = P(both, None, None)
    in_specs = (deep,) + (P(),) * 6 + (deep, P(both), P(both)) + (P(),) * 7
    out_specs = (P(),) * 8 + (deep,)
    return jax.shard_map(
        functools.partial(body, Links(mesh)), mesh=mesh, in_specs=in_specs, out_specs=out_specs, check_vma=False
    )
```

```python
import functools
import jax
import jax.numpy as jnp
from jax import lax
from jax.experimental import pallas as pl
from jax.experimental.pallas import tpu as pltpu
from jax.sharding import PartitionSpec as P

HEAD = 64
LANES = 128
f32 = jnp.float32
bf16 = jnp.bfloat16
GELU_C = 0.7978845608028654
GELU_A = 0.044715
SHIFT = 50.0
SAFE = 80.0
NOTE = 16
PITCH = 8
VMEM = 60 * 1024 * 1024
HOP_VMEM = 12 * 1024 * 1024


def dot(a, b):
    return jnp.dot(a, b, preferred_element_type=f32)


def dot_nt(a, b):
    return lax.dot_general(a, b, (((1,), (1,)), ((), ())), preferred_element_type=f32)


def dot_tn(a, b):
    return lax.dot_general(a, b, (((0,), (0,)), ((), ())), preferred_element_type=f32)


def norm_parts(x):
    mu = jnp.mean(x, -1, keepdims=True)
    c = x - mu
    rstd = lax.rsqrt(jnp.mean(c * c, -1, keepdims=True) + 1e-6)
    return c * rstd, rstd


def whole(a):
    return pl.BlockSpec(a.shape, lambda *_: (0,) * a.ndim)


def params(limit=VMEM):
    return pltpu.CompilerParams(vmem_limit_bytes=limit)


def cost(us):
    return pl.CostEstimate(flops=int(us * 1.1e9), bytes_accessed=0, transcendentals=0)


def split_bf16(v):
    hi = v.astype(bf16)
    return hi, (v - hi.astype(f32)).astype(bf16)


def count_rows(valid_ref, d):
    count = jnp.sum(valid_ref[...].astype(f32), 1, keepdims=True)
    return jnp.broadcast_to(count, (NOTE, d)).astype(bf16)


def stack_heads(a, low, zero):
    return jnp.concatenate([jnp.where(low, a, zero), jnp.where(low, zero, a)], 0)


def image_kernel(
    seqs, x_ref, valid_ref, gains_ref, shifts_ref, wqkv_ref, wo_ref, wup_ref, wdown_ref, out_ref,
    qkv, att, sc, ec, hs, ms,
):
    tokens, _, d = x_ref.shape
    pad = -(-tokens // 8) * 8
    pitch = seqs + PITCH
    rows, pair = seqs * tokens, 2 * pad
    step = pl.program_id(0)
    ff = wup_ref.shape[1]
    hp = d // LANES

    @pl.when(step == 0)
    def _():
        qkv[:, tokens * pitch :] = jnp.zeros((3 * hp, (pad - tokens) * pitch, LANES), f32)

    x = x_ref[...].astype(f32).reshape(rows, d)
    n1 = (norm_parts(x)[0] * gains_ref[0:1, :] + shifts_ref[0:1, :]).astype(bf16)
    for c in range(3):
        r = dot(n1, wqkv_ref[:, c * d : (c + 1) * d])
        r = r * HEAD**-0.5 if c == 0 else r
        for p in range(hp):
            for t in range(tokens):
                qkv[c * hp + p, t * pitch : t * pitch + seqs] = r[t * seqs : (t + 1) * seqs, p * LANES : (p + 1) * LANES]

    low = lax.broadcasted_iota(jnp.int32, (pair, LANES), 1) < HEAD
    key_lane = lax.broadcasted_iota(jnp.int32, (pair, 2 * pair), 1)
    query_row = lax.broadcasted_iota(jnp.int32, (pair, 2 * pair), 0)
    first_head = key_lane < pair
    key_row = jnp.where(first_head, key_lane, key_lane - pair)
    second_image = key_row >= pad
    key_pos = jnp.where(second_image, key_row - pad, key_row)
    bias = jnp.where((key_pos < tokens) & (second_image == (query_row >= pad)), 0.0, -1e30)
    zero, one = jnp.zeros((pair, LANES), bf16), jnp.ones((pair, LANES), bf16)
    ones = stack_heads(one, low, zero)

    def pick(j, b):
        return jnp.concatenate([qkv[j, pl.ds(2 * b + i, pad, stride=pitch), :] for i in range(2)], 0).astype(bf16)

    def attend(b, p, e):
        v = stack_heads(pick(2 * hp + p, b), low, zero)
        o = dot(e, jnp.concatenate([v, ones], 1))
        o = o[:, :LANES] / o[:, LANES:]
        for i in range(2):
            att[p, pl.ds(2 * b + i, pad, stride=pitch), :] = o[i * pad : (i + 1) * pad]

    big = jnp.zeros((pair, 2 * pair), f32)
    for b in range(seqs // 2):
        for p in range(hp):
            s = dot_nt(pick(p, b), stack_heads(pick(hp + p, b), low, zero))
            big = jnp.maximum(big, jnp.abs(s))
            sc[b * hp + p] = s
    for i in range(seqs // 2 * hp):
        ec[i] = jnp.exp(sc[i] + bias).astype(bf16)
    for b in range(seqs // 2):
        for p in range(hp):
            attend(b, p, ec[b * hp + p])

    @pl.when(jnp.logical_not(jnp.max(big) < SAFE))
    def _():
        for b in range(seqs // 2):

            @pl.loop(0, hp)
            def _(p):
                s = sc[b * hp + p] + bias
                top0 = jnp.max(jnp.where(first_head, s, -2e30), -1, keepdims=True)
                top1 = jnp.max(jnp.where(first_head, -2e30, s), -1, keepdims=True)
                attend(b, p, jnp.exp(s - jnp.where(first_head, top0, top1)).astype(bf16))

    attended = jnp.concatenate(
        [jnp.concatenate([att[p, t * pitch : t * pitch + seqs] for p in range(hp)], 1) for t in range(tokens)], 0
    ).astype(bf16)
    mid = x_ref[...].astype(f32).reshape(rows, d) + dot(attended, wo_ref[...])
    at = pl.ds(pl.multiple_of(step * seqs, seqs), seqs)
    ms[at, :] = jnp.sum(mid.reshape(tokens, seqs, d), 0)
    n2 = (norm_parts(mid)[0] * gains_ref[1:2, :] + shifts_ref[1:2, :]).astype(bf16)
    chunk = 512
    for c in range(0, ff, chunk):
        v = dot(n2, wup_ref[:, c : c + chunk])
        t = jnp.tanh(v * (GELU_C + (GELU_C * GELU_A) * (v * v)))
        h = (0.5 * v) * (1.0 + t)
        hs[at, c : c + chunk] = jnp.sum(h.reshape(tokens, seqs, chunk), 0)

    @pl.when(step == pl.num_programs(0) - 1)
    def _():
        hi, lo = split_bf16(hs[...] * (1.0 / tokens))
        u = ms[...] * (1.0 / tokens) + dot(hi, wdown_ref[...]) + dot(lo, wdown_ref[...])
        n = u.shape[0]
        out_ref[:n] = (u * lax.rsqrt(jnp.sum(u * u, -1, keepdims=True) + 1e-6)).astype(bf16)
        if out_ref.shape[0] > n:
            out_ref[n:] = count_rows(valid_ref, d)


def image_embed(xt, valid, gains, shifts, wqkv, wo, wup, wdown, start, count, note, seqs=16):
    tokens, _, d = xt.shape
    ff = wup.shape[1]
    pad = -(-tokens // 8) * 8
    pitch = seqs + PITCH
    tiles = seqs // 2 * (d // LANES)
    first = start // seqs
    rows = count + (NOTE if note else 0)
    return pl.pallas_call(
        functools.partial(image_kernel, seqs),
        grid=(count // seqs,),
        in_specs=[pl.BlockSpec((tokens, seqs, d), lambda i: (0, i + first, 0))]
        + [whole(a) for a in (valid, gains, shifts, wqkv, wo, wup, wdown)],
        out_specs=pl.BlockSpec((rows, d), lambda i: (0, 0)),
        out_shape=jax.ShapeDtypeStruct((rows, d), bf16),
        scratch_shapes=[
            pltpu.VMEM((3 * d // LANES, pitch * pad, LANES), f32),
            pltpu.VMEM((d // LANES, pitch * pad, LANES), f32),
            pltpu.VMEM((tiles, 2 * pad, 4 * pad), f32),
            pltpu.VMEM((tiles, 2 * pad, 4 * pad), bf16),
            pltpu.VMEM((count, ff), f32),
            pltpu.VMEM((count, d), f32),
        ],
        compiler_params=params(),
        cost_estimate=cost(0.45 * count),
        name="image_block",
    )(xt, valid, gains, shifts, wqkv, wo, wup, wdown)


def real_tokens(length, txt):
    seqs = length.shape[0]
    spread = jnp.broadcast_to(length[:, None, :], (seqs, txt, 1)).reshape(seqs * txt, 1)
    pos = lax.broadcasted_iota(jnp.int32, (seqs * txt, 1), 0) % txt
    return jnp.where(pos.astype(f32) < spread, 1.0, 0.0)


def text_forward_kernel(
    txt, held, x_ref, key_ref, flen_ref, gains_ref, shifts_ref, wqkv_ref, wo_ref, wup_ref, wdown_ref, *refs,
):
    (n1_ref, qkv_ref, probs_ref, att_ref, n2_ref, slope_ref, stat_ref, hpool_ref, u_ref, emb_ref, ms, sc, ec) = refs[held:]
    step = pl.program_id(0)
    rows, d = x_ref.shape
    ff = wup_ref.shape[1]
    seqs = rows // txt
    x = x_ref[...].astype(f32)
    xhat1, rstd1 = norm_parts(x)
    n1 = (xhat1 * gains_ref[0:1, :] + shifts_ref[0:1, :]).astype(bf16)
    n1_ref[...] = n1
    qkv_ref[:, :d] = (dot(n1, wqkv_ref[:, :d]) * HEAD**-0.5).astype(bf16)
    qkv_ref[:, d:] = dot(n1, wqkv_ref[:, d:]).astype(bf16)
    low = lax.broadcasted_iota(jnp.int32, (LANES, LANES), 1) < HEAD
    same = (
        lax.broadcasted_iota(jnp.int32, (LANES, LANES), 0) // txt
        == lax.broadcasted_iota(jnp.int32, (LANES, LANES), 1) // txt
    )
    zero = jnp.zeros((LANES, LANES), bf16)
    hp = d // LANES
    tiles = [(g, p) for g in range(rows // LANES) for p in range(hp)]

    def attend(g, p, probs):
        r = slice(g * LANES, (g + 1) * LANES)
        probs_ref[g * hp + p] = probs
        v = qkv_ref[r, 2 * d + p * LANES : 2 * d + (p + 1) * LANES]
        att_ref[r, p * LANES : (p + 1) * LANES] = dot(probs, stack_heads(v, low, zero)).astype(bf16)

    def share(s, top):
        halves = []
        for h in range(2):
            sh = s[:, h * LANES : (h + 1) * LANES]
            e = jnp.exp(sh - jnp.max(sh, -1, keepdims=True)) if top else jnp.exp(sh)
            halves.append(e / jnp.sum(e, -1, keepdims=True))
        return jnp.concatenate(halves, 1).astype(bf16)

    big = jnp.zeros((LANES, 2 * LANES), f32)
    for g, p in tiles:
        r = slice(g * LANES, (g + 1) * LANES)
        bias = jnp.where(same & (key_ref[0, g : g + 1, :] > 0), 0.0, -1e30)
        q = qkv_ref[r, p * LANES : (p + 1) * LANES]
        k = qkv_ref[r, d + p * LANES : d + (p + 1) * LANES]
        s = dot_nt(q, stack_heads(k, low, zero))
        big = jnp.maximum(big, jnp.abs(s))
        sc[g * hp + p] = s + jnp.concatenate([bias, bias], 1)
    for g, p in tiles:
        ec[g * hp + p] = share(sc[g * hp + p], False)
    for g, p in tiles:
        attend(g, p, ec[g * hp + p])

    @pl.when(jnp.logical_not(jnp.max(big) < SAFE))
    def _():
        for g, p in tiles:
            attend(g, p, share(sc[g * hp + p], True))

    mid = x + dot(att_ref[...], wo_ref[...])
    xhat2, rstd2 = norm_parts(mid)
    lane = lax.broadcasted_iota(jnp.int32, (rows, LANES), 1)
    hi1, hi2 = rstd1.astype(bf16).astype(f32), rstd2.astype(bf16).astype(f32)
    stat = jnp.where(lane < 64, jnp.where(lane < 32, hi1, rstd1 - hi1), jnp.where(lane < 96, hi2, rstd2 - hi2))
    stat_ref[...] = stat.astype(bf16)
    at = pl.ds(pl.multiple_of(step * seqs, seqs), seqs)
    keep = real_tokens(flen_ref[at, :], txt)
    n2 = ((xhat2 * gains_ref[1:2, :] + shifts_ref[1:2, :]) * keep).astype(bf16)
    n2_ref[...] = n2
    ms[at, :] = jnp.sum((mid * keep).reshape(seqs, txt, d), 1)
    chunk = 512
    for c in range(0, ff, chunk):
        v = dot(n2, wup_ref[:, c : c + chunk])
        v2 = v * v
        t = jnp.tanh(v * (GELU_C + (GELU_C * GELU_A) * v2))
        half = 0.5 + 0.5 * t
        h = v * half
        slope = half + h * (1.0 - t) * (GELU_C + (3.0 * GELU_C * GELU_A) * v2)
        slope_ref[:, c : c + chunk] = (slope * keep).astype(bf16)
        hpool_ref[at, c : c + chunk] = jnp.sum(h.reshape(seqs, txt, chunk), 1)

    @pl.when(step == pl.num_programs(0) - 1)
    def _():
        hi, lo = split_bf16(hpool_ref[...])
        pooled = ms[...] + dot(hi, wdown_ref[...]) + dot(lo, wdown_ref[...])
        u = pooled / flen_ref[...]
        u_ref[...] = u
        emb_ref[...] = (u * lax.rsqrt(jnp.sum(u * u, -1, keepdims=True) + 1e-6)).astype(bf16)


def text_forward(piece, pieces, held, x, key_ok, flen, gains, shifts, wqkv, wo, wup, wdown, txt, rows=512):
    total, d = x.shape
    ff = wup.shape[1]
    pairs = total // txt
    hp = d // LANES
    part = pairs // pieces
    steps = total // pieces // rows
    first = piece * steps
    block = lambda *tail: pl.BlockSpec((rows,) + tail, lambda i: (i + first,) + (0,) * len(tail))
    still = lambda *shape: pl.BlockSpec(shape, lambda i: (piece, 0))
    shape = jax.ShapeDtypeStruct
    key3 = key_ok.reshape(total // rows, rows // LANES, LANES)
    args = (x, key3, flen, gains, shifts, wqkv, wo, wup, wdown)
    return pl.pallas_call(
        functools.partial(text_forward_kernel, txt, len(held)),
        grid=(steps,),
        in_specs=[
            block(d), pl.BlockSpec((1, rows // LANES, LANES), lambda i: (i + first, 0, 0)), still(part, 1)
        ]
        + [whole(a) for a in args[3:]]
        + [pl.BlockSpec(memory_space=pl.ANY)] * len(held),
        out_specs=[
            block(d), block(3 * d), pl.BlockSpec((rows // LANES * hp, LANES, 2 * LANES), lambda i: (i + first, 0, 0)),
            block(d), block(d), block(ff), block(LANES), still(part, ff), still(part, d), still(part, d),
        ],
        out_shape=[
            shape((total, d), bf16), shape((total, 3 * d), bf16), shape((total // LANES * hp, LANES, 2 * LANES), bf16),
            shape((total, d), bf16), shape((total, d), bf16), shape((total, ff), bf16), shape((total, LANES), bf16),
            shape((pairs, ff), f32), shape((pairs, d), f32), shape((pairs, d), bf16),
        ],
        input_output_aliases={len(args) + i: i for i in range(len(held))},
        scratch_shapes=[
            pltpu.VMEM((part, d), f32),
            pltpu.VMEM((rows // LANES * hp, LANES, 2 * LANES), f32),
            pltpu.VMEM((rows // LANES * hp, LANES, 2 * LANES), bf16),
        ],
        compiler_params=params(),
        cost_estimate=cost(0.013 * total / pieces),
        name="text_forward",
    )(*args, *held)


def scores_kernel(
    group, place_ref, own_ref, other_ref, mask_ref, scale_ref, a0_ref, a1_ref,
    s_ref, all_ref, col_out, okay_out, row_out,
):
    step = pl.program_id(0)
    pairs = own_ref.shape[0]
    scale = scale_ref[0]
    mask = mask_ref[...]
    inner = lax.rem(place_ref[0], group)
    late = lax.bitwise_xor(step, lax.div(place_ref[0], group)) >= pl.num_programs(0) // 2
    texts = jnp.concatenate([own_ref[...], other_ref[...]], 0)

    @pl.when(step == 0)
    def _():
        row_out[...] = jnp.zeros_like(row_out)
        row_out[:, 3:4] = mask

    lane = lax.broadcasted_iota(jnp.int32, (1, pairs), 1).astype(f32)
    for k in range(group):
        at = lax.bitwise_xor(k, inner)
        cols = slice(k * pairs, (k + 1) * pairs)
        a = jnp.where(late, a1_ref[at], a0_ref[at])
        images = a[:pairs]
        count = a[pairs : pairs + 1, 0:1].astype(f32)
        okay = jnp.where(lane < count, 1.0, 0.0)
        okay_out[0:1, cols] = okay
        all_ref[cols, :] = images
        s = scale * dot_nt(texts, images)
        s_ref[:, cols] = s
        up = jnp.exp(s - SHIFT)
        down = jnp.exp(jnp.minimum(s, 0.0) + SHIFT)
        col_out[0:1, cols] = jnp.sum(up * mask, 0, keepdims=True)
        col_out[1:2, cols] = jnp.sum(down * mask, 0, keepdims=True)
        row_out[:, 0:1] += jnp.sum(up * okay, 1, keepdims=True)
        row_out[:, 1:2] += jnp.sum(down * okay, 1, keepdims=True)
        row_out[:, 2:3] += jnp.broadcast_to(count, (2 * pairs, 1))


def pair_scores(place, own, other, mask, scale, a0, a1):
    slots, _, d = a0.shape
    pairs = own.shape[0]
    group = min(8, slots)
    groups = slots // group
    cols = group * pairs
    keep = lambda *_: (0, 0)
    turn = lambda i, s: (lax.rem(lax.bitwise_xor(i, lax.div(s[0], group)), groups), 0, 0)
    still = lambda a: pl.BlockSpec(a.shape, keep)
    shape = jax.ShapeDtypeStruct
    return pl.pallas_call(
        functools.partial(scores_kernel, group),
        grid_spec=pltpu.PrefetchScalarGridSpec(
            num_scalar_prefetch=1,
            grid=(2 * groups,),
            in_specs=[still(own), still(other), still(mask), pl.BlockSpec(memory_space=pltpu.SMEM)]
            + [pl.BlockSpec((group,) + a.shape[1:], turn) for a in (a0, a1)],
            out_specs=[
                pl.BlockSpec((2 * pairs, cols), lambda i, s: (0, i)),
                pl.BlockSpec((cols, d), lambda i, s: (i, 0)),
                pl.BlockSpec((2, cols), lambda i, s: (0, i)),
                pl.BlockSpec((1, cols), lambda i, s: (0, i)),
                pl.BlockSpec((2 * pairs, 4), keep),
            ],
        ),
        out_shape=[
            shape((2 * pairs, 2 * groups * cols), f32), shape((2 * groups * cols, d), bf16),
            shape((2, 2 * groups * cols), f32), shape((1, 2 * groups * cols), f32), shape((2 * pairs, 4), f32),
        ],
        compiler_params=params(),
        cost_estimate=cost(4.0),
        name="pair_scores",
    )(place, own, other, mask, scale, a0, a1)


def log_sum(up, down):
    fine = up >= 1.9287498479639178e-22
    return jnp.where(
        fine, jnp.log(jnp.where(fine, up, 1.0)) + SHIFT, jnp.log(jnp.where(fine, 1.0, down)) - SHIFT
    )


def gradient_kernel(
    dp, scale_ref, s_ref, all_ref, col_ref, got_ref, okay_ref, row_ref, swap_ref, text_ref, a_ref,
    grad_ref, back_ref, loss_ref,
):
    step = pl.program_id(0)
    pairs = text_ref.shape[0]
    row = row_ref[...] + jnp.concatenate([swap_ref[pairs:], swap_ref[:pairs]], 0)
    factor = 0.5 / row[0:1, 2:3]
    mask = row_ref[:, 3:4]
    okay = okay_ref[...]
    row_lse = log_sum(row[:, 0:1], row[:, 1:2])
    col = col_ref[...] + got_ref[...]
    col_lse = log_sum(col[0:1, :], col[1:2, :])

    @pl.when(step == 0)
    def _():
        grad_ref[...] = jnp.zeros_like(grad_ref)
        back_ref[...] = jnp.zeros_like(back_ref)
        loss_ref[...] = jnp.zeros_like(loss_ref)
        t = text_ref[...].astype(f32) * a_ref[:pairs].astype(f32)
        diag = scale_ref[0] * jnp.sum(t, -1, keepdims=True)
        m = mask[:pairs]
        loss_ref[0:1, 0:1] = factor * jnp.sum(m * (row_lse[:pairs] - 2.0 * diag), 0, keepdims=True)
        loss_ref[1:2, 0:1] = -2.0 * factor * jnp.sum(m * diag, 0, keepdims=True)

    s = s_ref[...]
    g = jnp.exp(jnp.minimum(s - row_lse, 1.0)) + jnp.exp(jnp.minimum(s - col_lse, 1.0))
    g = g * ((factor * mask) * okay)
    grad = dot(g.astype(bf16), all_ref[...])
    grad_ref[...] += grad[:pairs]
    back_ref[...] += grad[pairs:]
    cols = jnp.sum(jnp.where(okay > 0, col_lse, 0.0), 1, keepdims=True)
    loss_ref[0:1, 0:1] += factor * (cols * (1.0 / dp))
    loss_ref[1:2, 0:1] += jnp.sum(jnp.sum(g * s, 0, keepdims=True), 1, keepdims=True)


def pair_gradients(dp, scale, scores, images, col, got, okay, row, swap, texts, a):
    pairs, d = texts.shape
    cols = min(8, dp) * pairs
    still = lambda *shape: pl.BlockSpec(shape, lambda i: (0, 0))
    shape = jax.ShapeDtypeStruct
    return pl.pallas_call(
        functools.partial(gradient_kernel, dp),
        grid=(dp * pairs // cols,),
        in_specs=[
            pl.BlockSpec(memory_space=pltpu.SMEM),
            pl.BlockSpec((2 * pairs, cols), lambda i: (0, i)),
            pl.BlockSpec((cols, d), lambda i: (i, 0)),
            pl.BlockSpec((2, cols), lambda i: (0, i)),
            pl.BlockSpec((2, cols), lambda i: (0, i)),
            pl.BlockSpec((1, cols), lambda i: (0, i)),
        ]
        + [whole(x) for x in (row, swap, texts, a)],
        out_specs=[still(pairs, d), still(pairs, d), still(8, LANES)],
        out_shape=[shape((pairs, d), f32), shape((pairs, d), f32), shape((8, LANES), f32)],
        compiler_params=params(),
        cost_estimate=cost(3.0),
        name="pair_gradients",
    )(scale, scores, images, col, got, okay, row, swap, texts, a)


def spread_rows(a, txt):
    seqs, width = a.shape
    return jnp.broadcast_to(a[:, None, :], (seqs, txt, width)).reshape(seqs * txt, width)


def backward_up_kernel(
    txt, scale_ref, rep_ref, part_ref, back_ref, row_ref, swap_ref, a_ref, u_ref, len_ref, hpool_ref, n2_ref, slope_ref,
    wdown_ref, send_ref, keep_ref, gd_ref, dh_ref, down, acc,
):
    step = pl.program_id(0)
    rows, d = n2_ref.shape
    ff = slope_ref.shape[1]
    seqs = rows // txt

    @pl.when(step == 0)
    def _():
        pairs = part_ref.shape[0]
        scale = scale_ref[0]
        factor = 0.5 / (row_ref[0:1, 2:3] + swap_ref[0:1, 2:3])
        images = a_ref[:pairs].astype(f32)
        u = u_ref[...]
        r = lax.rsqrt(jnp.sum(u * u, -1, keepdims=True) + 1e-6)
        g = scale * (part_ref[...] + back_ref[...]) - (2.0 * scale) * (factor * row_ref[:pairs, 3:4]) * images
        du = (r * g - (r * r * r) * u * jnp.sum(u * g, -1, keepdims=True)) / len_ref[...]
        gd_ref[...] = du
        low = du.astype(bf16)
        dh_ref[...] = dot_nt(low, wdown_ref[...])
        hi, lo = split_bf16(hpool_ref[...])
        down[...] = (dot_tn(hi, low) + dot_tn(lo, low)).astype(bf16)
        acc[...] = jnp.zeros_like(acc)

    at = pl.ds(pl.multiple_of(step * seqs, seqs), seqs)
    chunk = 512
    for c in range(0, ff, chunk):
        cs = slice(c, c + chunk)
        grad_before = (spread_rows(dh_ref[at, cs], txt) * slope_ref[:, cs].astype(f32)).astype(bf16)
        acc[:, cs] += dot_tn(n2_ref[...], grad_before)

    @pl.when(step == pl.num_programs(0) - 1)
    def _():
        first = rep_ref[0] == 0
        for b in range(ff // d):
            r = slice(b * d, (b + 1) * d)
            up = acc[:, r].astype(bf16)
            keep_ref[r] = jnp.where(first, down[r], up)
            send_ref[r] = jnp.where(first, up, down[r])


def backward_up(scale, rep, part, back, row, swap, a, u, flen, hpool, n2, slope, wdown, txt, rows=512):
    tokens, d = n2.shape
    pairs, ff = hpool.shape
    block = lambda w: pl.BlockSpec((rows, w), lambda i: (i, 0))
    shape = jax.ShapeDtypeStruct
    smem = pl.BlockSpec(memory_space=pltpu.SMEM)
    outs = [shape((ff, d), bf16), shape((ff, d), bf16), shape((pairs, d), f32), shape((pairs, ff), f32)]
    return pl.pallas_call(
        functools.partial(backward_up_kernel, txt),
        grid=(tokens // rows,),
        in_specs=[smem, smem]
        + [whole(x) for x in (part, back, row, swap, a, u, flen, hpool)]
        + [block(d), block(ff), whole(wdown)],
        out_specs=[whole(x) for x in outs],
        out_shape=outs,
        scratch_shapes=[pltpu.VMEM((ff, d), bf16), pltpu.VMEM((d, ff), f32)],
        compiler_params=params(),
        cost_estimate=cost(0.006 * tokens),
        name="backward_up",
    )(scale, rep, part, back, row, swap, a, u, flen, hpool, n2, slope, wdown)


def backward_middle_kernel(
    txt, gd_ref, dh_ref, len_ref, n2_ref, slope_ref, stat_ref, att_ref, gains_ref, shifts_ref, wup_ref, wo_ref,
    gmid_ref, datt_ref, dwo_ref, gain_ref, acc,
):
    step = pl.program_id(0)
    rows, d = n2_ref.shape
    ff = wup_ref.shape[1]

    @pl.when(step == 0)
    def _():
        acc[...] = jnp.zeros_like(acc)
        gain_ref[...] = jnp.zeros_like(gain_ref)

    dn2 = jnp.zeros((rows, d), f32)
    chunk = 512
    for c in range(0, ff, chunk):
        cs = slice(c, c + chunk)
        grad_before = (spread_rows(dh_ref[:, cs], txt) * slope_ref[:, cs].astype(f32)).astype(bf16)
        dn2 += dot_nt(grad_before, wup_ref[:, cs])
    xhat = (n2_ref[...].astype(f32) - shifts_ref[1:2, :]) / gains_ref[1:2, :]
    stat = stat_ref[...].astype(f32)
    gain_ref[0:1, :] += jnp.sum(dn2 * xhat, 0, keepdims=True)
    gain_ref[1:2, :] += jnp.sum(dn2, 0, keepdims=True)
    gn = dn2 * gains_ref[1:2, :]
    dmid = (stat[:, 64:65] + stat[:, 96:97]) * (
        gn - jnp.mean(gn, -1, keepdims=True) - xhat * jnp.mean(gn * xhat, -1, keepdims=True)
    )
    gmid = spread_rows(gd_ref[...], txt) * real_tokens(len_ref[...], txt) + dmid
    gmid_ref[...] = gmid
    branch = gmid.astype(bf16)
    acc[...] += dot_tn(att_ref[...], branch)
    datt_ref[...] = dot_nt(branch, wo_ref[...]).astype(bf16)

    @pl.when(step == pl.num_programs(0) - 1)
    def _():
        dwo_ref[...] = acc[...].astype(bf16)


def backward_middle(gd, dh, flen, n2, slope, stat, att, gains, shifts, wup, wo, txt, rows=512):
    tokens, d = n2.shape
    ff = wup.shape[1]
    block = lambda w: pl.BlockSpec((rows, w), lambda i: (i, 0))
    lead = lambda w: pl.BlockSpec((rows // txt, w), lambda i: (i, 0))
    shape = jax.ShapeDtypeStruct
    sums = [shape((d, d), bf16), shape((8, d), f32)]
    return pl.pallas_call(
        functools.partial(backward_middle_kernel, txt),
        grid=(tokens // rows,),
        in_specs=[lead(d), lead(ff), lead(1), block(d), block(ff), block(LANES), block(d)]
        + [whole(x) for x in (gains, shifts, wup, wo)],
        out_specs=[block(d), block(d)] + [whole(x) for x in sums],
        out_shape=[shape((tokens, d), f32), shape((tokens, d), bf16)] + sums,
        scratch_shapes=[pltpu.VMEM((d, d), f32)],
        compiler_params=params(),
        cost_estimate=cost(0.006 * tokens),
        name="backward_middle",
    )(gd, dh, flen, n2, slope, stat, att, gains, shifts, wup, wo)


def backward_attention_kernel(
    held, last, rep_ref, datt_ref, qkv_ref, probs_ref, n1_ref, dwo_ref, gain2_ref, sums_ref, gains_ref, shifts_ref, wqkv_ref,
    *refs
):
    old_acc, old_flat = refs[1:3] if held else (None, None)
    gq_ref, *outs = refs[held:-4]
    acc, flat, sc, ec = refs[-4:]
    step = pl.program_id(0)
    rows, d = n1_ref.shape
    low = lax.broadcasted_iota(jnp.int32, (LANES, LANES), 1) < HEAD
    zero = jnp.zeros((LANES, LANES), bf16)

    @pl.when(step == 0)
    def _():
        acc[...] = old_acc[...] if held else jnp.zeros_like(acc)
        flat[...] = old_flat[...] if held else jnp.zeros_like(flat)

    hp = d // LANES
    tiles = [(g, p) for g in range(rows // LANES) for p in range(hp)]
    at = lambda g, p, part: (slice(g * LANES, (g + 1) * LANES), slice(part * d + p * LANES, part * d + (p + 1) * LANES))
    for g, p in tiles:
        sc[g * hp + p] = dot_nt(datt_ref[at(g, p, 0)], stack_heads(qkv_ref[at(g, p, 2)], low, zero))
    for g, p in tiles:
        i = g * hp + p
        probs = probs_ref[i].astype(f32)
        halves = []
        for h in range(2):
            hs = slice(h * LANES, (h + 1) * LANES)
            ph, dh = probs[:, hs], sc[i, :, hs]
            halves.append(ph * (dh - jnp.sum(ph * dh, -1, keepdims=True)))
        ec[i] = jnp.concatenate(halves, 1).astype(bf16)
    for g, p in tiles:
        dv = dot_tn(probs_ref[g * hp + p], datt_ref[at(g, p, 0)])
        gq_ref[at(g, p, 2)] = jnp.where(low, dv[:LANES], dv[LANES:]).astype(bf16)
    for g, p in tiles:
        keys = stack_heads(qkv_ref[at(g, p, 1)], low, zero)
        gq_ref[at(g, p, 0)] = (dot(ec[g * hp + p], keys) * HEAD**-0.5).astype(bf16)
    for g, p in tiles:
        dk = dot_tn(ec[g * hp + p], qkv_ref[at(g, p, 0)])
        gq_ref[at(g, p, 1)] = jnp.where(low, dk[:LANES], dk[LANES:]).astype(bf16)
    gq = gq_ref[...]
    acc[...] += dot_tn(n1_ref[...], gq)
    flat[0:1, :] += jnp.sum(gq.astype(f32), 0, keepdims=True)

    @pl.when(step == pl.num_programs(0) - 1)
    def _():
        if not last:
            outs[0][...] = acc[...]
            outs[1][...] = flat[...]
            return
        send_ref, keep_ref, small_ref = outs
        w = wqkv_ref[...]
        ones = jnp.ones((8, 3 * d), bf16)
        hi, lo = split_bf16(acc[...] * w.astype(f32))
        spread = dot_nt(ones, hi) + dot_nt(ones, lo)
        hi, lo = split_bf16(flat[...])
        dshift = (dot_nt(hi, w) + dot_nt(lo, w))[0:1]
        dgain = (spread[0:1] - shifts_ref[0:1, :] * dshift) / gains_ref[0:1, :]
        small = [dgain, gain2_ref[0:1, :], dshift, gain2_ref[1:2, :]]
        small += [jnp.broadcast_to(sums_ref[i : i + 1, 0:1], (1, d)) for i in range(2)]
        small = jnp.concatenate(small + [jnp.zeros((2, d), f32)], 0)
        small_ref[...] = small
        first = rep_ref[0] == 0
        parts = [acc[:, b * d : (b + 1) * d].astype(bf16) for b in range(3)] + [dwo_ref[...]]
        for b in range(2):
            keep_ref[b * d : (b + 1) * d] = jnp.where(first, parts[b], parts[b + 2])
            send_ref[b * d : (b + 1) * d] = jnp.where(first, parts[b + 2], parts[b])
        put_small(send_ref, 2 * d, small)


def backward_attention(piece, pieces, held, rep, datt, qkv, probs, n1, dwo, gain2, sums, gains, shifts, wqkv, rows=512):
    tokens, d = n1.shape
    steps = tokens // pieces // rows
    first = piece * steps
    last = piece == pieces - 1
    block = lambda w: pl.BlockSpec((rows, w), lambda i: (i + first, 0))
    shape = jax.ShapeDtypeStruct
    if last:
        outs = [shape((2 * d + NOTE, d), bf16), shape((2 * d, d), bf16), shape((8, d), f32)]
    else:
        outs = [shape((d, 3 * d), f32), shape((8, 3 * d), f32)]
    args = (rep, datt, qkv, probs, n1, dwo, gain2, sums, gains, shifts, wqkv)
    return pl.pallas_call(
        functools.partial(backward_attention_kernel, len(held), last),
        grid=(steps,),
        in_specs=[
            pl.BlockSpec(memory_space=pltpu.SMEM), block(d), block(3 * d),
            pl.BlockSpec((rows // LANES * (d // LANES), LANES, 2 * LANES), lambda i: (i + first, 0, 0)),
            block(d),
        ]
        + [whole(x) for x in args[5:]]
        + ([pl.BlockSpec(memory_space=pl.ANY)] + [whole(x) for x in held[1:]] if held else []),
        out_specs=[block(3 * d)] + [whole(x) for x in outs],
        out_shape=[shape((tokens, 3 * d), bf16)] + outs,
        input_output_aliases={len(args): 0} if held else {},
        scratch_shapes=[
            pltpu.VMEM((d, 3 * d), f32),
            pltpu.VMEM((8, 3 * d), f32),
            pltpu.VMEM((rows // LANES * (d // LANES), LANES, 2 * LANES), f32),
            pltpu.VMEM((rows // LANES * (d // LANES), LANES, 2 * LANES), bf16),
        ],
        compiler_params=params(),
        cost_estimate=cost(0.009 * tokens / pieces),
        name="backward_attention",
    )(*args, *held)


def backward_input_kernel(gq_ref, gmid_ref, n1_ref, stat_ref, gains_ref, shifts_ref, wqkv_ref, *refs):
    dx_ref = refs[-1]
    gn = dot_nt(gq_ref[...], wqkv_ref[...]) * gains_ref[0:1, :]
    xhat = (n1_ref[...].astype(f32) - shifts_ref[0:1, :]) / gains_ref[0:1, :]
    stat = stat_ref[...].astype(f32)
    dx_ref[...] = gmid_ref[...] + (stat[:, 0:1] + stat[:, 32:33]) * (
        gn - jnp.mean(gn, -1, keepdims=True) - xhat * jnp.mean(gn * xhat, -1, keepdims=True)
    )


def backward_input(piece, pieces, held, gq, gmid, n1, stat, gains, shifts, wqkv, rows=512):
    tokens, d = gmid.shape
    steps = tokens // pieces // rows
    block = lambda w: pl.BlockSpec((rows, w), lambda i: (i + piece * steps, 0))
    args = (gq, gmid, n1, stat, gains, shifts, wqkv)
    return pl.pallas_call(
        backward_input_kernel,
        grid=(steps,),
        in_specs=[block(3 * d), block(d), block(d), block(LANES), whole(gains), whole(shifts), whole(wqkv)]
        + [pl.BlockSpec(memory_space=pl.ANY)] * len(held),
        out_specs=block(d),
        out_shape=jax.ShapeDtypeStruct((tokens, d), f32),
        input_output_aliases={len(args): 0} if held else {},
        compiler_params=params(2 * HOP_VMEM),
        cost_estimate=cost(0.004 * tokens / pieces),
        name="backward_input",
    )(*args, *held)


def finish_kernel(places, rep_ref, own_ref, got_ref, *out_refs):
    first = rep_ref[0] == 0
    for out, top, left, begin, n, part in places:
        a = own_ref[begin : begin + n, :]
        b = got_ref[begin : begin + n, :]
        mine = first if part == 0 else jnp.logical_not(first)
        out_refs[out][top : top + n, left : left + a.shape[1]] = jnp.where(mine, a, b).astype(f32)


def finish(rep, own, got, shapes, segments):
    half = own.shape[0]
    places = []
    for row, count, out, top, left in segments:
        while count:
            part, begin = divmod(row, half)
            n = min(count, half - begin)
            places.append((out, top, left, begin, n, part))
            row, top, count = row + n, top + n, count - n
    outs = [jax.ShapeDtypeStruct(s, f32) for s in shapes]
    return pl.pallas_call(
        functools.partial(finish_kernel, places),
        grid=(1,),
        in_specs=[pl.BlockSpec(memory_space=pltpu.SMEM), whole(own), whole(got)],
        out_specs=[whole(x) for x in outs],
        out_shape=outs,
        compiler_params=params(2 * HOP_VMEM),
        cost_estimate=cost(3.0),
        name="finish",
    )(rep, own, got)


class Links:
    def __init__(self, mesh):
        self.dp, self.rep = mesh.shape["dp"], mesh.shape["rep"]
        self.bits = (self.dp - 1).bit_length()
        assert self.dp == 1 << self.bits and self.rep == 2
        near, far = list(range(min(2, self.bits))), list(range(2, self.bits))
        turn = lambda bits: list(zip(bits, bits[::-1]))
        self.near, self.far = turn(near), turn(far)
        self.gather_order = [(b, b) for b in far[::-1]] + self.near

    def bit(self, pair):
        place = lax.axis_index("dp")
        return jnp.where(lax.axis_index("rep") == 0, (place >> pair[0]) & 1, (place >> pair[1]) & 1)

    def across(self, x, pair):
        moves = [(2 * i + r, 2 * (i ^ (1 << pair[r])) + r) for i in range(self.dp) for r in range(2)]
        return lax.ppermute(x, ("dp", "rep"), moves)

    def core(self, x):
        return lax.ppermute(x, "rep", [(0, 1), (1, 0)])


def put_small(ref, at, small):
    hi, lo = split_bf16(small)
    ref[at : at + NOTE] = jnp.concatenate([hi, lo], 0)


def hop_kernel(kind, late, with_small, v_ref, x_ref, got_ref, *refs):
    n, d = x_ref.shape
    refs = list(refs)
    small_ref = refs.pop(0) if with_small else None
    low = v_ref[0] == 0
    if kind == "join":
        x, got = x_ref[...], got_ref[...]
        refs[0][:n] = jnp.where(low, x, got)
        refs[0][n:] = jnp.where(low, got, x)
        return
    add = lambda r: (x_ref[r].astype(f32) + got_ref[r].astype(f32)).astype(bf16)
    send_ref, keep_ref = refs[0], refs[1]
    if late == "half":
        m = n // 2
        a, b = add(slice(0, m)), add(slice(m, n))
        keep_ref[...] = jnp.where(low, a, b)
        send_ref[:m] = jnp.where(low, b, a)
    else:
        m = n
        x = add(slice(0, n))
        keep_ref[...] = x
        if late == "full":
            send_ref[:m] = x
    if with_small:
        hi, lo = got_ref[n : n + NOTE // 2], got_ref[n + NOTE // 2 :]
        small = small_ref[...] + (hi.astype(f32) + lo.astype(f32))
        refs[2][...] = small
        if send_ref.shape[0] > m:
            put_small(send_ref, m, small)


class Reduction:
    def __init__(self, links, send, keep, small=None):
        self.kind = None
        self.links, self.send, self.x, self.small = links, send, keep, small
        self.plan = (
            [("core", None)]
            + [("half", p) for p in links.near]
            + [("full", p) for p in links.far]
            + [("join", p) for p in links.near[::-1]]
            + [("last", None)]
        )

    def start(self, *after):
        links = self.links
        self.kind, self.pair = self.plan.pop(0)
        if after:
            self.send, *after = beside(self.send, *after)
        self.got = links.core(self.send) if self.pair is None else links.across(self.send, self.pair)
        return after

    def end(self):
        kind, x, links = self.kind, self.x, self.links
        if kind == "last":
            return
        n, d = x.shape
        shape = jax.ShapeDtypeStruct
        late, pair = self.plan[0]
        if kind == "join":
            v, outs = links.bit(self.pair), [shape((2 * n, d), bf16)]
        else:
            v = links.bit(pair) if late == "half" else jnp.zeros((), jnp.int32)
            m = n // 2 if late == "half" else n
            more = NOTE if self.small is not None and late in ("half", "full") else 0
            outs = [shape((m + more if late in ("half", "full") else NOTE, d), bf16), shape((m, d), bf16)]
        args = [v.astype(jnp.int32).reshape(1), x, self.got]
        with_small = self.small is not None and kind != "join"
        if with_small:
            args.append(self.small)
            outs.append(shape(self.small.shape, f32))
        out = pl.pallas_call(
            functools.partial(hop_kernel, kind, late, with_small),
            in_specs=[pl.BlockSpec(memory_space=pltpu.SMEM)] + [pl.BlockSpec(memory_space=pltpu.VMEM)] * (len(args) - 1),
            out_specs=[pl.BlockSpec(memory_space=pltpu.VMEM)] * len(outs),
            out_shape=outs,
            compiler_params=params(HOP_VMEM),
            cost_estimate=cost(1.0),
            name="hop",
        )(*args)
        if kind == "join":
            self.send = self.x = out[0]
            return
        self.x = out[1]
        self.send = out[0] if late in ("half", "full") else self.x
        if with_small:
            self.small = out[2]


def beside(*values):
    return lax.optimization_barrier(values)


def body(
    links, image_in, img_gains, img_shifts, img_qkv, img_out, img_up, img_down, text_in, lengths, valid,
    txt_gains, txt_shifts, txt_qkv, txt_out, txt_up, txt_down, log_scale,
):
    dp, bits = links.dp, links.bits
    pairs, txt, d = text_in.shape
    ff = txt_up.shape[1]
    tokens = pairs * txt
    scale = jnp.exp(log_scale).reshape(1)
    rep = lax.axis_index("rep").astype(jnp.int32).reshape(1)
    order = links.gather_order

    own_mask = valid.astype(f32)
    row_mask = jnp.concatenate([own_mask, links.core(own_mask)])[:, None]
    flen = lengths.astype(f32)[:, None]
    key_ok = (jnp.arange(txt)[None, :] < lengths[:, None]).astype(f32).reshape(tokens // LANES, LANES)

    image_args = (valid[None, :], img_gains, img_shifts, img_qkv, img_out, img_up, img_down)
    emb = image_embed(image_in.transpose(1, 0, 2), *image_args, 0, pairs, True)
    text_args = (txt_gains, txt_shifts, txt_qkv, txt_out, txt_up, txt_down)
    text_x, emb = beside(text_in.reshape(tokens, d), emb)
    steps, pieces = list(order), 4
    a, held = emb[None], []
    for piece in range(pieces):
        if steps:
            got = links.across(a, steps.pop(0))
        held = list(text_forward(piece, pieces, held, text_x, key_ok, flen, *text_args, txt))
        if steps:
            text_x, got, held[-1] = beside(text_x, got, held[-1])
            a = jnp.concatenate([a, got], 0)
    while steps:
        got = links.across(a, steps.pop(0))
        if steps:
            a = jnp.concatenate([a, got], 0)
    n1, qkv, probs, att, n2, slope, stat, hpool, u, text_emb = held

    place = sum(links.bit(order[i]) << i for i in range(bits)).astype(jnp.int32).reshape(1)
    scores, images, col, okay, row = pair_scores(
        place, text_emb, links.core(text_emb), row_mask, scale, a, got
    )
    swap = links.core(row)
    for pair in order[:-1]:
        col = col + links.across(col, pair)
    col_got = links.across(col, order[-1])
    part, other, sums = pair_gradients(dp, scale, scores, images, col, col_got, okay, row, swap, text_emb, emb)
    back = links.core(other)

    ffn_send, ffn_keep, gd, dh = backward_up(scale, rep, part, back, row, swap, emb, u, flen, hpool, n2, slope, txt_down, txt)
    first = Reduction(links, ffn_send, ffn_keep)
    first.start()
    gmid, datt, dwo, gain2 = backward_middle(
        gd, dh, flen, n2, slope, stat, att, txt_gains, txt_shifts, txt_up, txt_out, txt
    )
    held = []
    for piece in range(2):
        datt, first.got, *held = beside(datt, first.got, *held)
        first.end()
        first.start()
        held = list(backward_attention(
            piece, 2, held, rep, datt, qkv, probs, n1, dwo, gain2, sums, txt_gains, txt_shifts, txt_qkv
        ))
    gq, att_send, att_keep, small = held
    second = Reduction(links, att_send, att_keep, small)
    dx, done = [], []

    def inputs(piece, stream):
        gq_now, stream.x = beside(gq, stream.x)
        dx[:] = [backward_input(piece, 2, dx, gq_now, gmid, n1, stat, txt_gains, txt_shifts, txt_qkv)]

    other = {first: second, second: first}
    far = len(links.far)
    for act, stream in (
        [("s", second), ("e", first), ("s", first), ("e", second), ("s", second), ("i", 0), ("e", second), ("s", second)]
        + [("e", first), ("s", first), ("e", second), ("s", second), ("i", 1), ("e", second), ("s", second)]
        + [("e", first), ("s", first), ("e", second), ("s", second), ("e", first), ("s", first)] * (far > 0)
    ):
        if act == "i":
            inputs(stream, second)
        elif act == "e":
            stream.end()
        elif stream.plan:
            if stream is second and second.kind is None:
                stream.start()
            else:
                other[stream].x, *dx[:] = stream.start(other[stream].x, *dx)
    while first.plan or second.plan:
        for stream in (second, first):
            if stream.plan:
                stream.end()
                stream.start()
    grad_down, grad_up = finish(
        rep, first.x, first.got, [(ff, d), (d, ff)], [(0, ff, 0, 0, 0)] + [(ff + i * d, d, 1, 0, i * d) for i in range(ff // d)]
    )
    grad_qkv, grad_out = finish(
        rep, second.x, second.got, [(d, 3 * d), (d, d)], [(i * d, d, 0, 0, i * d) for i in range(3)] + [(3 * d, d, 1, 0, 0)]
    )
    small, dx = second.small, dx[0]
    return (
        small[4, 0],
        small[0:2],
        small[2:4],
        grad_qkv,
        grad_out,
        grad_up,
        grad_down,
        small[5, 0],
        dx.reshape(pairs, txt, d),
    )


def solution(mesh):
    both = ("dp", "rep")
    deep = P(both, None, None)
    in_specs = (deep,) + (P(),) * 6 + (deep, P(both), P(both)) + (P(),) * 7
    out_specs = (P(),) * 8 + (deep,)
    return jax.shard_map(
        functools.partial(body, Links(mesh)), mesh=mesh, in_specs=in_specs, out_specs=out_specs, check_vma=False
    )
```

```python
import functools
import jax
import jax.numpy as jnp
from jax import lax
from jax.experimental import pallas as pl
from jax.experimental.pallas import tpu as pltpu
from jax.sharding import PartitionSpec as P

HEAD = 64
LANES = 128
f32 = jnp.float32
bf16 = jnp.bfloat16
GELU_C = 0.7978845608028654
GELU_A = 0.044715
SHIFT = 50.0
SAFE = 80.0
NOTE = 16
PITCH = 8
VMEM = 60 * 1024 * 1024
HOP_VMEM = 12 * 1024 * 1024


def dot(a, b):
    return jnp.dot(a, b, preferred_element_type=f32)


def dot_nt(a, b):
    return lax.dot_general(a, b, (((1,), (1,)), ((), ())), preferred_element_type=f32)


def dot_tn(a, b):
    return lax.dot_general(a, b, (((0,), (0,)), ((), ())), preferred_element_type=f32)


def norm_parts(x):
    mu = jnp.mean(x, -1, keepdims=True)
    c = x - mu
    rstd = lax.rsqrt(jnp.mean(c * c, -1, keepdims=True) + 1e-6)
    return c * rstd, rstd


def whole(a):
    return pl.BlockSpec(a.shape, lambda *_: (0,) * a.ndim)


def params(limit=VMEM):
    return pltpu.CompilerParams(vmem_limit_bytes=limit)


def cost(us):
    return pl.CostEstimate(flops=int(us * 1.1e9), bytes_accessed=0, transcendentals=0)


def split_bf16(v):
    hi = v.astype(bf16)
    return hi, (v - hi.astype(f32)).astype(bf16)


def count_rows(valid_ref, d):
    count = jnp.sum(valid_ref[...].astype(f32), 1, keepdims=True)
    return jnp.broadcast_to(count, (NOTE, d)).astype(bf16)


def stack_heads(a, low, zero):
    return jnp.concatenate([jnp.where(low, a, zero), jnp.where(low, zero, a)], 0)


def image_kernel(
    seqs, x_ref, valid_ref, gains_ref, shifts_ref, wqkv_ref, wo_ref, wup_ref, wdown_ref, out_ref,
    qkv, att, sc, ec, hs, ms,
):
    tokens, _, d = x_ref.shape
    pad = -(-tokens // 8) * 8
    pitch = seqs + PITCH
    rows, pair = seqs * tokens, 2 * pad
    step = pl.program_id(0)
    ff = wup_ref.shape[1]
    hp = d // LANES

    @pl.when(step == 0)
    def _():
        qkv[:, tokens * pitch :] = jnp.zeros((3 * hp, (pad - tokens) * pitch, LANES), f32)

    x = x_ref[...].astype(f32).reshape(rows, d)
    n1 = (norm_parts(x)[0] * gains_ref[0:1, :] + shifts_ref[0:1, :]).astype(bf16)
    for c in range(3):
        r = dot(n1, wqkv_ref[:, c * d : (c + 1) * d])
        r = r * HEAD**-0.5 if c == 0 else r
        for p in range(hp):
            for t in range(tokens):
                qkv[c * hp + p, t * pitch : t * pitch + seqs] = r[t * seqs : (t + 1) * seqs, p * LANES : (p + 1) * LANES]

    low = lax.broadcasted_iota(jnp.int32, (pair, LANES), 1) < HEAD
    key_lane = lax.broadcasted_iota(jnp.int32, (pair, 2 * pair), 1)
    query_row = lax.broadcasted_iota(jnp.int32, (pair, 2 * pair), 0)
    first_head = key_lane < pair
    key_row = jnp.where(first_head, key_lane, key_lane - pair)
    second_image = key_row >= pad
    key_pos = jnp.where(second_image, key_row - pad, key_row)
    bias = jnp.where((key_pos < tokens) & (second_image == (query_row >= pad)), 0.0, -1e30)
    zero, one = jnp.zeros((pair, LANES), bf16), jnp.ones((pair, LANES), bf16)
    ones = stack_heads(one, low, zero)

    def pick(j, b):
        return jnp.concatenate([qkv[j, pl.ds(2 * b + i, pad, stride=pitch), :] for i in range(2)], 0).astype(bf16)

    def attend(b, p, e):
        v = stack_heads(pick(2 * hp + p, b), low, zero)
        o = dot(e, jnp.concatenate([v, ones], 1))
        o = o[:, :LANES] / o[:, LANES:]
        for i in range(2):
            att[p, pl.ds(2 * b + i, pad, stride=pitch), :] = o[i * pad : (i + 1) * pad]

    big = jnp.zeros((pair, 2 * pair), f32)
    for b in range(seqs // 2):
        for p in range(hp):
            s = dot_nt(pick(p, b), stack_heads(pick(hp + p, b), low, zero))
            big = jnp.maximum(big, jnp.abs(s))
            sc[b * hp + p] = s
    for i in range(seqs // 2 * hp):
        ec[i] = jnp.exp(sc[i] + bias).astype(bf16)
    for b in range(seqs // 2):
        for p in range(hp):
            attend(b, p, ec[b * hp + p])

    @pl.when(jnp.logical_not(jnp.max(big) < SAFE))
    def _():
        for b in range(seqs // 2):

            @pl.loop(0, hp)
            def _(p):
                s = sc[b * hp + p] + bias
                top0 = jnp.max(jnp.where(first_head, s, -2e30), -1, keepdims=True)
                top1 = jnp.max(jnp.where(first_head, -2e30, s), -1, keepdims=True)
                attend(b, p, jnp.exp(s - jnp.where(first_head, top0, top1)).astype(bf16))

    attended = jnp.concatenate(
        [jnp.concatenate([att[p, t * pitch : t * pitch + seqs] for p in range(hp)], 1) for t in range(tokens)], 0
    ).astype(bf16)
    mid = x_ref[...].astype(f32).reshape(rows, d) + dot(attended, wo_ref[...])
    at = pl.ds(pl.multiple_of(step * seqs, seqs), seqs)
    ms[at, :] = jnp.sum(mid.reshape(tokens, seqs, d), 0)
    n2 = (norm_parts(mid)[0] * gains_ref[1:2, :] + shifts_ref[1:2, :]).astype(bf16)
    chunk = 512
    for c in range(0, ff, chunk):
        v = dot(n2, wup_ref[:, c : c + chunk])
        t = jnp.tanh(v * (GELU_C + (GELU_C * GELU_A) * (v * v)))
        h = (0.5 * v) * (1.0 + t)
        hs[at, c : c + chunk] = jnp.sum(h.reshape(tokens, seqs, chunk), 0)

    @pl.when(step == pl.num_programs(0) - 1)
    def _():
        hi, lo = split_bf16(hs[...] * (1.0 / tokens))
        u = ms[...] * (1.0 / tokens) + dot(hi, wdown_ref[...]) + dot(lo, wdown_ref[...])
        n = u.shape[0]
        out_ref[:n] = (u * lax.rsqrt(jnp.sum(u * u, -1, keepdims=True) + 1e-6)).astype(bf16)
        if out_ref.shape[0] > n:
            out_ref[n:] = count_rows(valid_ref, d)


def image_embed(xt, valid, gains, shifts, wqkv, wo, wup, wdown, start, count, note, seqs=16):
    tokens, _, d = xt.shape
    ff = wup.shape[1]
    pad = -(-tokens // 8) * 8
    pitch = seqs + PITCH
    tiles = seqs // 2 * (d // LANES)
    first = start // seqs
    rows = count + (NOTE if note else 0)
    return pl.pallas_call(
        functools.partial(image_kernel, seqs),
        grid=(count // seqs,),
        in_specs=[pl.BlockSpec((tokens, seqs, d), lambda i: (0, i + first, 0))]
        + [whole(a) for a in (valid, gains, shifts, wqkv, wo, wup, wdown)],
        out_specs=pl.BlockSpec((rows, d), lambda i: (0, 0)),
        out_shape=jax.ShapeDtypeStruct((rows, d), bf16),
        scratch_shapes=[
            pltpu.VMEM((3 * d // LANES, pitch * pad, LANES), f32),
            pltpu.VMEM((d // LANES, pitch * pad, LANES), f32),
            pltpu.VMEM((tiles, 2 * pad, 4 * pad), f32),
            pltpu.VMEM((tiles, 2 * pad, 4 * pad), bf16),
            pltpu.VMEM((count, ff), f32),
            pltpu.VMEM((count, d), f32),
        ],
        compiler_params=params(),
        cost_estimate=cost(0.45 * count),
        name="image_block",
    )(xt, valid, gains, shifts, wqkv, wo, wup, wdown)


def real_tokens(length, txt):
    seqs = length.shape[0]
    spread = jnp.broadcast_to(length[:, None, :], (seqs, txt, 1)).reshape(seqs * txt, 1)
    pos = lax.broadcasted_iota(jnp.int32, (seqs * txt, 1), 0) % txt
    return jnp.where(pos.astype(f32) < spread, 1.0, 0.0)


def text_forward_kernel(
    txt, held, x_ref, key_ref, flen_ref, gains_ref, shifts_ref, wqkv_ref, wo_ref, wup_ref, wdown_ref, *refs,
):
    (n1_ref, qkv_ref, probs_ref, att_ref, n2_ref, slope_ref, stat_ref, hpool_ref, u_ref, emb_ref, ms, sc, ec) = refs[held:]
    step = pl.program_id(0)
    rows, d = x_ref.shape
    ff = wup_ref.shape[1]
    seqs = rows // txt
    x = x_ref[...].astype(f32)
    xhat1, rstd1 = norm_parts(x)
    n1 = (xhat1 * gains_ref[0:1, :] + shifts_ref[0:1, :]).astype(bf16)
    n1_ref[...] = n1
    qkv_ref[:, :d] = (dot(n1, wqkv_ref[:, :d]) * HEAD**-0.5).astype(bf16)
    qkv_ref[:, d:] = dot(n1, wqkv_ref[:, d:]).astype(bf16)
    low = lax.broadcasted_iota(jnp.int32, (LANES, LANES), 1) < HEAD
    same = (
        lax.broadcasted_iota(jnp.int32, (LANES, LANES), 0) // txt
        == lax.broadcasted_iota(jnp.int32, (LANES, LANES), 1) // txt
    )
    zero = jnp.zeros((LANES, LANES), bf16)
    hp = d // LANES
    tiles = [(g, p) for g in range(rows // LANES) for p in range(hp)]

    def attend(g, p, probs):
        r = slice(g * LANES, (g + 1) * LANES)
        probs_ref[g * hp + p] = probs
        v = qkv_ref[r, 2 * d + p * LANES : 2 * d + (p + 1) * LANES]
        att_ref[r, p * LANES : (p + 1) * LANES] = dot(probs, stack_heads(v, low, zero)).astype(bf16)

    def share(s, top):
        halves = []
        for h in range(2):
            sh = s[:, h * LANES : (h + 1) * LANES]
            e = jnp.exp(sh - jnp.max(sh, -1, keepdims=True)) if top else jnp.exp(sh)
            halves.append(e / jnp.sum(e, -1, keepdims=True))
        return jnp.concatenate(halves, 1).astype(bf16)

    big = jnp.zeros((LANES, 2 * LANES), f32)
    for g, p in tiles:
        r = slice(g * LANES, (g + 1) * LANES)
        bias = jnp.where(same & (key_ref[0, g : g + 1, :] > 0), 0.0, -1e30)
        q = qkv_ref[r, p * LANES : (p + 1) * LANES]
        k = qkv_ref[r, d + p * LANES : d + (p + 1) * LANES]
        s = dot_nt(q, stack_heads(k, low, zero))
        big = jnp.maximum(big, jnp.abs(s))
        sc[g * hp + p] = s + jnp.concatenate([bias, bias], 1)
    for g, p in tiles:
        ec[g * hp + p] = share(sc[g * hp + p], False)
    for g, p in tiles:
        attend(g, p, ec[g * hp + p])

    @pl.when(jnp.logical_not(jnp.max(big) < SAFE))
    def _():
        for g, p in tiles:
            attend(g, p, share(sc[g * hp + p], True))

    mid = x + dot(att_ref[...], wo_ref[...])
    xhat2, rstd2 = norm_parts(mid)
    lane = lax.broadcasted_iota(jnp.int32, (rows, LANES), 1)
    hi1, hi2 = rstd1.astype(bf16).astype(f32), rstd2.astype(bf16).astype(f32)
    stat = jnp.where(lane < 64, jnp.where(lane < 32, hi1, rstd1 - hi1), jnp.where(lane < 96, hi2, rstd2 - hi2))
    stat_ref[...] = stat.astype(bf16)
    at = pl.ds(pl.multiple_of(step * seqs, seqs), seqs)
    keep = real_tokens(flen_ref[at, :], txt)
    n2 = ((xhat2 * gains_ref[1:2, :] + shifts_ref[1:2, :]) * keep).astype(bf16)
    n2_ref[...] = n2
    ms[at, :] = jnp.sum((mid * keep).reshape(seqs, txt, d), 1)
    chunk = 512
    for c in range(0, ff, chunk):
        v = dot(n2, wup_ref[:, c : c + chunk])
        v2 = v * v
        t = jnp.tanh(v * (GELU_C + (GELU_C * GELU_A) * v2))
        half = 0.5 + 0.5 * t
        h = v * half
        slope = half + h * (1.0 - t) * (GELU_C + (3.0 * GELU_C * GELU_A) * v2)
        slope_ref[:, c : c + chunk] = (slope * keep).astype(bf16)
        hpool_ref[at, c : c + chunk] = jnp.sum(h.reshape(seqs, txt, chunk), 1)

    @pl.when(step == pl.num_programs(0) - 1)
    def _():
        hi, lo = split_bf16(hpool_ref[...])
        pooled = ms[...] + dot(hi, wdown_ref[...]) + dot(lo, wdown_ref[...])
        u = pooled / flen_ref[...]
        u_ref[...] = u
        emb_ref[...] = (u * lax.rsqrt(jnp.sum(u * u, -1, keepdims=True) + 1e-6)).astype(bf16)


def text_forward(piece, pieces, held, x, key_ok, flen, gains, shifts, wqkv, wo, wup, wdown, txt, rows=512):
    total, d = x.shape
    ff = wup.shape[1]
    pairs = total // txt
    hp = d // LANES
    part = pairs // pieces
    steps = total // pieces // rows
    first = piece * steps
    block = lambda *tail: pl.BlockSpec((rows,) + tail, lambda i: (i + first,) + (0,) * len(tail))
    still = lambda *shape: pl.BlockSpec(shape, lambda i: (piece, 0))
    shape = jax.ShapeDtypeStruct
    key3 = key_ok.reshape(total // rows, rows // LANES, LANES)
    args = (x, key3, flen, gains, shifts, wqkv, wo, wup, wdown)
    return pl.pallas_call(
        functools.partial(text_forward_kernel, txt, len(held)),
        grid=(steps,),
        in_specs=[
            block(d), pl.BlockSpec((1, rows // LANES, LANES), lambda i: (i + first, 0, 0)), still(part, 1)
        ]
        + [whole(a) for a in args[3:]]
        + [pl.BlockSpec(memory_space=pl.ANY)] * len(held),
        out_specs=[
            block(d), block(3 * d), pl.BlockSpec((rows // LANES * hp, LANES, 2 * LANES), lambda i: (i + first, 0, 0)),
            block(d), block(d), block(ff), block(LANES), still(part, ff), still(part, d), still(part, d),
        ],
        out_shape=[
            shape((total, d), bf16), shape((total, 3 * d), bf16), shape((total // LANES * hp, LANES, 2 * LANES), bf16),
            shape((total, d), bf16), shape((total, d), bf16), shape((total, ff), bf16), shape((total, LANES), bf16),
            shape((pairs, ff), f32), shape((pairs, d), f32), shape((pairs, d), bf16),
        ],
        input_output_aliases={len(args) + i: i for i in range(len(held))},
        scratch_shapes=[
            pltpu.VMEM((part, d), f32),
            pltpu.VMEM((rows // LANES * hp, LANES, 2 * LANES), f32),
            pltpu.VMEM((rows // LANES * hp, LANES, 2 * LANES), bf16),
        ],
        compiler_params=params(30 * 1024 * 1024),
        cost_estimate=cost(0.013 * total / pieces),
        name="text_forward",
    )(*args, *held)


def scores_kernel(
    group, place_ref, own_ref, other_ref, own_valid_ref, other_valid_ref, scale_ref, a0_ref, a1_ref,
    s_ref, all_ref, col_out, okay_out, row_out,
):
    step = pl.program_id(0)
    pairs = own_ref.shape[0]
    scale = scale_ref[0]
    row = lax.broadcasted_iota(jnp.int32, (pairs, 1), 0).astype(f32)
    mask = [jnp.where(row < jnp.sum(v[...], 1, keepdims=True), 1.0, 0.0) for v in (own_valid_ref, other_valid_ref)]
    mask = jnp.concatenate(mask, 0)
    inner = lax.rem(place_ref[0], group)
    late = lax.bitwise_xor(step, lax.div(place_ref[0], group)) >= pl.num_programs(0) // 2
    texts = jnp.concatenate([own_ref[...], other_ref[...]], 0)

    @pl.when(step == 0)
    def _():
        row_out[...] = jnp.zeros_like(row_out)
        row_out[:, 3:4] = mask

    lane = lax.broadcasted_iota(jnp.int32, (1, pairs), 1).astype(f32)
    for k in range(group):
        at = lax.bitwise_xor(k, inner)
        cols = slice(k * pairs, (k + 1) * pairs)
        a = jnp.where(late, a1_ref[at], a0_ref[at])
        images = a[:pairs]
        count = a[pairs : pairs + 1, 0:1].astype(f32)
        okay = jnp.where(lane < count, 1.0, 0.0)
        okay_out[0:1, cols] = okay
        all_ref[cols, :] = images
        s = scale * dot_nt(texts, images)
        s_ref[:, cols] = s
        up = jnp.exp(s - SHIFT)
        down = jnp.exp(jnp.minimum(s, 0.0) + SHIFT)
        col_out[0:1, cols] = jnp.sum(up * mask, 0, keepdims=True)
        col_out[1:2, cols] = jnp.sum(down * mask, 0, keepdims=True)
        row_out[:, 0:1] += jnp.sum(up * okay, 1, keepdims=True)
        row_out[:, 1:2] += jnp.sum(down * okay, 1, keepdims=True)
        row_out[:, 2:3] += jnp.broadcast_to(count, (2 * pairs, 1))


def pair_scores(place, own, other, own_valid, other_valid, scale, a0, a1):
    slots, _, d = a0.shape
    pairs = own.shape[0]
    group = min(8, slots)
    groups = slots // group
    cols = group * pairs
    keep = lambda *_: (0, 0)
    turn = lambda i, s: (lax.rem(lax.bitwise_xor(i, lax.div(s[0], group)), groups), 0, 0)
    still = lambda a: pl.BlockSpec(a.shape, keep)
    shape = jax.ShapeDtypeStruct
    return pl.pallas_call(
        functools.partial(scores_kernel, group),
        grid_spec=pltpu.PrefetchScalarGridSpec(
            num_scalar_prefetch=1,
            grid=(2 * groups,),
            in_specs=[still(own), still(other), still(own_valid), still(other_valid), pl.BlockSpec(memory_space=pltpu.SMEM)]
            + [pl.BlockSpec((group,) + a.shape[1:], turn) for a in (a0, a1)],
            out_specs=[
                pl.BlockSpec((2 * pairs, cols), lambda i, s: (0, i)),
                pl.BlockSpec((cols, d), lambda i, s: (i, 0)),
                pl.BlockSpec((2, cols), lambda i, s: (0, i)),
                pl.BlockSpec((1, cols), lambda i, s: (0, i)),
                pl.BlockSpec((2 * pairs, 4), keep),
            ],
        ),
        out_shape=[
            shape((2 * pairs, 2 * groups * cols), f32), shape((2 * groups * cols, d), bf16),
            shape((2, 2 * groups * cols), f32), shape((1, 2 * groups * cols), f32), shape((2 * pairs, 4), f32),
        ],
        compiler_params=params(2 * HOP_VMEM),
        cost_estimate=cost(4.0),
        name="pair_scores",
    )(place, own, other, own_valid, other_valid, scale, a0, a1)


def log_sum(up, down):
    fine = up >= 1.9287498479639178e-22
    return jnp.where(
        fine, jnp.log(jnp.where(fine, up, 1.0)) + SHIFT, jnp.log(jnp.where(fine, 1.0, down)) - SHIFT
    )


def gradient_kernel(
    dp, scale_ref, s_ref, all_ref, col_ref, got_ref, okay_ref, row_ref, swap_ref, text_ref, a_ref,
    grad_ref, back_ref, loss_ref,
):
    step = pl.program_id(0)
    pairs = text_ref.shape[0]
    row = row_ref[...] + jnp.concatenate([swap_ref[pairs:], swap_ref[:pairs]], 0)
    factor = 0.5 / row[0:1, 2:3]
    mask = row_ref[:, 3:4]
    okay = okay_ref[...]
    row_lse = log_sum(row[:, 0:1], row[:, 1:2])
    col = col_ref[...] + got_ref[...]
    col_lse = log_sum(col[0:1, :], col[1:2, :])

    @pl.when(step == 0)
    def _():
        grad_ref[...] = jnp.zeros_like(grad_ref)
        back_ref[...] = jnp.zeros_like(back_ref)
        loss_ref[...] = jnp.zeros_like(loss_ref)
        t = text_ref[...].astype(f32) * a_ref[:pairs].astype(f32)
        diag = scale_ref[0] * jnp.sum(t, -1, keepdims=True)
        m = mask[:pairs]
        loss_ref[0:1, 0:1] = factor * jnp.sum(m * (row_lse[:pairs] - 2.0 * diag), 0, keepdims=True)
        loss_ref[1:2, 0:1] = -2.0 * factor * jnp.sum(m * diag, 0, keepdims=True)

    s = s_ref[...]
    g = jnp.exp(jnp.minimum(s - row_lse, 1.0)) + jnp.exp(jnp.minimum(s - col_lse, 1.0))
    g = g * ((factor * mask) * okay)
    grad = dot(g.astype(bf16), all_ref[...])
    grad_ref[...] += grad[:pairs]
    back_ref[...] += grad[pairs:]
    cols = jnp.sum(jnp.where(okay > 0, col_lse, 0.0), 1, keepdims=True)
    loss_ref[0:1, 0:1] += factor * (cols * (1.0 / dp))
    loss_ref[1:2, 0:1] += jnp.sum(jnp.sum(g * s, 0, keepdims=True), 1, keepdims=True)


def pair_gradients(dp, scale, scores, images, col, got, okay, row, swap, texts, a):
    pairs, d = texts.shape
    cols = min(8, dp) * pairs
    still = lambda *shape: pl.BlockSpec(shape, lambda i: (0, 0))
    shape = jax.ShapeDtypeStruct
    return pl.pallas_call(
        functools.partial(gradient_kernel, dp),
        grid=(dp * pairs // cols,),
        in_specs=[
            pl.BlockSpec(memory_space=pltpu.SMEM),
            pl.BlockSpec((2 * pairs, cols), lambda i: (0, i)),
            pl.BlockSpec((cols, d), lambda i: (i, 0)),
            pl.BlockSpec((2, cols), lambda i: (0, i)),
            pl.BlockSpec((2, cols), lambda i: (0, i)),
            pl.BlockSpec((1, cols), lambda i: (0, i)),
        ]
        + [whole(x) for x in (row, swap, texts, a)],
        out_specs=[still(pairs, d), still(pairs, d), still(8, LANES)],
        out_shape=[shape((pairs, d), f32), shape((pairs, d), f32), shape((8, LANES), f32)],
        compiler_params=params(2 * HOP_VMEM),
        cost_estimate=cost(3.0),
        name="pair_gradients",
    )(scale, scores, images, col, got, okay, row, swap, texts, a)


def spread_rows(a, txt):
    seqs, width = a.shape
    return jnp.broadcast_to(a[:, None, :], (seqs, txt, width)).reshape(seqs * txt, width)


def backward_up_kernel(
    txt, scale_ref, rep_ref, part_ref, back_ref, row_ref, swap_ref, a_ref, u_ref, len_ref, hpool_ref, n2_ref, slope_ref,
    wdown_ref, send_ref, keep_ref, gd_ref, dh_ref, down, acc,
):
    step = pl.program_id(0)
    rows, d = n2_ref.shape
    ff = slope_ref.shape[1]
    seqs = rows // txt

    @pl.when(step == 0)
    def _():
        pairs = part_ref.shape[0]
        scale = scale_ref[0]
        factor = 0.5 / (row_ref[0:1, 2:3] + swap_ref[0:1, 2:3])
        images = a_ref[:pairs].astype(f32)
        u = u_ref[...]
        r = lax.rsqrt(jnp.sum(u * u, -1, keepdims=True) + 1e-6)
        g = scale * (part_ref[...] + back_ref[...]) - (2.0 * scale) * (factor * row_ref[:pairs, 3:4]) * images
        du = (r * g - (r * r * r) * u * jnp.sum(u * g, -1, keepdims=True)) / len_ref[...]
        gd_ref[...] = du
        low = du.astype(bf16)
        dh_ref[...] = dot_nt(low, wdown_ref[...])
        hi, lo = split_bf16(hpool_ref[...])
        down[...] = (dot_tn(hi, low) + dot_tn(lo, low)).astype(bf16)
        acc[...] = jnp.zeros_like(acc)

    at = pl.ds(pl.multiple_of(step * seqs, seqs), seqs)
    chunk = 512
    for c in range(0, ff, chunk):
        cs = slice(c, c + chunk)
        grad_before = (spread_rows(dh_ref[at, cs], txt) * slope_ref[:, cs].astype(f32)).astype(bf16)
        acc[:, cs] += dot_tn(n2_ref[...], grad_before)

    @pl.when(step == pl.num_programs(0) - 1)
    def _():
        first = rep_ref[0] == 0
        for b in range(ff // d):
            r = slice(b * d, (b + 1) * d)
            up = acc[:, r].astype(bf16)
            keep_ref[r] = jnp.where(first, down[r], up)
            send_ref[r] = jnp.where(first, up, down[r])


def backward_up(scale, rep, part, back, row, swap, a, u, flen, hpool, n2, slope, wdown, txt, rows=512):
    tokens, d = n2.shape
    pairs, ff = hpool.shape
    block = lambda w: pl.BlockSpec((rows, w), lambda i: (i, 0))
    shape = jax.ShapeDtypeStruct
    smem = pl.BlockSpec(memory_space=pltpu.SMEM)
    outs = [shape((ff, d), bf16), shape((ff, d), bf16), shape((pairs, d), f32), shape((pairs, ff), f32)]
    return pl.pallas_call(
        functools.partial(backward_up_kernel, txt),
        grid=(tokens // rows,),
        in_specs=[smem, smem]
        + [whole(x) for x in (part, back, row, swap, a, u, flen, hpool)]
        + [block(d), block(ff), whole(wdown)],
        out_specs=[whole(x) for x in outs],
        out_shape=outs,
        scratch_shapes=[pltpu.VMEM((ff, d), bf16), pltpu.VMEM((d, ff), f32)],
        compiler_params=params(30 * 1024 * 1024),
        cost_estimate=cost(0.006 * tokens),
        name="backward_up",
    )(scale, rep, part, back, row, swap, a, u, flen, hpool, n2, slope, wdown)


def backward_middle_kernel(
    txt, gd_ref, dh_ref, len_ref, n2_ref, slope_ref, stat_ref, att_ref, gains_ref, shifts_ref, wup_ref, wo_ref,
    gmid_ref, datt_ref, dwo_ref, gain_ref, acc,
):
    step = pl.program_id(0)
    rows, d = n2_ref.shape
    ff = wup_ref.shape[1]

    @pl.when(step == 0)
    def _():
        acc[...] = jnp.zeros_like(acc)
        gain_ref[...] = jnp.zeros_like(gain_ref)

    dn2 = jnp.zeros((rows, d), f32)
    chunk = 512
    for c in range(0, ff, chunk):
        cs = slice(c, c + chunk)
        grad_before = (spread_rows(dh_ref[:, cs], txt) * slope_ref[:, cs].astype(f32)).astype(bf16)
        dn2 += dot_nt(grad_before, wup_ref[:, cs])
    xhat = (n2_ref[...].astype(f32) - shifts_ref[1:2, :]) / gains_ref[1:2, :]
    stat = stat_ref[...].astype(f32)
    gain_ref[0:1, :] += jnp.sum(dn2 * xhat, 0, keepdims=True)
    gain_ref[1:2, :] += jnp.sum(dn2, 0, keepdims=True)
    gn = dn2 * gains_ref[1:2, :]
    dmid = (stat[:, 64:65] + stat[:, 96:97]) * (
        gn - jnp.mean(gn, -1, keepdims=True) - xhat * jnp.mean(gn * xhat, -1, keepdims=True)
    )
    gmid = spread_rows(gd_ref[...], txt) * real_tokens(len_ref[...], txt) + dmid
    gmid_ref[...] = gmid
    branch = gmid.astype(bf16)
    acc[...] += dot_tn(att_ref[...], branch)
    datt_ref[...] = dot_nt(branch, wo_ref[...]).astype(bf16)

    @pl.when(step == pl.num_programs(0) - 1)
    def _():
        dwo_ref[...] = acc[...].astype(bf16)


def backward_middle(gd, dh, flen, n2, slope, stat, att, gains, shifts, wup, wo, txt, rows=512):
    tokens, d = n2.shape
    ff = wup.shape[1]
    block = lambda w: pl.BlockSpec((rows, w), lambda i: (i, 0))
    lead = lambda w: pl.BlockSpec((rows // txt, w), lambda i: (i, 0))
    shape = jax.ShapeDtypeStruct
    sums = [shape((d, d), bf16), shape((8, d), f32)]
    return pl.pallas_call(
        functools.partial(backward_middle_kernel, txt),
        grid=(tokens // rows,),
        in_specs=[lead(d), lead(ff), lead(1), block(d), block(ff), block(LANES), block(d)]
        + [whole(x) for x in (gains, shifts, wup, wo)],
        out_specs=[block(d), block(d)] + [whole(x) for x in sums],
        out_shape=[shape((tokens, d), f32), shape((tokens, d), bf16)] + sums,
        scratch_shapes=[pltpu.VMEM((d, d), f32)],
        compiler_params=params(30 * 1024 * 1024),
        cost_estimate=cost(0.006 * tokens),
        name="backward_middle",
    )(gd, dh, flen, n2, slope, stat, att, gains, shifts, wup, wo)


def backward_attention_kernel(
    held, last, rep_ref, datt_ref, qkv_ref, probs_ref, n1_ref, dwo_ref, gain2_ref, sums_ref, gains_ref, shifts_ref, wqkv_ref,
    *refs
):
    old_acc, old_flat = refs[1:3] if held else (None, None)
    gq_ref, *outs = refs[held:-4]
    acc, flat, sc, ec = refs[-4:]
    step = pl.program_id(0)
    rows, d = n1_ref.shape
    low = lax.broadcasted_iota(jnp.int32, (LANES, LANES), 1) < HEAD
    zero = jnp.zeros((LANES, LANES), bf16)

    @pl.when(step == 0)
    def _():
        acc[...] = old_acc[...] if held else jnp.zeros_like(acc)
        flat[...] = old_flat[...] if held else jnp.zeros_like(flat)

    hp = d // LANES
    tiles = [(g, p) for g in range(rows // LANES) for p in range(hp)]
    at = lambda g, p, part: (slice(g * LANES, (g + 1) * LANES), slice(part * d + p * LANES, part * d + (p + 1) * LANES))
    for g, p in tiles:
        sc[g * hp + p] = dot_nt(datt_ref[at(g, p, 0)], stack_heads(qkv_ref[at(g, p, 2)], low, zero))
    for g, p in tiles:
        i = g * hp + p
        probs = probs_ref[i].astype(f32)
        halves = []
        for h in range(2):
            hs = slice(h * LANES, (h + 1) * LANES)
            ph, dh = probs[:, hs], sc[i, :, hs]
            halves.append(ph * (dh - jnp.sum(ph * dh, -1, keepdims=True)))
        ec[i] = jnp.concatenate(halves, 1).astype(bf16)
    for g, p in tiles:
        dv = dot_tn(probs_ref[g * hp + p], datt_ref[at(g, p, 0)])
        gq_ref[at(g, p, 2)] = jnp.where(low, dv[:LANES], dv[LANES:]).astype(bf16)
    for g, p in tiles:
        keys = stack_heads(qkv_ref[at(g, p, 1)], low, zero)
        gq_ref[at(g, p, 0)] = (dot(ec[g * hp + p], keys) * HEAD**-0.5).astype(bf16)
    for g, p in tiles:
        dk = dot_tn(ec[g * hp + p], qkv_ref[at(g, p, 0)])
        gq_ref[at(g, p, 1)] = jnp.where(low, dk[:LANES], dk[LANES:]).astype(bf16)
    gq = gq_ref[...]
    acc[...] += dot_tn(n1_ref[...], gq)
    flat[0:1, :] += jnp.sum(gq.astype(f32), 0, keepdims=True)

    @pl.when(step == pl.num_programs(0) - 1)
    def _():
        if not last:
            outs[0][...] = acc[...]
            outs[1][...] = flat[...]
            return
        send_ref, keep_ref, small_ref = outs
        w = wqkv_ref[...]
        ones = jnp.ones((8, 3 * d), bf16)
        hi, lo = split_bf16(acc[...] * w.astype(f32))
        spread = dot_nt(ones, hi) + dot_nt(ones, lo)
        hi, lo = split_bf16(flat[...])
        dshift = (dot_nt(hi, w) + dot_nt(lo, w))[0:1]
        dgain = (spread[0:1] - shifts_ref[0:1, :] * dshift) / gains_ref[0:1, :]
        small = [dgain, gain2_ref[0:1, :], dshift, gain2_ref[1:2, :]]
        small += [jnp.broadcast_to(sums_ref[i : i + 1, 0:1], (1, d)) for i in range(2)]
        small = jnp.concatenate(small + [jnp.zeros((2, d), f32)], 0)
        small_ref[...] = small
        first = rep_ref[0] == 0
        parts = [acc[:, b * d : (b + 1) * d].astype(bf16) for b in range(3)] + [dwo_ref[...]]
        for b in range(2):
            keep_ref[b * d : (b + 1) * d] = jnp.where(first, parts[b], parts[b + 2])
            send_ref[b * d : (b + 1) * d] = jnp.where(first, parts[b + 2], parts[b])
        put_small(send_ref, 2 * d, small)


def backward_attention(piece, pieces, held, rep, datt, qkv, probs, n1, dwo, gain2, sums, gains, shifts, wqkv, rows=512):
    tokens, d = n1.shape
    steps = tokens // pieces // rows
    first = piece * steps
    last = piece == pieces - 1
    block = lambda w: pl.BlockSpec((rows, w), lambda i: (i + first, 0))
    shape = jax.ShapeDtypeStruct
    if last:
        outs = [shape((2 * d + NOTE, d), bf16), shape((2 * d, d), bf16), shape((8, d), f32)]
    else:
        outs = [shape((d, 3 * d), f32), shape((8, 3 * d), f32)]
    args = (rep, datt, qkv, probs, n1, dwo, gain2, sums, gains, shifts, wqkv)
    return pl.pallas_call(
        functools.partial(backward_attention_kernel, len(held), last),
        grid=(steps,),
        in_specs=[
            pl.BlockSpec(memory_space=pltpu.SMEM), block(d), block(3 * d),
            pl.BlockSpec((rows // LANES * (d // LANES), LANES, 2 * LANES), lambda i: (i + first, 0, 0)),
            block(d),
        ]
        + [whole(x) for x in args[5:]]
        + ([pl.BlockSpec(memory_space=pl.ANY)] + [whole(x) for x in held[1:]] if held else []),
        out_specs=[block(3 * d)] + [whole(x) for x in outs],
        out_shape=[shape((tokens, 3 * d), bf16)] + outs,
        input_output_aliases={len(args): 0} if held else {},
        scratch_shapes=[
            pltpu.VMEM((d, 3 * d), f32),
            pltpu.VMEM((8, 3 * d), f32),
            pltpu.VMEM((rows // LANES * (d // LANES), LANES, 2 * LANES), f32),
            pltpu.VMEM((rows // LANES * (d // LANES), LANES, 2 * LANES), bf16),
        ],
        compiler_params=params(30 * 1024 * 1024),
        cost_estimate=cost(0.009 * tokens / pieces),
        name="backward_attention",
    )(*args, *held)


def backward_input_kernel(gq_ref, gmid_ref, n1_ref, stat_ref, gains_ref, shifts_ref, wqkv_ref, *refs):
    dx_ref = refs[-1]
    gn = dot_nt(gq_ref[...], wqkv_ref[...]) * gains_ref[0:1, :]
    xhat = (n1_ref[...].astype(f32) - shifts_ref[0:1, :]) / gains_ref[0:1, :]
    stat = stat_ref[...].astype(f32)
    dx_ref[...] = gmid_ref[...] + (stat[:, 0:1] + stat[:, 32:33]) * (
        gn - jnp.mean(gn, -1, keepdims=True) - xhat * jnp.mean(gn * xhat, -1, keepdims=True)
    )


def backward_input(piece, pieces, held, gq, gmid, n1, stat, gains, shifts, wqkv, rows=512):
    tokens, d = gmid.shape
    steps = tokens // pieces // rows
    block = lambda w: pl.BlockSpec((rows, w), lambda i: (i + piece * steps, 0))
    args = (gq, gmid, n1, stat, gains, shifts, wqkv)
    return pl.pallas_call(
        backward_input_kernel,
        grid=(steps,),
        in_specs=[block(3 * d), block(d), block(d), block(LANES), whole(gains), whole(shifts), whole(wqkv)]
        + [pl.BlockSpec(memory_space=pl.ANY)] * len(held),
        out_specs=block(d),
        out_shape=jax.ShapeDtypeStruct((tokens, d), f32),
        input_output_aliases={len(args): 0} if held else {},
        compiler_params=params(2 * HOP_VMEM),
        cost_estimate=cost(0.004 * tokens / pieces),
        name="backward_input",
    )(*args, *held)


def finish_kernel(places, rep_ref, own_ref, got_ref, *out_refs):
    first = rep_ref[0] == 0
    for out, top, left, begin, n, part in places:
        a = own_ref[begin : begin + n, :]
        b = got_ref[begin : begin + n, :]
        mine = first if part == 0 else jnp.logical_not(first)
        out_refs[out][top : top + n, left : left + a.shape[1]] = jnp.where(mine, a, b).astype(f32)


def finish(rep, own, got, shapes, segments):
    half = own.shape[0]
    places = []
    for row, count, out, top, left in segments:
        while count:
            part, begin = divmod(row, half)
            n = min(count, half - begin)
            places.append((out, top, left, begin, n, part))
            row, top, count = row + n, top + n, count - n
    outs = [jax.ShapeDtypeStruct(s, f32) for s in shapes]
    return pl.pallas_call(
        functools.partial(finish_kernel, places),
        grid=(1,),
        in_specs=[pl.BlockSpec(memory_space=pltpu.SMEM), whole(own), whole(got)],
        out_specs=[whole(x) for x in outs],
        out_shape=outs,
        compiler_params=params(2 * HOP_VMEM),
        cost_estimate=cost(3.0),
        name="finish",
    )(rep, own, got)


class Links:
    def __init__(self, mesh):
        self.dp, self.rep = mesh.shape["dp"], mesh.shape["rep"]
        self.bits = (self.dp - 1).bit_length()
        assert self.dp == 1 << self.bits and self.rep == 2
        near, far = list(range(min(2, self.bits))), list(range(2, self.bits))
        turn = lambda bits: list(zip(bits, bits[::-1]))
        self.near, self.far = turn(near), turn(far)
        self.gather_order = [(b, b) for b in far[::-1]] + self.near

    def bit(self, pair):
        place = lax.axis_index("dp")
        return jnp.where(lax.axis_index("rep") == 0, (place >> pair[0]) & 1, (place >> pair[1]) & 1)

    def across(self, x, pair):
        moves = [(2 * i + r, 2 * (i ^ (1 << pair[r])) + r) for i in range(self.dp) for r in range(2)]
        return lax.ppermute(x, ("dp", "rep"), moves)

    def core(self, x):
        return lax.ppermute(x, "rep", [(0, 1), (1, 0)])


def put_small(ref, at, small):
    hi, lo = split_bf16(small)
    ref[at : at + NOTE] = jnp.concatenate([hi, lo], 0)


def hop_kernel(kind, late, with_small, v_ref, x_ref, got_ref, *refs):
    n, d = x_ref.shape
    refs = list(refs)
    small_ref = refs.pop(0) if with_small else None
    low = v_ref[0] == 0
    if kind == "join":
        x, got = x_ref[...], got_ref[...]
        refs[0][:n] = jnp.where(low, x, got)
        refs[0][n:] = jnp.where(low, got, x)
        return
    add = lambda r: (x_ref[r].astype(f32) + got_ref[r].astype(f32)).astype(bf16)
    send_ref, keep_ref = refs[0], refs[1]
    if late == "half":
        m = n // 2
        a, b = add(slice(0, m)), add(slice(m, n))
        keep_ref[...] = jnp.where(low, a, b)
        send_ref[:m] = jnp.where(low, b, a)
    else:
        m = n
        x = add(slice(0, n))
        keep_ref[...] = x
        if late == "full":
            send_ref[:m] = x
    if with_small:
        hi, lo = got_ref[n : n + NOTE // 2], got_ref[n + NOTE // 2 :]
        small = small_ref[...] + (hi.astype(f32) + lo.astype(f32))
        refs[2][...] = small
        if send_ref.shape[0] > m:
            put_small(send_ref, m, small)


class Reduction:
    def __init__(self, links, send, keep, small=None):
        self.kind = None
        self.links, self.send, self.x, self.small = links, send, keep, small
        self.plan = (
            [("core", None)]
            + [("half", p) for p in links.near]
            + [("full", p) for p in links.far]
            + [("join", p) for p in links.near[::-1]]
            + [("last", None)]
        )

    def start(self, *after):
        links = self.links
        self.kind, self.pair = self.plan.pop(0)
        if after:
            self.send, *after = beside(self.send, *after)
        self.got = links.core(self.send) if self.pair is None else links.across(self.send, self.pair)
        return after

    def end(self):
        kind, x, links = self.kind, self.x, self.links
        if kind == "last":
            return
        n, d = x.shape
        shape = jax.ShapeDtypeStruct
        late, pair = self.plan[0]
        if kind == "join":
            v, outs = links.bit(self.pair), [shape((2 * n, d), bf16)]
        else:
            v = links.bit(pair) if late == "half" else jnp.zeros((), jnp.int32)
            m = n // 2 if late == "half" else n
            more = NOTE if self.small is not None and late in ("half", "full") else 0
            outs = [shape((m + more if late in ("half", "full") else NOTE, d), bf16), shape((m, d), bf16)]
        args = [v.astype(jnp.int32).reshape(1), x, self.got]
        with_small = self.small is not None and kind != "join"
        if with_small:
            args.append(self.small)
            outs.append(shape(self.small.shape, f32))
        out = pl.pallas_call(
            functools.partial(hop_kernel, kind, late, with_small),
            in_specs=[pl.BlockSpec(memory_space=pltpu.SMEM)] + [pl.BlockSpec(memory_space=pltpu.VMEM)] * (len(args) - 1),
            out_specs=[pl.BlockSpec(memory_space=pltpu.VMEM)] * len(outs),
            out_shape=outs,
            compiler_params=params(HOP_VMEM),
            cost_estimate=cost(1.0),
            name="hop",
        )(*args)
        if kind == "join":
            self.send = self.x = out[0]
            return
        self.x = out[1]
        self.send = out[0] if late in ("half", "full") else self.x
        if with_small:
            self.small = out[2]


def beside(*values):
    return lax.optimization_barrier(values)


def body(
    links, image_in, img_gains, img_shifts, img_qkv, img_out, img_up, img_down, text_in, lengths, valid,
    txt_gains, txt_shifts, txt_qkv, txt_out, txt_up, txt_down, log_scale,
):
    dp, bits = links.dp, links.bits
    pairs, txt, d = text_in.shape
    ff = txt_up.shape[1]
    tokens = pairs * txt
    scale = jnp.exp(log_scale).reshape(1)
    rep = lax.axis_index("rep").astype(jnp.int32).reshape(1)
    order = links.gather_order

    own_valid = valid.astype(f32)[None, :]
    other_valid = links.core(own_valid)
    flen = lengths.astype(f32)[:, None]
    key_ok = (jnp.arange(txt)[None, :] < lengths[:, None]).astype(f32).reshape(tokens // LANES, LANES)

    image_args = (valid[None, :], img_gains, img_shifts, img_qkv, img_out, img_up, img_down)
    emb = image_embed(image_in.transpose(1, 0, 2), *image_args, 0, pairs, True)
    text_args = (txt_gains, txt_shifts, txt_qkv, txt_out, txt_up, txt_down)
    text_x, emb = beside(text_in.reshape(tokens, d), emb)
    steps, pieces = list(order), 4
    a, held = emb[None], []
    for piece in range(pieces):
        if steps:
            got = links.across(a, steps.pop(0))
        held = list(text_forward(piece, pieces, held, text_x, key_ok, flen, *text_args, txt))
        if steps:
            text_x, got, held[-1] = beside(text_x, got, held[-1])
            a = jnp.concatenate([a, got], 0)
    while steps:
        got = links.across(a, steps.pop(0))
        if steps:
            a = jnp.concatenate([a, got], 0)
    n1, qkv, probs, att, n2, slope, stat, hpool, u, text_emb = held

    place = sum(links.bit(order[i]) << i for i in range(bits)).astype(jnp.int32).reshape(1)
    scores, images, col, okay, row = pair_scores(
        place, text_emb, links.core(text_emb), own_valid, other_valid, scale, a, got
    )
    swap = links.core(row)
    for pair in order[:-1]:
        col = col + links.across(col, pair)
    col_got = links.across(col, order[-1])
    part, other, sums = pair_gradients(dp, scale, scores, images, col, col_got, okay, row, swap, text_emb, emb)
    back = links.core(other)

    ffn_send, ffn_keep, gd, dh = backward_up(scale, rep, part, back, row, swap, emb, u, flen, hpool, n2, slope, txt_down, txt)
    first = Reduction(links, ffn_send, ffn_keep)
    first.start()
    gmid, datt, dwo, gain2 = backward_middle(
        gd, dh, flen, n2, slope, stat, att, txt_gains, txt_shifts, txt_up, txt_out, txt
    )
    held = []
    for piece in range(2):
        datt, first.got, *held = beside(datt, first.got, *held)
        first.end()
        first.start()
        held = list(backward_attention(
            piece, 2, held, rep, datt, qkv, probs, n1, dwo, gain2, sums, txt_gains, txt_shifts, txt_qkv
        ))
    gq, att_send, att_keep, small = held
    att_send, first.got = beside(att_send, first.got)
    second = Reduction(links, att_send, att_keep, small)
    dx, done = [], []

    def inputs(piece, stream):
        gq_now, stream.x = beside(gq, stream.x)
        dx[:] = [backward_input(piece, 2, dx, gq_now, gmid, n1, stat, txt_gains, txt_shifts, txt_qkv)]

    other = {first: second, second: first}
    far = len(links.far)
    for act, stream in (
        [("s", second), ("e", first), ("s", first), ("e", second), ("s", second), ("i", 0), ("e", second), ("s", second)]
        + [("e", first), ("s", first), ("e", second), ("s", second), ("i", 1), ("e", second), ("s", second)]
        + [("e", first), ("s", first), ("e", second), ("s", second), ("e", first), ("s", first)] * (far > 0)
    ):
        if act == "i":
            inputs(stream, second)
        elif act == "e":
            stream.end()
        elif stream.plan:
            if stream is second and second.kind is None:
                stream.start()
            else:
                other[stream].x, *dx[:] = stream.start(other[stream].x, *dx)
    while first.plan or second.plan:
        for stream in (second, first):
            if stream.plan:
                stream.end()
                stream.start()
    grad_down, grad_up = finish(
        rep, first.x, first.got, [(ff, d), (d, ff)], [(0, ff, 0, 0, 0)] + [(ff + i * d, d, 1, 0, i * d) for i in range(ff // d)]
    )
    grad_qkv, grad_out = finish(
        rep, second.x, second.got, [(d, 3 * d), (d, d)], [(i * d, d, 0, 0, i * d) for i in range(3)] + [(3 * d, d, 1, 0, 0)]
    )
    small, dx = second.small, dx[0]
    return (
        small[4, 0],
        small[0:2],
        small[2:4],
        grad_qkv,
        grad_out,
        grad_up,
        grad_down,
        small[5, 0],
        dx.reshape(pairs, txt, d),
    )


def solution(mesh):
    both = ("dp", "rep")
    deep = P(both, None, None)
    in_specs = (deep,) + (P(),) * 6 + (deep, P(both), P(both)) + (P(),) * 7
    out_specs = (P(),) * 8 + (deep,)
    return jax.shard_map(
        functools.partial(body, Links(mesh)), mesh=mesh, in_specs=in_specs, out_specs=out_specs, check_vma=False
    )
```

```python
import functools
import jax
import jax.numpy as jnp
from jax import lax
from jax.experimental import pallas as pl
from jax.experimental.pallas import tpu as pltpu
from jax.sharding import PartitionSpec as P

HEAD = 64
LANES = 128
f32 = jnp.float32
bf16 = jnp.bfloat16
GELU_C = 0.7978845608028654
GELU_A = 0.044715
SHIFT = 50.0
SAFE = 80.0
NOTE = 16
PITCH = 8
VMEM = 60 * 1024 * 1024
HOP_VMEM = 12 * 1024 * 1024


def dot(a, b):
    return jnp.dot(a, b, preferred_element_type=f32)


def dot_nt(a, b):
    return lax.dot_general(a, b, (((1,), (1,)), ((), ())), preferred_element_type=f32)


def dot_tn(a, b):
    return lax.dot_general(a, b, (((0,), (0,)), ((), ())), preferred_element_type=f32)


def norm_parts(x):
    mu = jnp.mean(x, -1, keepdims=True)
    c = x - mu
    rstd = lax.rsqrt(jnp.mean(c * c, -1, keepdims=True) + 1e-6)
    return c * rstd, rstd


def whole(a):
    return pl.BlockSpec(a.shape, lambda *_: (0,) * a.ndim)


def params(limit=VMEM):
    return pltpu.CompilerParams(vmem_limit_bytes=limit)


def cost(us):
    return pl.CostEstimate(flops=int(us * 1.1e9), bytes_accessed=0, transcendentals=0)


def split_bf16(v):
    hi = v.astype(bf16)
    return hi, (v - hi.astype(f32)).astype(bf16)


def count_rows(valid_ref, d):
    count = jnp.sum(valid_ref[...].astype(f32), 1, keepdims=True)
    return jnp.broadcast_to(count, (NOTE, d)).astype(bf16)


def stack_heads(a, low, zero):
    return jnp.concatenate([jnp.where(low, a, zero), jnp.where(low, zero, a)], 0)


def image_kernel(
    seqs, x_ref, old_ref, valid_ref, gains_ref, shifts_ref, wqkv_ref, wo_ref, wup_ref, wdown_ref, out_ref,
    qkv, att, sc, ec, hs, ms,
):
    tokens, _, d = x_ref.shape
    pad = -(-tokens // 8) * 8
    pitch = seqs + PITCH
    rows, pair = seqs * tokens, 2 * pad
    step, last = pl.program_id(0), pl.num_programs(0) - 1
    now, then = lax.rem(step, 2), lax.rem(step + 1, 2)
    ff = wup_ref.shape[1]
    hp = d // LANES

    @pl.when(step == 0)
    def _():
        qkv[:, tokens * pitch :] = jnp.zeros((3 * hp, (pad - tokens) * pitch, LANES), f32)

    low = lax.broadcasted_iota(jnp.int32, (pair, LANES), 1) < HEAD
    key_lane = lax.broadcasted_iota(jnp.int32, (pair, 2 * pair), 1)
    query_row = lax.broadcasted_iota(jnp.int32, (pair, 2 * pair), 0)
    first_head = key_lane < pair
    key_row = jnp.where(first_head, key_lane, key_lane - pair)
    second_image = key_row >= pad
    key_pos = jnp.where(second_image, key_row - pad, key_row)
    bias = jnp.where((key_pos < tokens) & (second_image == (query_row >= pad)), 0.0, -1e30)
    zero, one = jnp.zeros((pair, LANES), bf16), jnp.ones((pair, LANES), bf16)
    ones = stack_heads(one, low, zero)
    tiles = [(b, p) for b in range(seqs // 2) for p in range(hp)]

    def pick(j, b):
        return jnp.concatenate([qkv[j, pl.ds(2 * b + i, pad, stride=pitch), :] for i in range(2)], 0).astype(bf16)

    def attend(b, p, e):
        v = stack_heads(pick(2 * hp + p, b), low, zero)
        o = dot(e, jnp.concatenate([v, ones], 1))
        o = o[:, :LANES] / o[:, LANES:]
        for i in range(2):
            att[now, p, pl.ds(2 * b + i, pad, stride=pitch), :] = o[i * pad : (i + 1) * pad]

    def project(n1, c):
        r = dot(n1, wqkv_ref[:, c * d : (c + 1) * d])
        r = r * HEAD**-0.5 if c == 0 else r
        for p in range(hp):
            for t in range(tokens):
                qkv[c * hp + p, t * pitch : t * pitch + seqs] = r[t * seqs : (t + 1) * seqs, p * LANES : (p + 1) * LANES]

    def attention():
        x = x_ref[...].astype(f32).reshape(rows, d)
        n1 = (norm_parts(x)[0] * gains_ref[0:1, :] + shifts_ref[0:1, :]).astype(bf16)
        for c in range(3):
            project(n1, c)
            yield
        big = jnp.zeros((pair, 2 * pair), f32)
        for b, p in tiles:
            s = dot_nt(pick(p, b), stack_heads(pick(hp + p, b), low, zero))
            big = jnp.maximum(big, jnp.abs(s))
            sc[b * hp + p] = s
        yield
        for i in range(len(tiles)):
            ec[i] = jnp.exp(sc[i] + bias).astype(bf16)
        yield
        for b, p in tiles:
            attend(b, p, ec[b * hp + p])
        yield big

    def recheck(big):
        @pl.when(jnp.logical_not(jnp.max(big) < SAFE))
        def _():
            for b in range(seqs // 2):

                @pl.loop(0, hp)
                def _(p):
                    s = sc[b * hp + p] + bias
                    top0 = jnp.max(jnp.where(first_head, s, -2e30), -1, keepdims=True)
                    top1 = jnp.max(jnp.where(first_head, -2e30, s), -1, keepdims=True)
                    attend(b, p, jnp.exp(s - jnp.where(first_head, top0, top1)).astype(bf16))

    def forward():
        attended = jnp.concatenate(
            [jnp.concatenate([att[then, p, t * pitch : t * pitch + seqs] for p in range(hp)], 1) for t in range(tokens)], 0
        ).astype(bf16)
        mid = old_ref[...].astype(f32).reshape(rows, d) + dot(attended, wo_ref[...])
        at = pl.ds(pl.multiple_of((step - 1) * seqs, seqs), seqs)
        ms[at, :] = jnp.sum(mid.reshape(tokens, seqs, d), 0)
        n2 = (norm_parts(mid)[0] * gains_ref[1:2, :] + shifts_ref[1:2, :]).astype(bf16)
        yield
        chunk = ff // 2
        for c in range(0, ff, chunk):
            v = dot(n2, wup_ref[:, c : c + chunk])
            t = jnp.tanh(v * (GELU_C + (GELU_C * GELU_A) * (v * v)))
            h = (0.5 * v) * (1.0 + t)
            hs[at, c : c + chunk] = jnp.sum(h.reshape(tokens, seqs, chunk), 0)
            yield

    def run(*works):
        works, given = list(works), None
        while works:
            for w in list(works):
                try:
                    value = next(w)
                    given = given if value is None else value
                except StopIteration:
                    works.remove(w)
        return given

    @pl.when(step == 0)
    def _():
        recheck(run(attention()))

    @pl.when((step > 0) & (step < last))
    def _():
        recheck(run(attention(), forward()))

    @pl.when(step == last)
    def _():
        run(forward())
        hi, lo = split_bf16(hs[...] * (1.0 / tokens))
        u = ms[...] * (1.0 / tokens) + dot(hi, wdown_ref[...]) + dot(lo, wdown_ref[...])
        n = u.shape[0]
        out_ref[:n] = (u * lax.rsqrt(jnp.sum(u * u, -1, keepdims=True) + 1e-6)).astype(bf16)
        if out_ref.shape[0] > n:
            out_ref[n:] = count_rows(valid_ref, d)


def image_embed(xt, valid, gains, shifts, wqkv, wo, wup, wdown, start, count, note, seqs=16):
    tokens, _, d = xt.shape
    ff = wup.shape[1]
    pad = -(-tokens // 8) * 8
    pitch = seqs + PITCH
    tiles = seqs // 2 * (d // LANES)
    first, groups = start // seqs, count // seqs
    rows = count + (NOTE if note else 0)
    return pl.pallas_call(
        functools.partial(image_kernel, seqs),
        grid=(groups + 1,),
        in_specs=[
            pl.BlockSpec((tokens, seqs, d), lambda i: (0, jnp.minimum(i, groups - 1) + first, 0)),
            pl.BlockSpec((tokens, seqs, d), lambda i: (0, jnp.maximum(i - 1, 0) + first, 0)),
        ]
        + [whole(a) for a in (valid, gains, shifts, wqkv, wo, wup, wdown)],
        out_specs=pl.BlockSpec((rows, d), lambda i: (0, 0)),
        out_shape=jax.ShapeDtypeStruct((rows, d), bf16),
        scratch_shapes=[
            pltpu.VMEM((3 * d // LANES, pitch * pad, LANES), f32),
            pltpu.VMEM((2, d // LANES, pitch * pad, LANES), f32),
            pltpu.VMEM((tiles, 2 * pad, 4 * pad), f32),
            pltpu.VMEM((tiles, 2 * pad, 4 * pad), bf16),
            pltpu.VMEM((count, ff), f32),
            pltpu.VMEM((count, d), f32),
        ],
        compiler_params=params(),
        cost_estimate=cost(0.45 * count),
        name="image_block",
    )(xt, xt, valid, gains, shifts, wqkv, wo, wup, wdown)


def real_tokens(length, txt):
    seqs = length.shape[0]
    spread = jnp.broadcast_to(length[:, None, :], (seqs, txt, 1)).reshape(seqs * txt, 1)
    pos = lax.broadcasted_iota(jnp.int32, (seqs * txt, 1), 0) % txt
    return jnp.where(pos.astype(f32) < spread, 1.0, 0.0)


def text_forward_kernel(
    txt, held, x_ref, key_ref, flen_ref, gains_ref, shifts_ref, wqkv_ref, wo_ref, wup_ref, wdown_ref, *refs,
):
    (n1_ref, qkv_ref, probs_ref, att_ref, n2_ref, slope_ref, stat_ref, hpool_ref, u_ref, emb_ref, ms, sc, ec) = refs[held:]
    step = pl.program_id(0)
    rows, d = x_ref.shape
    ff = wup_ref.shape[1]
    seqs = rows // txt
    x = x_ref[...].astype(f32)
    xhat1, rstd1 = norm_parts(x)
    n1 = (xhat1 * gains_ref[0:1, :] + shifts_ref[0:1, :]).astype(bf16)
    n1_ref[...] = n1
    qkv_ref[:, :d] = (dot(n1, wqkv_ref[:, :d]) * HEAD**-0.5).astype(bf16)
    qkv_ref[:, d:] = dot(n1, wqkv_ref[:, d:]).astype(bf16)
    low = lax.broadcasted_iota(jnp.int32, (LANES, LANES), 1) < HEAD
    same = (
        lax.broadcasted_iota(jnp.int32, (LANES, LANES), 0) // txt
        == lax.broadcasted_iota(jnp.int32, (LANES, LANES), 1) // txt
    )
    zero = jnp.zeros((LANES, LANES), bf16)
    hp = d // LANES
    tiles = [(g, p) for g in range(rows // LANES) for p in range(hp)]

    def attend(g, p, probs):
        r = slice(g * LANES, (g + 1) * LANES)
        probs_ref[g * hp + p] = probs
        v = qkv_ref[r, 2 * d + p * LANES : 2 * d + (p + 1) * LANES]
        att_ref[r, p * LANES : (p + 1) * LANES] = dot(probs, stack_heads(v, low, zero)).astype(bf16)

    def share(s, top):
        halves = []
        for h in range(2):
            sh = s[:, h * LANES : (h + 1) * LANES]
            e = jnp.exp(sh - jnp.max(sh, -1, keepdims=True)) if top else jnp.exp(sh)
            halves.append(e / jnp.sum(e, -1, keepdims=True))
        return jnp.concatenate(halves, 1).astype(bf16)

    big = jnp.zeros((LANES, 2 * LANES), f32)
    for g, p in tiles:
        r = slice(g * LANES, (g + 1) * LANES)
        bias = jnp.where(same & (key_ref[0, g : g + 1, :] > 0), 0.0, -1e30)
        q = qkv_ref[r, p * LANES : (p + 1) * LANES]
        k = qkv_ref[r, d + p * LANES : d + (p + 1) * LANES]
        s = dot_nt(q, stack_heads(k, low, zero))
        big = jnp.maximum(big, jnp.abs(s))
        sc[g * hp + p] = s + jnp.concatenate([bias, bias], 1)
    for g, p in tiles:
        ec[g * hp + p] = share(sc[g * hp + p], False)
    for g, p in tiles:
        attend(g, p, ec[g * hp + p])

    @pl.when(jnp.logical_not(jnp.max(big) < SAFE))
    def _():
        for g, p in tiles:
            attend(g, p, share(sc[g * hp + p], True))

    mid = x + dot(att_ref[...], wo_ref[...])
    xhat2, rstd2 = norm_parts(mid)
    lane = lax.broadcasted_iota(jnp.int32, (rows, LANES), 1)
    hi1, hi2 = rstd1.astype(bf16).astype(f32), rstd2.astype(bf16).astype(f32)
    stat = jnp.where(lane < 64, jnp.where(lane < 32, hi1, rstd1 - hi1), jnp.where(lane < 96, hi2, rstd2 - hi2))
    stat_ref[...] = stat.astype(bf16)
    at = pl.ds(pl.multiple_of(step * seqs, seqs), seqs)
    keep = real_tokens(flen_ref[at, :], txt)
    n2 = ((xhat2 * gains_ref[1:2, :] + shifts_ref[1:2, :]) * keep).astype(bf16)
    n2_ref[...] = n2
    ms[at, :] = jnp.sum((mid * keep).reshape(seqs, txt, d), 1)
    chunk = 512
    for c in range(0, ff, chunk):
        v = dot(n2, wup_ref[:, c : c + chunk])
        v2 = v * v
        t = jnp.tanh(v * (GELU_C + (GELU_C * GELU_A) * v2))
        half = 0.5 + 0.5 * t
        h = v * half
        slope = half + h * (1.0 - t) * (GELU_C + (3.0 * GELU_C * GELU_A) * v2)
        slope_ref[:, c : c + chunk] = (slope * keep).astype(bf16)
        hpool_ref[at, c : c + chunk] = jnp.sum(h.reshape(seqs, txt, chunk), 1)

    @pl.when(step == pl.num_programs(0) - 1)
    def _():
        hi, lo = split_bf16(hpool_ref[...])
        pooled = ms[...] + dot(hi, wdown_ref[...]) + dot(lo, wdown_ref[...])
        u = pooled / flen_ref[...]
        u_ref[...] = u
        emb_ref[...] = (u * lax.rsqrt(jnp.sum(u * u, -1, keepdims=True) + 1e-6)).astype(bf16)


def text_forward(piece, pieces, held, x, key_ok, flen, gains, shifts, wqkv, wo, wup, wdown, txt, rows=512):
    total, d = x.shape
    ff = wup.shape[1]
    pairs = total // txt
    hp = d // LANES
    part = pairs // pieces
    steps = total // pieces // rows
    first = piece * steps
    block = lambda *tail: pl.BlockSpec((rows,) + tail, lambda i: (i + first,) + (0,) * len(tail))
    still = lambda *shape: pl.BlockSpec(shape, lambda i: (piece, 0))
    shape = jax.ShapeDtypeStruct
    key3 = key_ok.reshape(total // rows, rows // LANES, LANES)
    args = (x, key3, flen, gains, shifts, wqkv, wo, wup, wdown)
    return pl.pallas_call(
        functools.partial(text_forward_kernel, txt, len(held)),
        grid=(steps,),
        in_specs=[
            block(d), pl.BlockSpec((1, rows // LANES, LANES), lambda i: (i + first, 0, 0)), still(part, 1)
        ]
        + [whole(a) for a in args[3:]]
        + [pl.BlockSpec(memory_space=pl.ANY)] * len(held),
        out_specs=[
            block(d), block(3 * d), pl.BlockSpec((rows // LANES * hp, LANES, 2 * LANES), lambda i: (i + first, 0, 0)),
            block(d), block(d), block(ff), block(LANES), still(part, ff), still(part, d), still(part, d),
        ],
        out_shape=[
            shape((total, d), bf16), shape((total, 3 * d), bf16), shape((total // LANES * hp, LANES, 2 * LANES), bf16),
            shape((total, d), bf16), shape((total, d), bf16), shape((total, ff), bf16), shape((total, LANES), bf16),
            shape((pairs, ff), f32), shape((pairs, d), f32), shape((pairs, d), bf16),
        ],
        input_output_aliases={len(args) + i: i for i in range(len(held))},
        scratch_shapes=[
            pltpu.VMEM((part, d), f32),
            pltpu.VMEM((rows // LANES * hp, LANES, 2 * LANES), f32),
            pltpu.VMEM((rows // LANES * hp, LANES, 2 * LANES), bf16),
        ],
        compiler_params=params(30 * 1024 * 1024),
        cost_estimate=cost(0.013 * total / pieces),
        name="text_forward",
    )(*args, *held)


def scores_kernel(
    group, place_ref, own_ref, other_ref, own_valid_ref, other_valid_ref, scale_ref, a0_ref, a1_ref,
    s_ref, all_ref, col_out, okay_out, row_out,
):
    step = pl.program_id(0)
    pairs = own_ref.shape[0]
    scale = scale_ref[0]
    row = lax.broadcasted_iota(jnp.int32, (pairs, 1), 0).astype(f32)
    mask = [jnp.where(row < jnp.sum(v[...], 1, keepdims=True), 1.0, 0.0) for v in (own_valid_ref, other_valid_ref)]
    mask = jnp.concatenate(mask, 0)
    inner = lax.rem(place_ref[0], group)
    late = lax.bitwise_xor(step, lax.div(place_ref[0], group)) >= pl.num_programs(0) // 2
    texts = jnp.concatenate([own_ref[...], other_ref[...]], 0)

    @pl.when(step == 0)
    def _():
        row_out[...] = jnp.zeros_like(row_out)
        row_out[:, 3:4] = mask

    lane = lax.broadcasted_iota(jnp.int32, (1, pairs), 1).astype(f32)
    for k in range(group):
        at = lax.bitwise_xor(k, inner)
        cols = slice(k * pairs, (k + 1) * pairs)
        a = jnp.where(late, a1_ref[at], a0_ref[at])
        images = a[:pairs]
        count = a[pairs : pairs + 1, 0:1].astype(f32)
        okay = jnp.where(lane < count, 1.0, 0.0)
        okay_out[0:1, cols] = okay
        all_ref[cols, :] = images
        s = scale * dot_nt(texts, images)
        s_ref[:, cols] = s
        up = jnp.exp(s - SHIFT)
        down = jnp.exp(jnp.minimum(s, 0.0) + SHIFT)
        col_out[0:1, cols] = jnp.sum(up * mask, 0, keepdims=True)
        col_out[1:2, cols] = jnp.sum(down * mask, 0, keepdims=True)
        row_out[:, 0:1] += jnp.sum(up * okay, 1, keepdims=True)
        row_out[:, 1:2] += jnp.sum(down * okay, 1, keepdims=True)
        row_out[:, 2:3] += jnp.broadcast_to(count, (2 * pairs, 1))


def pair_scores(place, own, other, own_valid, other_valid, scale, a0, a1):
    slots, _, d = a0.shape
    pairs = own.shape[0]
    group = min(8, slots)
    groups = slots // group
    cols = group * pairs
    keep = lambda *_: (0, 0)
    turn = lambda i, s: (lax.rem(lax.bitwise_xor(i, lax.div(s[0], group)), groups), 0, 0)
    still = lambda a: pl.BlockSpec(a.shape, keep)
    shape = jax.ShapeDtypeStruct
    return pl.pallas_call(
        functools.partial(scores_kernel, group),
        grid_spec=pltpu.PrefetchScalarGridSpec(
            num_scalar_prefetch=1,
            grid=(2 * groups,),
            in_specs=[still(own), still(other), still(own_valid), still(other_valid), pl.BlockSpec(memory_space=pltpu.SMEM)]
            + [pl.BlockSpec((group,) + a.shape[1:], turn) for a in (a0, a1)],
            out_specs=[
                pl.BlockSpec((2 * pairs, cols), lambda i, s: (0, i)),
                pl.BlockSpec((cols, d), lambda i, s: (i, 0)),
                pl.BlockSpec((2, cols), lambda i, s: (0, i)),
                pl.BlockSpec((1, cols), lambda i, s: (0, i)),
                pl.BlockSpec((2 * pairs, 4), keep),
            ],
        ),
        out_shape=[
            shape((2 * pairs, 2 * groups * cols), f32), shape((2 * groups * cols, d), bf16),
            shape((2, 2 * groups * cols), f32), shape((1, 2 * groups * cols), f32), shape((2 * pairs, 4), f32),
        ],
        compiler_params=params(2 * HOP_VMEM),
        cost_estimate=cost(4.0),
        name="pair_scores",
    )(place, own, other, own_valid, other_valid, scale, a0, a1)


def log_sum(up, down):
    fine = up >= 1.9287498479639178e-22
    return jnp.where(
        fine, jnp.log(jnp.where(fine, up, 1.0)) + SHIFT, jnp.log(jnp.where(fine, 1.0, down)) - SHIFT
    )


def gradient_kernel(
    dp, scale_ref, s_ref, all_ref, col_ref, got_ref, okay_ref, row_ref, swap_ref, text_ref, a_ref,
    grad_ref, back_ref, loss_ref,
):
    step = pl.program_id(0)
    pairs = text_ref.shape[0]
    row = row_ref[...] + jnp.concatenate([swap_ref[pairs:], swap_ref[:pairs]], 0)
    factor = 0.5 / row[0:1, 2:3]
    mask = row_ref[:, 3:4]
    okay = okay_ref[...]
    row_lse = log_sum(row[:, 0:1], row[:, 1:2])
    col = col_ref[...] + got_ref[...]
    col_lse = log_sum(col[0:1, :], col[1:2, :])

    @pl.when(step == 0)
    def _():
        grad_ref[...] = jnp.zeros_like(grad_ref)
        back_ref[...] = jnp.zeros_like(back_ref)
        loss_ref[...] = jnp.zeros_like(loss_ref)
        t = text_ref[...].astype(f32) * a_ref[:pairs].astype(f32)
        diag = scale_ref[0] * jnp.sum(t, -1, keepdims=True)
        m = mask[:pairs]
        loss_ref[0:1, 0:1] = factor * jnp.sum(m * (row_lse[:pairs] - 2.0 * diag), 0, keepdims=True)
        loss_ref[1:2, 0:1] = -2.0 * factor * jnp.sum(m * diag, 0, keepdims=True)

    s = s_ref[...]
    g = jnp.exp(jnp.minimum(s - row_lse, 1.0)) + jnp.exp(jnp.minimum(s - col_lse, 1.0))
    g = g * ((factor * mask) * okay)
    grad = dot(g.astype(bf16), all_ref[...])
    grad_ref[...] += grad[:pairs]
    back_ref[...] += grad[pairs:]
    cols = jnp.sum(jnp.where(okay > 0, col_lse, 0.0), 1, keepdims=True)
    loss_ref[0:1, 0:1] += factor * (cols * (1.0 / dp))
    loss_ref[1:2, 0:1] += jnp.sum(jnp.sum(g * s, 0, keepdims=True), 1, keepdims=True)


def pair_gradients(dp, scale, scores, images, col, got, okay, row, swap, texts, a):
    pairs, d = texts.shape
    cols = min(8, dp) * pairs
    still = lambda *shape: pl.BlockSpec(shape, lambda i: (0, 0))
    shape = jax.ShapeDtypeStruct
    return pl.pallas_call(
        functools.partial(gradient_kernel, dp),
        grid=(dp * pairs // cols,),
        in_specs=[
            pl.BlockSpec(memory_space=pltpu.SMEM),
            pl.BlockSpec((2 * pairs, cols), lambda i: (0, i)),
            pl.BlockSpec((cols, d), lambda i: (i, 0)),
            pl.BlockSpec((2, cols), lambda i: (0, i)),
            pl.BlockSpec((2, cols), lambda i: (0, i)),
            pl.BlockSpec((1, cols), lambda i: (0, i)),
        ]
        + [whole(x) for x in (row, swap, texts, a)],
        out_specs=[still(pairs, d), still(pairs, d), still(8, LANES)],
        out_shape=[shape((pairs, d), f32), shape((pairs, d), f32), shape((8, LANES), f32)],
        compiler_params=params(2 * HOP_VMEM),
        cost_estimate=cost(3.0),
        name="pair_gradients",
    )(scale, scores, images, col, got, okay, row, swap, texts, a)


def spread_rows(a, txt):
    seqs, width = a.shape
    return jnp.broadcast_to(a[:, None, :], (seqs, txt, width)).reshape(seqs * txt, width)


def backward_up_kernel(
    txt, scale_ref, rep_ref, part_ref, back_ref, row_ref, swap_ref, a_ref, u_ref, len_ref, hpool_ref, n2_ref, slope_ref,
    wdown_ref, send_ref, keep_ref, gd_ref, dh_ref, down, acc,
):
    step = pl.program_id(0)
    rows, d = n2_ref.shape
    ff = slope_ref.shape[1]
    seqs = rows // txt

    @pl.when(step == 0)
    def _():
        pairs = part_ref.shape[0]
        scale = scale_ref[0]
        factor = 0.5 / (row_ref[0:1, 2:3] + swap_ref[0:1, 2:3])
        images = a_ref[:pairs].astype(f32)
        u = u_ref[...]
        r = lax.rsqrt(jnp.sum(u * u, -1, keepdims=True) + 1e-6)
        g = scale * (part_ref[...] + back_ref[...]) - (2.0 * scale) * (factor * row_ref[:pairs, 3:4]) * images
        du = (r * g - (r * r * r) * u * jnp.sum(u * g, -1, keepdims=True)) / len_ref[...]
        gd_ref[...] = du
        low = du.astype(bf16)
        dh_ref[...] = dot_nt(low, wdown_ref[...])
        hi, lo = split_bf16(hpool_ref[...])
        down[...] = (dot_tn(hi, low) + dot_tn(lo, low)).astype(bf16)
        acc[...] = jnp.zeros_like(acc)

    at = pl.ds(pl.multiple_of(step * seqs, seqs), seqs)
    chunk = 512
    for c in range(0, ff, chunk):
        cs = slice(c, c + chunk)
        grad_before = (spread_rows(dh_ref[at, cs], txt) * slope_ref[:, cs].astype(f32)).astype(bf16)
        acc[:, cs] += dot_tn(n2_ref[...], grad_before)

    @pl.when(step == pl.num_programs(0) - 1)
    def _():
        first = rep_ref[0] == 0
        for b in range(ff // d):
            r = slice(b * d, (b + 1) * d)
            up = acc[:, r].astype(bf16)
            keep_ref[r] = jnp.where(first, down[r], up)
            send_ref[r] = jnp.where(first, up, down[r])


def backward_up(scale, rep, part, back, row, swap, a, u, flen, hpool, n2, slope, wdown, txt, rows=512):
    tokens, d = n2.shape
    pairs, ff = hpool.shape
    block = lambda w: pl.BlockSpec((rows, w), lambda i: (i, 0))
    shape = jax.ShapeDtypeStruct
    smem = pl.BlockSpec(memory_space=pltpu.SMEM)
    outs = [shape((ff, d), bf16), shape((ff, d), bf16), shape((pairs, d), f32), shape((pairs, ff), f32)]
    return pl.pallas_call(
        functools.partial(backward_up_kernel, txt),
        grid=(tokens // rows,),
        in_specs=[smem, smem]
        + [whole(x) for x in (part, back, row, swap, a, u, flen, hpool)]
        + [block(d), block(ff), whole(wdown)],
        out_specs=[whole(x) for x in outs],
        out_shape=outs,
        scratch_shapes=[pltpu.VMEM((ff, d), bf16), pltpu.VMEM((d, ff), f32)],
        compiler_params=params(30 * 1024 * 1024),
        cost_estimate=cost(0.006 * tokens),
        name="backward_up",
    )(scale, rep, part, back, row, swap, a, u, flen, hpool, n2, slope, wdown)


def backward_middle_kernel(
    txt, gd_ref, dh_ref, len_ref, n2_ref, slope_ref, stat_ref, att_ref, gains_ref, shifts_ref, wup_ref, wo_ref,
    gmid_ref, datt_ref, dwo_ref, gain_ref, acc,
):
    step = pl.program_id(0)
    rows, d = n2_ref.shape
    ff = wup_ref.shape[1]

    @pl.when(step == 0)
    def _():
        acc[...] = jnp.zeros_like(acc)
        gain_ref[...] = jnp.zeros_like(gain_ref)

    dn2 = jnp.zeros((rows, d), f32)
    chunk = 512
    for c in range(0, ff, chunk):
        cs = slice(c, c + chunk)
        grad_before = (spread_rows(dh_ref[:, cs], txt) * slope_ref[:, cs].astype(f32)).astype(bf16)
        dn2 += dot_nt(grad_before, wup_ref[:, cs])
    xhat = (n2_ref[...].astype(f32) - shifts_ref[1:2, :]) / gains_ref[1:2, :]
    stat = stat_ref[...].astype(f32)
    gain_ref[0:1, :] += jnp.sum(dn2 * xhat, 0, keepdims=True)
    gain_ref[1:2, :] += jnp.sum(dn2, 0, keepdims=True)
    gn = dn2 * gains_ref[1:2, :]
    dmid = (stat[:, 64:65] + stat[:, 96:97]) * (
        gn - jnp.mean(gn, -1, keepdims=True) - xhat * jnp.mean(gn * xhat, -1, keepdims=True)
    )
    gmid = spread_rows(gd_ref[...], txt) * real_tokens(len_ref[...], txt) + dmid
    gmid_ref[...] = gmid
    branch = gmid.astype(bf16)
    acc[...] += dot_tn(att_ref[...], branch)
    datt_ref[...] = dot_nt(branch, wo_ref[...]).astype(bf16)

    @pl.when(step == pl.num_programs(0) - 1)
    def _():
        dwo_ref[...] = acc[...].astype(bf16)


def backward_middle(gd, dh, flen, n2, slope, stat, att, gains, shifts, wup, wo, txt, rows=512):
    tokens, d = n2.shape
    ff = wup.shape[1]
    block = lambda w: pl.BlockSpec((rows, w), lambda i: (i, 0))
    lead = lambda w: pl.BlockSpec((rows // txt, w), lambda i: (i, 0))
    shape = jax.ShapeDtypeStruct
    sums = [shape((d, d), bf16), shape((8, d), f32)]
    return pl.pallas_call(
        functools.partial(backward_middle_kernel, txt),
        grid=(tokens // rows,),
        in_specs=[lead(d), lead(ff), lead(1), block(d), block(ff), block(LANES), block(d)]
        + [whole(x) for x in (gains, shifts, wup, wo)],
        out_specs=[block(d), block(d)] + [whole(x) for x in sums],
        out_shape=[shape((tokens, d), f32), shape((tokens, d), bf16)] + sums,
        scratch_shapes=[pltpu.VMEM((d, d), f32)],
        compiler_params=params(30 * 1024 * 1024),
        cost_estimate=cost(0.006 * tokens),
        name="backward_middle",
    )(gd, dh, flen, n2, slope, stat, att, gains, shifts, wup, wo)


def backward_attention_kernel(
    held, last, rep_ref, datt_ref, qkv_ref, probs_ref, n1_ref, dwo_ref, gain2_ref, sums_ref, gains_ref, shifts_ref, wqkv_ref,
    *refs
):
    old_acc, old_flat = refs[1:3] if held else (None, None)
    gq_ref, *outs = refs[held:-4]
    acc, flat, sc, ec = refs[-4:]
    step = pl.program_id(0)
    rows, d = n1_ref.shape
    low = lax.broadcasted_iota(jnp.int32, (LANES, LANES), 1) < HEAD
    zero = jnp.zeros((LANES, LANES), bf16)

    @pl.when(step == 0)
    def _():
        acc[...] = old_acc[...] if held else jnp.zeros_like(acc)
        flat[...] = old_flat[...] if held else jnp.zeros_like(flat)

    hp = d // LANES
    tiles = [(g, p) for g in range(rows // LANES) for p in range(hp)]
    at = lambda g, p, part: (slice(g * LANES, (g + 1) * LANES), slice(part * d + p * LANES, part * d + (p + 1) * LANES))
    for g, p in tiles:
        sc[g * hp + p] = dot_nt(datt_ref[at(g, p, 0)], stack_heads(qkv_ref[at(g, p, 2)], low, zero))
    for g, p in tiles:
        i = g * hp + p
        probs = probs_ref[i].astype(f32)
        halves = []
        for h in range(2):
            hs = slice(h * LANES, (h + 1) * LANES)
            ph, dh = probs[:, hs], sc[i, :, hs]
            halves.append(ph * (dh - jnp.sum(ph * dh, -1, keepdims=True)))
        ec[i] = jnp.concatenate(halves, 1).astype(bf16)
    for g, p in tiles:
        dv = dot_tn(probs_ref[g * hp + p], datt_ref[at(g, p, 0)])
        gq_ref[at(g, p, 2)] = jnp.where(low, dv[:LANES], dv[LANES:]).astype(bf16)
    for g, p in tiles:
        keys = stack_heads(qkv_ref[at(g, p, 1)], low, zero)
        gq_ref[at(g, p, 0)] = (dot(ec[g * hp + p], keys) * HEAD**-0.5).astype(bf16)
    for g, p in tiles:
        dk = dot_tn(ec[g * hp + p], qkv_ref[at(g, p, 0)])
        gq_ref[at(g, p, 1)] = jnp.where(low, dk[:LANES], dk[LANES:]).astype(bf16)
    gq = gq_ref[...]
    acc[...] += dot_tn(n1_ref[...], gq)
    flat[0:1, :] += jnp.sum(gq.astype(f32), 0, keepdims=True)

    @pl.when(step == pl.num_programs(0) - 1)
    def _():
        if not last:
            outs[0][...] = acc[...]
            outs[1][...] = flat[...]
            return
        send_ref, keep_ref, small_ref = outs
        w = wqkv_ref[...]
        ones = jnp.ones((8, 3 * d), bf16)
        hi, lo = split_bf16(acc[...] * w.astype(f32))
        spread = dot_nt(ones, hi) + dot_nt(ones, lo)
        hi, lo = split_bf16(flat[...])
        dshift = (dot_nt(hi, w) + dot_nt(lo, w))[0:1]
        dgain = (spread[0:1] - shifts_ref[0:1, :] * dshift) / gains_ref[0:1, :]
        small = [dgain, gain2_ref[0:1, :], dshift, gain2_ref[1:2, :]]
        small += [jnp.broadcast_to(sums_ref[i : i + 1, 0:1], (1, d)) for i in range(2)]
        small = jnp.concatenate(small + [jnp.zeros((2, d), f32)], 0)
        small_ref[...] = small
        first = rep_ref[0] == 0
        parts = [acc[:, b * d : (b + 1) * d].astype(bf16) for b in range(3)] + [dwo_ref[...]]
        for b in range(2):
            keep_ref[b * d : (b + 1) * d] = jnp.where(first, parts[b], parts[b + 2])
            send_ref[b * d : (b + 1) * d] = jnp.where(first, parts[b + 2], parts[b])
        put_small(send_ref, 2 * d, small)


def backward_attention(piece, pieces, held, rep, datt, qkv, probs, n1, dwo, gain2, sums, gains, shifts, wqkv, rows=512):
    tokens, d = n1.shape
    steps = tokens // pieces // rows
    first = piece * steps
    last = piece == pieces - 1
    block = lambda w: pl.BlockSpec((rows, w), lambda i: (i + first, 0))
    shape = jax.ShapeDtypeStruct
    if last:
        outs = [shape((2 * d + NOTE, d), bf16), shape((2 * d, d), bf16), shape((8, d), f32)]
    else:
        outs = [shape((d, 3 * d), f32), shape((8, 3 * d), f32)]
    args = (rep, datt, qkv, probs, n1, dwo, gain2, sums, gains, shifts, wqkv)
    return pl.pallas_call(
        functools.partial(backward_attention_kernel, len(held), last),
        grid=(steps,),
        in_specs=[
            pl.BlockSpec(memory_space=pltpu.SMEM), block(d), block(3 * d),
            pl.BlockSpec((rows // LANES * (d // LANES), LANES, 2 * LANES), lambda i: (i + first, 0, 0)),
            block(d),
        ]
        + [whole(x) for x in args[5:]]
        + ([pl.BlockSpec(memory_space=pl.ANY)] + [whole(x) for x in held[1:]] if held else []),
        out_specs=[block(3 * d)] + [whole(x) for x in outs],
        out_shape=[shape((tokens, 3 * d), bf16)] + outs,
        input_output_aliases={len(args): 0} if held else {},
        scratch_shapes=[
            pltpu.VMEM((d, 3 * d), f32),
            pltpu.VMEM((8, 3 * d), f32),
            pltpu.VMEM((rows // LANES * (d // LANES), LANES, 2 * LANES), f32),
            pltpu.VMEM((rows // LANES * (d // LANES), LANES, 2 * LANES), bf16),
        ],
        compiler_params=params(30 * 1024 * 1024),
        cost_estimate=cost(0.009 * tokens / pieces),
        name="backward_attention",
    )(*args, *held)


def backward_input_kernel(gq_ref, gmid_ref, n1_ref, stat_ref, gains_ref, shifts_ref, wqkv_ref, *refs):
    dx_ref = refs[-1]
    gn = dot_nt(gq_ref[...], wqkv_ref[...]) * gains_ref[0:1, :]
    xhat = (n1_ref[...].astype(f32) - shifts_ref[0:1, :]) / gains_ref[0:1, :]
    stat = stat_ref[...].astype(f32)
    dx_ref[...] = gmid_ref[...] + (stat[:, 0:1] + stat[:, 32:33]) * (
        gn - jnp.mean(gn, -1, keepdims=True) - xhat * jnp.mean(gn * xhat, -1, keepdims=True)
    )


def backward_input(piece, pieces, held, gq, gmid, n1, stat, gains, shifts, wqkv, rows=512):
    tokens, d = gmid.shape
    steps = tokens // pieces // rows
    block = lambda w: pl.BlockSpec((rows, w), lambda i: (i + piece * steps, 0))
    args = (gq, gmid, n1, stat, gains, shifts, wqkv)
    return pl.pallas_call(
        backward_input_kernel,
        grid=(steps,),
        in_specs=[block(3 * d), block(d), block(d), block(LANES), whole(gains), whole(shifts), whole(wqkv)]
        + [pl.BlockSpec(memory_space=pl.ANY)] * len(held),
        out_specs=block(d),
        out_shape=jax.ShapeDtypeStruct((tokens, d), f32),
        input_output_aliases={len(args): 0} if held else {},
        compiler_params=params(2 * HOP_VMEM),
        cost_estimate=cost(0.004 * tokens / pieces),
        name="backward_input",
    )(*args, *held)


def finish_kernel(places, rep_ref, own_ref, got_ref, *out_refs):
    first = rep_ref[0] == 0
    for out, top, left, begin, n, part in places:
        a = own_ref[begin : begin + n, :]
        b = got_ref[begin : begin + n, :]
        mine = first if part == 0 else jnp.logical_not(first)
        out_refs[out][top : top + n, left : left + a.shape[1]] = jnp.where(mine, a, b).astype(f32)


def finish(rep, own, got, shapes, segments):
    half = own.shape[0]
    places = []
    for row, count, out, top, left in segments:
        while count:
            part, begin = divmod(row, half)
            n = min(count, half - begin)
            places.append((out, top, left, begin, n, part))
            row, top, count = row + n, top + n, count - n
    outs = [jax.ShapeDtypeStruct(s, f32) for s in shapes]
    return pl.pallas_call(
        functools.partial(finish_kernel, places),
        grid=(1,),
        in_specs=[pl.BlockSpec(memory_space=pltpu.SMEM), whole(own), whole(got)],
        out_specs=[whole(x) for x in outs],
        out_shape=outs,
        compiler_params=params(2 * HOP_VMEM),
        cost_estimate=cost(3.0),
        name="finish",
    )(rep, own, got)


class Links:
    def __init__(self, mesh):
        self.dp, self.rep = mesh.shape["dp"], mesh.shape["rep"]
        self.bits = (self.dp - 1).bit_length()
        assert self.dp == 1 << self.bits and self.rep == 2
        near, far = list(range(min(2, self.bits))), list(range(2, self.bits))
        turn = lambda bits: list(zip(bits, bits[::-1]))
        self.near, self.far = turn(near), turn(far)
        self.gather_order = [(b, b) for b in far[::-1]] + self.near

    def bit(self, pair):
        place = lax.axis_index("dp")
        return jnp.where(lax.axis_index("rep") == 0, (place >> pair[0]) & 1, (place >> pair[1]) & 1)

    def across(self, x, pair):
        moves = [(2 * i + r, 2 * (i ^ (1 << pair[r])) + r) for i in range(self.dp) for r in range(2)]
        return lax.ppermute(x, ("dp", "rep"), moves)

    def core(self, x):
        return lax.ppermute(x, "rep", [(0, 1), (1, 0)])


def put_small(ref, at, small):
    hi, lo = split_bf16(small)
    ref[at : at + NOTE] = jnp.concatenate([hi, lo], 0)


def hop_kernel(kind, late, with_small, v_ref, x_ref, got_ref, *refs):
    n, d = x_ref.shape
    refs = list(refs)
    small_ref = refs.pop(0) if with_small else None
    low = v_ref[0] == 0
    if kind == "join":
        x, got = x_ref[...], got_ref[...]
        refs[0][:n] = jnp.where(low, x, got)
        refs[0][n:] = jnp.where(low, got, x)
        return
    add = lambda r: (x_ref[r].astype(f32) + got_ref[r].astype(f32)).astype(bf16)
    send_ref, keep_ref = refs[0], refs[1]
    if late == "half":
        m = n // 2
        a, b = add(slice(0, m)), add(slice(m, n))
        keep_ref[...] = jnp.where(low, a, b)
        send_ref[:m] = jnp.where(low, b, a)
    else:
        m = n
        x = add(slice(0, n))
        keep_ref[...] = x
        if late == "full":
            send_ref[:m] = x
    if with_small:
        hi, lo = got_ref[n : n + NOTE // 2], got_ref[n + NOTE // 2 :]
        small = small_ref[...] + (hi.astype(f32) + lo.astype(f32))
        refs[2][...] = small
        if send_ref.shape[0] > m:
            put_small(send_ref, m, small)


class Reduction:
    def __init__(self, links, send, keep, small=None):
        self.kind = None
        self.links, self.send, self.x, self.small = links, send, keep, small
        self.plan = (
            [("core", None)]
            + [("half", p) for p in links.near]
            + [("full", p) for p in links.far]
            + [("join", p) for p in links.near[::-1]]
            + [("last", None)]
        )

    def start(self, *after):
        links = self.links
        self.kind, self.pair = self.plan.pop(0)
        if after:
            self.send, *after = beside(self.send, *after)
        self.got = links.core(self.send) if self.pair is None else links.across(self.send, self.pair)
        return after

    def end(self):
        kind, x, links = self.kind, self.x, self.links
        if kind == "last":
            return
        n, d = x.shape
        shape = jax.ShapeDtypeStruct
        late, pair = self.plan[0]
        if kind == "join":
            v, outs = links.signs[self.pair], [shape((2 * n, d), bf16)]
        else:
            v = links.signs[pair] if late == "half" else links.any
            m = n // 2 if late == "half" else n
            more = NOTE if self.small is not None and late in ("half", "full") else 0
            outs = [shape((m + more if late in ("half", "full") else NOTE, d), bf16), shape((m, d), bf16)]
        args = [v, x, self.got]
        with_small = self.small is not None and kind != "join"
        if with_small:
            args.append(self.small)
            outs.append(shape(self.small.shape, f32))
        out = pl.pallas_call(
            functools.partial(hop_kernel, kind, late, with_small),
            in_specs=[pl.BlockSpec(memory_space=pltpu.SMEM)] + [pl.BlockSpec(memory_space=pltpu.VMEM)] * (len(args) - 1),
            out_specs=[pl.BlockSpec(memory_space=pltpu.VMEM)] * len(outs),
            out_shape=outs,
            compiler_params=params(HOP_VMEM),
            cost_estimate=cost(1.0),
            name="hop",
        )(*args)
        if kind == "join":
            self.send = self.x = out[0]
            return
        self.x = out[1]
        self.send = out[0] if late in ("half", "full") else self.x
        if with_small:
            self.small = out[2]


def beside(*values):
    return lax.optimization_barrier(values)


def body(
    links, image_in, img_gains, img_shifts, img_qkv, img_out, img_up, img_down, text_in, lengths, valid,
    txt_gains, txt_shifts, txt_qkv, txt_out, txt_up, txt_down, log_scale,
):
    dp, bits = links.dp, links.bits
    pairs, txt, d = text_in.shape
    ff = txt_up.shape[1]
    tokens = pairs * txt
    scale = jnp.exp(log_scale).reshape(1)
    rep = lax.axis_index("rep").astype(jnp.int32).reshape(1)
    order = links.gather_order

    own_valid = valid.astype(f32)[None, :]
    flen = lengths.astype(f32)[:, None]
    key_ok = (jnp.arange(txt)[None, :] < lengths[:, None]).astype(f32).reshape(tokens // LANES, LANES)

    xt = image_in.transpose(1, 0, 2)
    place = sum(links.bit(order[i]) << i for i in range(bits)).astype(jnp.int32).reshape(1)
    signs = [links.bit(pair).astype(jnp.int32).reshape(1) for pair in links.near]
    xt, flen, key_ok, own_valid, scale, rep, place, *signs = beside(
        xt, flen, key_ok, own_valid, scale, rep, place, *signs
    )
    links.signs = dict(zip(links.near, signs))
    links.any = rep
    other_valid = links.core(own_valid)
    image_args = (valid[None, :], img_gains, img_shifts, img_qkv, img_out, img_up, img_down)
    emb = image_embed(xt, *image_args, 0, pairs, True)
    text_args = (txt_gains, txt_shifts, txt_qkv, txt_out, txt_up, txt_down)
    text_x, emb = beside(text_in.reshape(tokens, d), emb)
    steps, pieces = list(order), 4
    a, held = emb[None], []
    for piece in range(pieces):
        if steps:
            got = links.across(a, steps.pop(0))
        held = list(text_forward(piece, pieces, held, text_x, key_ok, flen, *text_args, txt))
        if steps:
            text_x, got, held[-1] = beside(text_x, got, held[-1])
            a = jnp.concatenate([a, got], 0)
    while steps:
        got = links.across(a, steps.pop(0))
        if steps:
            a = jnp.concatenate([a, got], 0)
    n1, qkv, probs, att, n2, slope, stat, hpool, u, text_emb = held

    scores, images, col, okay, row = pair_scores(
        place, text_emb, links.core(text_emb), own_valid, other_valid, scale, a, got
    )
    swap = links.core(row)
    for pair in order[:-1]:
        col = col + links.across(col, pair)
    col_got = links.across(col, order[-1])
    part, other, sums = pair_gradients(dp, scale, scores, images, col, col_got, okay, row, swap, text_emb, emb)
    back = links.core(other)

    ffn_send, ffn_keep, gd, dh = backward_up(scale, rep, part, back, row, swap, emb, u, flen, hpool, n2, slope, txt_down, txt)
    first = Reduction(links, ffn_send, ffn_keep)
    first.start()
    gmid, datt, dwo, gain2 = backward_middle(
        gd, dh, flen, n2, slope, stat, att, txt_gains, txt_shifts, txt_up, txt_out, txt
    )
    held = []
    for piece in range(2):
        datt, first.got, *held = beside(datt, first.got, *held)
        first.end()
        first.start()
        held = list(backward_attention(
            piece, 2, held, rep, datt, qkv, probs, n1, dwo, gain2, sums, txt_gains, txt_shifts, txt_qkv
        ))
    gq, att_send, att_keep, small = held
    att_send, first.got = beside(att_send, first.got)
    second = Reduction(links, att_send, att_keep, small)
    dx, done = [], []

    def inputs(piece, stream):
        gq_now, stream.x = beside(gq, stream.x)
        dx[:] = [backward_input(piece, 2, dx, gq_now, gmid, n1, stat, txt_gains, txt_shifts, txt_qkv)]

    other = {first: second, second: first}
    far = len(links.far)
    for act, stream in (
        [("s", second), ("e", first), ("s", first), ("e", second), ("s", second), ("i", 0), ("e", second), ("s", second)]
        + [("e", first), ("s", first), ("e", second), ("s", second), ("i", 1), ("e", second), ("s", second)]
        + [("e", first), ("s", first), ("e", second), ("s", second), ("e", first), ("s", first)] * (far > 0)
    ):
        if act == "i":
            inputs(stream, second)
        elif act == "e":
            stream.end()
        elif stream.plan:
            if stream is second and second.kind is None:
                stream.start()
            else:
                other[stream].x, *dx[:] = stream.start(other[stream].x, *dx)
    while first.plan or second.plan:
        for stream in (second, first):
            if stream.plan:
                stream.end()
                stream.start()
    grad_down, grad_up = finish(
        rep, first.x, first.got, [(ff, d), (d, ff)], [(0, ff, 0, 0, 0)] + [(ff + i * d, d, 1, 0, i * d) for i in range(ff // d)]
    )
    grad_qkv, grad_out = finish(
        rep, second.x, second.got, [(d, 3 * d), (d, d)], [(i * d, d, 0, 0, i * d) for i in range(3)] + [(3 * d, d, 1, 0, 0)]
    )
    small, dx = second.small, dx[0]
    return (
        small[4, 0],
        small[0:2],
        small[2:4],
        grad_qkv,
        grad_out,
        grad_up,
        grad_down,
        small[5, 0],
        dx.reshape(pairs, txt, d),
    )


def solution(mesh):
    both = ("dp", "rep")
    deep = P(both, None, None)
    in_specs = (deep,) + (P(),) * 6 + (deep, P(both), P(both)) + (P(),) * 7
    out_specs = (P(),) * 8 + (deep,)
    return jax.shard_map(
        functools.partial(body, Links(mesh)), mesh=mesh, in_specs=in_specs, out_specs=out_specs, check_vma=False
    )
```

```python
import functools
import jax
import jax.numpy as jnp
from jax import lax
from jax.experimental import pallas as pl
from jax.experimental.pallas import tpu as pltpu
from jax.sharding import PartitionSpec as P

HEAD = 64
LANES = 128
f32 = jnp.float32
bf16 = jnp.bfloat16
GELU_C = 0.7978845608028654
GELU_A = 0.044715
SHIFT = 50.0
SAFE = 80.0
NOTE = 16
PITCH = 8
VMEM = 60 * 1024 * 1024
HOP_VMEM = 12 * 1024 * 1024


def dot(a, b):
    return jnp.dot(a, b, preferred_element_type=f32)


def dot_nt(a, b):
    return lax.dot_general(a, b, (((1,), (1,)), ((), ())), preferred_element_type=f32)


def dot_tn(a, b):
    return lax.dot_general(a, b, (((0,), (0,)), ((), ())), preferred_element_type=f32)


def norm_parts(x):
    mu = jnp.mean(x, -1, keepdims=True)
    c = x - mu
    rstd = lax.rsqrt(jnp.mean(c * c, -1, keepdims=True) + 1e-6)
    return c * rstd, rstd


def whole(a):
    return pl.BlockSpec(a.shape, lambda *_: (0,) * a.ndim)


def params(limit=VMEM):
    return pltpu.CompilerParams(vmem_limit_bytes=limit)


def cost(us):
    return pl.CostEstimate(flops=int(us * 1.1e9), bytes_accessed=0, transcendentals=0)


def split_bf16(v):
    hi = v.astype(bf16)
    return hi, (v - hi.astype(f32)).astype(bf16)


def count_rows(valid_ref, d):
    count = jnp.sum(valid_ref[...].astype(f32), 1, keepdims=True)
    return jnp.broadcast_to(count, (NOTE, d)).astype(bf16)


def stack_heads(a, low, zero):
    return jnp.concatenate([jnp.where(low, a, zero), jnp.where(low, zero, a)], 0)


def image_kernel(
    seqs, x_ref, old_ref, valid_ref, gains_ref, shifts_ref, wqkv_ref, wo_ref, wup_ref, wdown_ref, out_ref,
    qkv, att, sc, ec, hs, ms,
):
    tokens, _, d = x_ref.shape
    pad = -(-tokens // 8) * 8
    pitch = seqs + PITCH
    rows, pair = seqs * tokens, 2 * pad
    step, last = pl.program_id(0), pl.num_programs(0) - 1
    now, then = lax.rem(step, 2), lax.rem(step + 1, 2)
    ff = wup_ref.shape[1]
    hp = d // LANES

    @pl.when(step == 0)
    def _():
        qkv[:, tokens * pitch :] = jnp.zeros((3 * hp, (pad - tokens) * pitch, LANES), f32)

    low = lax.broadcasted_iota(jnp.int32, (pair, LANES), 1) < HEAD
    key_lane = lax.broadcasted_iota(jnp.int32, (pair, 2 * pair), 1)
    query_row = lax.broadcasted_iota(jnp.int32, (pair, 2 * pair), 0)
    first_head = key_lane < pair
    key_row = jnp.where(first_head, key_lane, key_lane - pair)
    second_image = key_row >= pad
    key_pos = jnp.where(second_image, key_row - pad, key_row)
    bias = jnp.where((key_pos < tokens) & (second_image == (query_row >= pad)), 0.0, -1e30)
    zero, one = jnp.zeros((pair, LANES), bf16), jnp.ones((pair, LANES), bf16)
    ones = stack_heads(one, low, zero)
    tiles = [(b, p) for b in range(seqs // 2) for p in range(hp)]

    def pick(j, b):
        return jnp.concatenate([qkv[j, pl.ds(2 * b + i, pad, stride=pitch), :] for i in range(2)], 0).astype(bf16)

    def attend(b, p, e):
        v = stack_heads(pick(2 * hp + p, b), low, zero)
        o = dot(e, jnp.concatenate([v, ones], 1))
        o = o[:, :LANES] / o[:, LANES:]
        for i in range(2):
            att[now, p, pl.ds(2 * b + i, pad, stride=pitch), :] = o[i * pad : (i + 1) * pad]

    def project(n1, c):
        r = dot(n1, wqkv_ref[:, c * d : (c + 1) * d])
        r = r * HEAD**-0.5 if c == 0 else r
        for p in range(hp):
            for t in range(tokens):
                qkv[c * hp + p, t * pitch : t * pitch + seqs] = r[t * seqs : (t + 1) * seqs, p * LANES : (p + 1) * LANES]

    def attention():
        x = x_ref[...].astype(f32).reshape(rows, d)
        n1 = (norm_parts(x)[0] * gains_ref[0:1, :] + shifts_ref[0:1, :]).astype(bf16)
        for c in range(3):
            project(n1, c)
            yield
        big = jnp.zeros((pair, 2 * pair), f32)
        for b, p in tiles:
            s = dot_nt(pick(p, b), stack_heads(pick(hp + p, b), low, zero))
            big = jnp.maximum(big, jnp.abs(s))
            sc[b * hp + p] = s
        yield
        for i in range(len(tiles)):
            ec[i] = jnp.exp(sc[i] + bias).astype(bf16)
        yield
        for b, p in tiles:
            attend(b, p, ec[b * hp + p])
        yield big

    def recheck(big):
        @pl.when(jnp.logical_not(jnp.max(big) < SAFE))
        def _():
            for b in range(seqs // 2):

                @pl.loop(0, hp)
                def _(p):
                    s = sc[b * hp + p] + bias
                    top0 = jnp.max(jnp.where(first_head, s, -2e30), -1, keepdims=True)
                    top1 = jnp.max(jnp.where(first_head, -2e30, s), -1, keepdims=True)
                    attend(b, p, jnp.exp(s - jnp.where(first_head, top0, top1)).astype(bf16))

    def forward():
        attended = jnp.concatenate(
            [jnp.concatenate([att[then, p, t * pitch : t * pitch + seqs] for p in range(hp)], 1) for t in range(tokens)], 0
        ).astype(bf16)
        mid = old_ref[...].astype(f32).reshape(rows, d) + dot(attended, wo_ref[...])
        at = pl.ds(pl.multiple_of((step - 1) * seqs, seqs), seqs)
        ms[at, :] = jnp.sum(mid.reshape(tokens, seqs, d), 0)
        n2 = (norm_parts(mid)[0] * gains_ref[1:2, :] + shifts_ref[1:2, :]).astype(bf16)
        yield
        chunk = ff // 2
        for c in range(0, ff, chunk):
            v = dot(n2, wup_ref[:, c : c + chunk])
            t = jnp.tanh(v * (GELU_C + (GELU_C * GELU_A) * (v * v)))
            h = (0.5 * v) * (1.0 + t)
            hs[at, c : c + chunk] = jnp.sum(h.reshape(tokens, seqs, chunk), 0)
            yield

    def run(*works):
        works, given = list(works), None
        while works:
            for w in list(works):
                try:
                    value = next(w)
                    given = given if value is None else value
                except StopIteration:
                    works.remove(w)
        return given

    @pl.when(step == 0)
    def _():
        recheck(run(attention()))

    @pl.when((step > 0) & (step < last))
    def _():
        recheck(run(attention(), forward()))

    @pl.when(step == last)
    def _():
        run(forward())
        hi, lo = split_bf16(hs[...] * (1.0 / tokens))
        u = ms[...] * (1.0 / tokens) + dot(hi, wdown_ref[...]) + dot(lo, wdown_ref[...])
        n = u.shape[0]
        out_ref[:n] = (u * lax.rsqrt(jnp.sum(u * u, -1, keepdims=True) + 1e-6)).astype(bf16)
        if out_ref.shape[0] > n:
            out_ref[n:] = count_rows(valid_ref, d)


def image_embed(xt, valid, gains, shifts, wqkv, wo, wup, wdown, start, count, note, seqs=16):
    tokens, _, d = xt.shape
    ff = wup.shape[1]
    pad = -(-tokens // 8) * 8
    pitch = seqs + PITCH
    tiles = seqs // 2 * (d // LANES)
    first, groups = start // seqs, count // seqs
    rows = count + (NOTE if note else 0)
    return pl.pallas_call(
        functools.partial(image_kernel, seqs),
        grid=(groups + 1,),
        in_specs=[
            pl.BlockSpec((tokens, seqs, d), lambda i: (0, jnp.minimum(i, groups - 1) + first, 0)),
            pl.BlockSpec((tokens, seqs, d), lambda i: (0, jnp.maximum(i - 1, 0) + first, 0)),
        ]
        + [whole(a) for a in (valid, gains, shifts, wqkv, wo, wup, wdown)],
        out_specs=pl.BlockSpec((rows, d), lambda i: (0, 0)),
        out_shape=jax.ShapeDtypeStruct((rows, d), bf16),
        scratch_shapes=[
            pltpu.VMEM((3 * d // LANES, pitch * pad, LANES), f32),
            pltpu.VMEM((2, d // LANES, pitch * pad, LANES), f32),
            pltpu.VMEM((tiles, 2 * pad, 4 * pad), f32),
            pltpu.VMEM((tiles, 2 * pad, 4 * pad), bf16),
            pltpu.VMEM((count, ff), f32),
            pltpu.VMEM((count, d), f32),
        ],
        compiler_params=params(56 * 1024 * 1024),
        cost_estimate=cost(0.45 * count),
        name="image_block",
    )(xt, xt, valid, gains, shifts, wqkv, wo, wup, wdown)


def real_tokens(length, txt):
    seqs = length.shape[0]
    spread = jnp.broadcast_to(length[:, None, :], (seqs, txt, 1)).reshape(seqs * txt, 1)
    pos = lax.broadcasted_iota(jnp.int32, (seqs * txt, 1), 0) % txt
    return jnp.where(pos.astype(f32) < spread, 1.0, 0.0)


def text_forward_kernel(
    txt, held, x_ref, key_ref, flen_ref, gains_ref, shifts_ref, wqkv_ref, wo_ref, wup_ref, wdown_ref, *refs,
):
    (n1_ref, qkv_ref, probs_ref, att_ref, n2_ref, slope_ref, stat_ref, hpool_ref, u_ref, emb_ref, ms, sc, ec) = refs[held:]
    step = pl.program_id(0)
    rows, d = x_ref.shape
    ff = wup_ref.shape[1]
    seqs = rows // txt
    x = x_ref[...].astype(f32)
    xhat1, rstd1 = norm_parts(x)
    n1 = (xhat1 * gains_ref[0:1, :] + shifts_ref[0:1, :]).astype(bf16)
    n1_ref[...] = n1
    qkv_ref[:, :d] = (dot(n1, wqkv_ref[:, :d]) * HEAD**-0.5).astype(bf16)
    qkv_ref[:, d:] = dot(n1, wqkv_ref[:, d:]).astype(bf16)
    low = lax.broadcasted_iota(jnp.int32, (LANES, LANES), 1) < HEAD
    same = (
        lax.broadcasted_iota(jnp.int32, (LANES, LANES), 0) // txt
        == lax.broadcasted_iota(jnp.int32, (LANES, LANES), 1) // txt
    )
    zero = jnp.zeros((LANES, LANES), bf16)
    hp = d // LANES
    tiles = [(g, p) for g in range(rows // LANES) for p in range(hp)]

    def attend(g, p, probs):
        r = slice(g * LANES, (g + 1) * LANES)
        probs_ref[g * hp + p] = probs
        v = qkv_ref[r, 2 * d + p * LANES : 2 * d + (p + 1) * LANES]
        att_ref[r, p * LANES : (p + 1) * LANES] = dot(probs, stack_heads(v, low, zero)).astype(bf16)

    def share(s, top):
        halves = []
        for h in range(2):
            sh = s[:, h * LANES : (h + 1) * LANES]
            e = jnp.exp(sh - jnp.max(sh, -1, keepdims=True)) if top else jnp.exp(sh)
            halves.append(e / jnp.sum(e, -1, keepdims=True))
        return jnp.concatenate(halves, 1).astype(bf16)

    big = jnp.zeros((LANES, 2 * LANES), f32)
    for g, p in tiles:
        r = slice(g * LANES, (g + 1) * LANES)
        bias = jnp.where(same & (key_ref[0, g : g + 1, :] > 0), 0.0, -1e30)
        q = qkv_ref[r, p * LANES : (p + 1) * LANES]
        k = qkv_ref[r, d + p * LANES : d + (p + 1) * LANES]
        s = dot_nt(q, stack_heads(k, low, zero))
        big = jnp.maximum(big, jnp.abs(s))
        sc[g * hp + p] = s + jnp.concatenate([bias, bias], 1)
    for g, p in tiles:
        ec[g * hp + p] = share(sc[g * hp + p], False)
    for g, p in tiles:
        attend(g, p, ec[g * hp + p])

    @pl.when(jnp.logical_not(jnp.max(big) < SAFE))
    def _():
        for g, p in tiles:
            attend(g, p, share(sc[g * hp + p], True))

    mid = x + dot(att_ref[...], wo_ref[...])
    xhat2, rstd2 = norm_parts(mid)
    lane = lax.broadcasted_iota(jnp.int32, (rows, LANES), 1)
    hi1, hi2 = rstd1.astype(bf16).astype(f32), rstd2.astype(bf16).astype(f32)
    stat = jnp.where(lane < 64, jnp.where(lane < 32, hi1, rstd1 - hi1), jnp.where(lane < 96, hi2, rstd2 - hi2))
    stat_ref[...] = stat.astype(bf16)
    at = pl.ds(pl.multiple_of(step * seqs, seqs), seqs)
    keep = real_tokens(flen_ref[at, :], txt)
    n2 = ((xhat2 * gains_ref[1:2, :] + shifts_ref[1:2, :]) * keep).astype(bf16)
    n2_ref[...] = n2
    ms[at, :] = jnp.sum((mid * keep).reshape(seqs, txt, d), 1)
    chunk = 512
    for c in range(0, ff, chunk):
        v = dot(n2, wup_ref[:, c : c + chunk])
        v2 = v * v
        t = jnp.tanh(v * (GELU_C + (GELU_C * GELU_A) * v2))
        half = 0.5 + 0.5 * t
        h = v * half
        slope = half + h * (1.0 - t) * (GELU_C + (3.0 * GELU_C * GELU_A) * v2)
        slope_ref[:, c : c + chunk] = (slope * keep).astype(bf16)
        hpool_ref[at, c : c + chunk] = jnp.sum(h.reshape(seqs, txt, chunk), 1)

    @pl.when(step == pl.num_programs(0) - 1)
    def _():
        hi, lo = split_bf16(hpool_ref[...])
        pooled = ms[...] + dot(hi, wdown_ref[...]) + dot(lo, wdown_ref[...])
        u = pooled / flen_ref[...]
        u_ref[...] = u
        emb_ref[...] = (u * lax.rsqrt(jnp.sum(u * u, -1, keepdims=True) + 1e-6)).astype(bf16)


def text_forward(piece, pieces, held, x, key_ok, flen, gains, shifts, wqkv, wo, wup, wdown, txt, rows=512):
    total, d = x.shape
    ff = wup.shape[1]
    pairs = total // txt
    hp = d // LANES
    part = pairs // pieces
    steps = total // pieces // rows
    first = piece * steps
    block = lambda *tail: pl.BlockSpec((rows,) + tail, lambda i: (i + first,) + (0,) * len(tail))
    still = lambda *shape: pl.BlockSpec(shape, lambda i: (piece, 0))
    shape = jax.ShapeDtypeStruct
    key3 = key_ok.reshape(total // rows, rows // LANES, LANES)
    args = (x, key3, flen, gains, shifts, wqkv, wo, wup, wdown)
    return pl.pallas_call(
        functools.partial(text_forward_kernel, txt, len(held)),
        grid=(steps,),
        in_specs=[
            block(d), pl.BlockSpec((1, rows // LANES, LANES), lambda i: (i + first, 0, 0)), still(part, 1)
        ]
        + [whole(a) for a in args[3:]]
        + [pl.BlockSpec(memory_space=pl.ANY)] * len(held),
        out_specs=[
            block(d), block(3 * d), pl.BlockSpec((rows // LANES * hp, LANES, 2 * LANES), lambda i: (i + first, 0, 0)),
            block(d), block(d), block(ff), block(LANES), still(part, ff), still(part, d), still(part, d),
        ],
        out_shape=[
            shape((total, d), bf16), shape((total, 3 * d), bf16), shape((total // LANES * hp, LANES, 2 * LANES), bf16),
            shape((total, d), bf16), shape((total, d), bf16), shape((total, ff), bf16), shape((total, LANES), bf16),
            shape((pairs, ff), f32), shape((pairs, d), f32), shape((pairs, d), bf16),
        ],
        input_output_aliases={len(args) + i: i for i in range(len(held))},
        scratch_shapes=[
            pltpu.VMEM((part, d), f32),
            pltpu.VMEM((rows // LANES * hp, LANES, 2 * LANES), f32),
            pltpu.VMEM((rows // LANES * hp, LANES, 2 * LANES), bf16),
        ],
        compiler_params=params(18 * 1024 * 1024),
        cost_estimate=cost(0.013 * total / pieces),
        name="text_forward",
    )(*args, *held)


def scores_kernel(
    group, place_ref, own_ref, other_ref, own_valid_ref, other_valid_ref, scale_ref, a0_ref, a1_ref,
    s_ref, all_ref, col_out, okay_out, row_out,
):
    step = pl.program_id(0)
    pairs = own_ref.shape[0]
    scale = scale_ref[0]
    row = lax.broadcasted_iota(jnp.int32, (pairs, 1), 0).astype(f32)
    mask = [jnp.where(row < jnp.sum(v[...], 1, keepdims=True), 1.0, 0.0) for v in (own_valid_ref, other_valid_ref)]
    mask = jnp.concatenate(mask, 0)
    inner = lax.rem(place_ref[0], group)
    late = lax.bitwise_xor(step, lax.div(place_ref[0], group)) >= pl.num_programs(0) // 2
    texts = jnp.concatenate([own_ref[...], other_ref[...]], 0)

    @pl.when(step == 0)
    def _():
        row_out[...] = jnp.zeros_like(row_out)
        row_out[:, 3:4] = mask

    lane = lax.broadcasted_iota(jnp.int32, (1, pairs), 1).astype(f32)
    for k in range(group):
        at = lax.bitwise_xor(k, inner)
        cols = slice(k * pairs, (k + 1) * pairs)
        a = jnp.where(late, a1_ref[at], a0_ref[at])
        images = a[:pairs]
        count = a[pairs : pairs + 1, 0:1].astype(f32)
        okay = jnp.where(lane < count, 1.0, 0.0)
        okay_out[0:1, cols] = okay
        all_ref[cols, :] = images
        s = scale * dot_nt(texts, images)
        s_ref[:, cols] = s
        up = jnp.exp(s - SHIFT)
        down = jnp.exp(jnp.minimum(s, 0.0) + SHIFT)
        col_out[0:1, cols] = jnp.sum(up * mask, 0, keepdims=True)
        col_out[1:2, cols] = jnp.sum(down * mask, 0, keepdims=True)
        row_out[:, 0:1] += jnp.sum(up * okay, 1, keepdims=True)
        row_out[:, 1:2] += jnp.sum(down * okay, 1, keepdims=True)
        row_out[:, 2:3] += jnp.broadcast_to(count, (2 * pairs, 1))


def pair_scores(place, own, other, own_valid, other_valid, scale, a0, a1):
    slots, _, d = a0.shape
    pairs = own.shape[0]
    group = min(8, slots)
    groups = slots // group
    cols = group * pairs
    keep = lambda *_: (0, 0)
    turn = lambda i, s: (lax.rem(lax.bitwise_xor(i, lax.div(s[0], group)), groups), 0, 0)
    still = lambda a: pl.BlockSpec(a.shape, keep)
    shape = jax.ShapeDtypeStruct
    return pl.pallas_call(
        functools.partial(scores_kernel, group),
        grid_spec=pltpu.PrefetchScalarGridSpec(
            num_scalar_prefetch=1,
            grid=(2 * groups,),
            in_specs=[still(own), still(other), still(own_valid), still(other_valid), pl.BlockSpec(memory_space=pltpu.SMEM)]
            + [pl.BlockSpec((group,) + a.shape[1:], turn) for a in (a0, a1)],
            out_specs=[
                pl.BlockSpec((2 * pairs, cols), lambda i, s: (0, i)),
                pl.BlockSpec((cols, d), lambda i, s: (i, 0)),
                pl.BlockSpec((2, cols), lambda i, s: (0, i)),
                pl.BlockSpec((1, cols), lambda i, s: (0, i)),
                pl.BlockSpec((2 * pairs, 4), keep),
            ],
        ),
        out_shape=[
            shape((2 * pairs, 2 * groups * cols), f32), shape((2 * groups * cols, d), bf16),
            shape((2, 2 * groups * cols), f32), shape((1, 2 * groups * cols), f32), shape((2 * pairs, 4), f32),
        ],
        compiler_params=params(12 * 1024 * 1024),
        cost_estimate=cost(4.0),
        name="pair_scores",
    )(place, own, other, own_valid, other_valid, scale, a0, a1)


def log_sum(up, down):
    fine = up >= 1.9287498479639178e-22
    return jnp.where(
        fine, jnp.log(jnp.where(fine, up, 1.0)) + SHIFT, jnp.log(jnp.where(fine, 1.0, down)) - SHIFT
    )


def gradient_kernel(
    dp, scale_ref, s_ref, all_ref, col_ref, got_ref, okay_ref, row_ref, swap_ref, text_ref, a_ref,
    grad_ref, back_ref, loss_ref,
):
    step = pl.program_id(0)
    pairs = text_ref.shape[0]
    row = row_ref[...] + jnp.concatenate([swap_ref[pairs:], swap_ref[:pairs]], 0)
    factor = 0.5 / row[0:1, 2:3]
    mask = row_ref[:, 3:4]
    okay = okay_ref[...]
    row_lse = log_sum(row[:, 0:1], row[:, 1:2])
    col = col_ref[...] + got_ref[...]
    col_lse = log_sum(col[0:1, :], col[1:2, :])

    @pl.when(step == 0)
    def _():
        grad_ref[...] = jnp.zeros_like(grad_ref)
        back_ref[...] = jnp.zeros_like(back_ref)
        loss_ref[...] = jnp.zeros_like(loss_ref)
        t = text_ref[...].astype(f32) * a_ref[:pairs].astype(f32)
        diag = scale_ref[0] * jnp.sum(t, -1, keepdims=True)
        m = mask[:pairs]
        loss_ref[0:1, 0:1] = factor * jnp.sum(m * (row_lse[:pairs] - 2.0 * diag), 0, keepdims=True)
        loss_ref[1:2, 0:1] = -2.0 * factor * jnp.sum(m * diag, 0, keepdims=True)

    s = s_ref[...]
    g = jnp.exp(jnp.minimum(s - row_lse, 1.0)) + jnp.exp(jnp.minimum(s - col_lse, 1.0))
    g = g * ((factor * mask) * okay)
    grad = dot(g.astype(bf16), all_ref[...])
    grad_ref[...] += grad[:pairs]
    back_ref[...] += grad[pairs:]
    cols = jnp.sum(jnp.where(okay > 0, col_lse, 0.0), 1, keepdims=True)
    loss_ref[0:1, 0:1] += factor * (cols * (1.0 / dp))
    loss_ref[1:2, 0:1] += jnp.sum(jnp.sum(g * s, 0, keepdims=True), 1, keepdims=True)


def pair_gradients(dp, scale, scores, images, col, got, okay, row, swap, texts, a):
    pairs, d = texts.shape
    cols = min(8, dp) * pairs
    still = lambda *shape: pl.BlockSpec(shape, lambda i: (0, 0))
    shape = jax.ShapeDtypeStruct
    return pl.pallas_call(
        functools.partial(gradient_kernel, dp),
        grid=(dp * pairs // cols,),
        in_specs=[
            pl.BlockSpec(memory_space=pltpu.SMEM),
            pl.BlockSpec((2 * pairs, cols), lambda i: (0, i)),
            pl.BlockSpec((cols, d), lambda i: (i, 0)),
            pl.BlockSpec((2, cols), lambda i: (0, i)),
            pl.BlockSpec((2, cols), lambda i: (0, i)),
            pl.BlockSpec((1, cols), lambda i: (0, i)),
        ]
        + [whole(x) for x in (row, swap, texts, a)],
        out_specs=[still(pairs, d), still(pairs, d), still(8, LANES)],
        out_shape=[shape((pairs, d), f32), shape((pairs, d), f32), shape((8, LANES), f32)],
        compiler_params=params(12 * 1024 * 1024),
        cost_estimate=cost(3.0),
        name="pair_gradients",
    )(scale, scores, images, col, got, okay, row, swap, texts, a)


def spread_rows(a, txt):
    seqs, width = a.shape
    return jnp.broadcast_to(a[:, None, :], (seqs, txt, width)).reshape(seqs * txt, width)


def backward_up_kernel(
    txt, scale_ref, rep_ref, part_ref, back_ref, row_ref, swap_ref, a_ref, u_ref, len_ref, hpool_ref, n2_ref, slope_ref,
    wdown_ref, send_ref, keep_ref, gd_ref, dh_ref, down, acc,
):
    step = pl.program_id(0)
    rows, d = n2_ref.shape
    ff = slope_ref.shape[1]
    seqs = rows // txt

    @pl.when(step == 0)
    def _():
        pairs = part_ref.shape[0]
        scale = scale_ref[0]
        factor = 0.5 / (row_ref[0:1, 2:3] + swap_ref[0:1, 2:3])
        images = a_ref[:pairs].astype(f32)
        u = u_ref[...]
        r = lax.rsqrt(jnp.sum(u * u, -1, keepdims=True) + 1e-6)
        g = scale * (part_ref[...] + back_ref[...]) - (2.0 * scale) * (factor * row_ref[:pairs, 3:4]) * images
        du = (r * g - (r * r * r) * u * jnp.sum(u * g, -1, keepdims=True)) / len_ref[...]
        gd_ref[...] = du
        low = du.astype(bf16)
        dh_ref[...] = dot_nt(low, wdown_ref[...])
        hi, lo = split_bf16(hpool_ref[...])
        down[...] = (dot_tn(hi, low) + dot_tn(lo, low)).astype(bf16)
        acc[...] = jnp.zeros_like(acc)

    at = pl.ds(pl.multiple_of(step * seqs, seqs), seqs)
    chunk = 512
    for c in range(0, ff, chunk):
        cs = slice(c, c + chunk)
        grad_before = (spread_rows(dh_ref[at, cs], txt) * slope_ref[:, cs].astype(f32)).astype(bf16)
        acc[:, cs] += dot_tn(n2_ref[...], grad_before)

    @pl.when(step == pl.num_programs(0) - 1)
    def _():
        first = rep_ref[0] == 0
        for b in range(ff // d):
            r = slice(b * d, (b + 1) * d)
            up = acc[:, r].astype(bf16)
            keep_ref[r] = jnp.where(first, down[r], up)
            send_ref[r] = jnp.where(first, up, down[r])


def backward_up(scale, rep, part, back, row, swap, a, u, flen, hpool, n2, slope, wdown, txt, rows=512):
    tokens, d = n2.shape
    pairs, ff = hpool.shape
    block = lambda w: pl.BlockSpec((rows, w), lambda i: (i, 0))
    shape = jax.ShapeDtypeStruct
    smem = pl.BlockSpec(memory_space=pltpu.SMEM)
    outs = [shape((ff, d), bf16), shape((ff, d), bf16), shape((pairs, d), f32), shape((pairs, ff), f32)]
    return pl.pallas_call(
        functools.partial(backward_up_kernel, txt),
        grid=(tokens // rows,),
        in_specs=[smem, smem]
        + [whole(x) for x in (part, back, row, swap, a, u, flen, hpool)]
        + [block(d), block(ff), whole(wdown)],
        out_specs=[whole(x) for x in outs],
        out_shape=outs,
        scratch_shapes=[pltpu.VMEM((ff, d), bf16), pltpu.VMEM((d, ff), f32)],
        compiler_params=params(16 * 1024 * 1024),
        cost_estimate=cost(0.006 * tokens),
        name="backward_up",
    )(scale, rep, part, back, row, swap, a, u, flen, hpool, n2, slope, wdown)


def backward_middle_kernel(
    txt, gd_ref, dh_ref, len_ref, n2_ref, slope_ref, stat_ref, att_ref, gains_ref, shifts_ref, wup_ref, wo_ref,
    gmid_ref, datt_ref, dwo_ref, gain_ref, acc,
):
    step = pl.program_id(0)
    rows, d = n2_ref.shape
    ff = wup_ref.shape[1]

    @pl.when(step == 0)
    def _():
        acc[...] = jnp.zeros_like(acc)
        gain_ref[...] = jnp.zeros_like(gain_ref)

    dn2 = jnp.zeros((rows, d), f32)
    chunk = 512
    for c in range(0, ff, chunk):
        cs = slice(c, c + chunk)
        grad_before = (spread_rows(dh_ref[:, cs], txt) * slope_ref[:, cs].astype(f32)).astype(bf16)
        dn2 += dot_nt(grad_before, wup_ref[:, cs])
    xhat = (n2_ref[...].astype(f32) - shifts_ref[1:2, :]) / gains_ref[1:2, :]
    stat = stat_ref[...].astype(f32)
    gain_ref[0:1, :] += jnp.sum(dn2 * xhat, 0, keepdims=True)
    gain_ref[1:2, :] += jnp.sum(dn2, 0, keepdims=True)
    gn = dn2 * gains_ref[1:2, :]
    dmid = (stat[:, 64:65] + stat[:, 96:97]) * (
        gn - jnp.mean(gn, -1, keepdims=True) - xhat * jnp.mean(gn * xhat, -1, keepdims=True)
    )
    gmid = spread_rows(gd_ref[...], txt) * real_tokens(len_ref[...], txt) + dmid
    gmid_ref[...] = gmid
    branch = gmid.astype(bf16)
    acc[...] += dot_tn(att_ref[...], branch)
    datt_ref[...] = dot_nt(branch, wo_ref[...]).astype(bf16)

    @pl.when(step == pl.num_programs(0) - 1)
    def _():
        dwo_ref[...] = acc[...].astype(bf16)


def backward_middle(gd, dh, flen, n2, slope, stat, att, gains, shifts, wup, wo, txt, rows=512):
    tokens, d = n2.shape
    ff = wup.shape[1]
    block = lambda w: pl.BlockSpec((rows, w), lambda i: (i, 0))
    lead = lambda w: pl.BlockSpec((rows // txt, w), lambda i: (i, 0))
    shape = jax.ShapeDtypeStruct
    sums = [shape((d, d), bf16), shape((8, d), f32)]
    return pl.pallas_call(
        functools.partial(backward_middle_kernel, txt),
        grid=(tokens // rows,),
        in_specs=[lead(d), lead(ff), lead(1), block(d), block(ff), block(LANES), block(d)]
        + [whole(x) for x in (gains, shifts, wup, wo)],
        out_specs=[block(d), block(d)] + [whole(x) for x in sums],
        out_shape=[shape((tokens, d), f32), shape((tokens, d), bf16)] + sums,
        scratch_shapes=[pltpu.VMEM((d, d), f32)],
        compiler_params=params(16 * 1024 * 1024),
        cost_estimate=cost(0.006 * tokens),
        name="backward_middle",
    )(gd, dh, flen, n2, slope, stat, att, gains, shifts, wup, wo)


def backward_attention_kernel(
    held, last, rep_ref, datt_ref, qkv_ref, probs_ref, n1_ref, dwo_ref, gain2_ref, sums_ref, gains_ref, shifts_ref, wqkv_ref,
    *refs
):
    old_acc, old_flat = refs[1:3] if held else (None, None)
    gq_ref, *outs = refs[held:-4]
    acc, flat, sc, ec = refs[-4:]
    step = pl.program_id(0)
    rows, d = n1_ref.shape
    low = lax.broadcasted_iota(jnp.int32, (LANES, LANES), 1) < HEAD
    zero = jnp.zeros((LANES, LANES), bf16)

    @pl.when(step == 0)
    def _():
        acc[...] = old_acc[...] if held else jnp.zeros_like(acc)
        flat[...] = old_flat[...] if held else jnp.zeros_like(flat)

    hp = d // LANES
    tiles = [(g, p) for g in range(rows // LANES) for p in range(hp)]
    at = lambda g, p, part: (slice(g * LANES, (g + 1) * LANES), slice(part * d + p * LANES, part * d + (p + 1) * LANES))
    for g, p in tiles:
        sc[g * hp + p] = dot_nt(datt_ref[at(g, p, 0)], stack_heads(qkv_ref[at(g, p, 2)], low, zero))
    for g, p in tiles:
        i = g * hp + p
        probs = probs_ref[i].astype(f32)
        halves = []
        for h in range(2):
            hs = slice(h * LANES, (h + 1) * LANES)
            ph, dh = probs[:, hs], sc[i, :, hs]
            halves.append(ph * (dh - jnp.sum(ph * dh, -1, keepdims=True)))
        ec[i] = jnp.concatenate(halves, 1).astype(bf16)
    for g, p in tiles:
        dv = dot_tn(probs_ref[g * hp + p], datt_ref[at(g, p, 0)])
        gq_ref[at(g, p, 2)] = jnp.where(low, dv[:LANES], dv[LANES:]).astype(bf16)
    for g, p in tiles:
        keys = stack_heads(qkv_ref[at(g, p, 1)], low, zero)
        gq_ref[at(g, p, 0)] = (dot(ec[g * hp + p], keys) * HEAD**-0.5).astype(bf16)
    for g, p in tiles:
        dk = dot_tn(ec[g * hp + p], qkv_ref[at(g, p, 0)])
        gq_ref[at(g, p, 1)] = jnp.where(low, dk[:LANES], dk[LANES:]).astype(bf16)
    gq = gq_ref[...]
    acc[...] += dot_tn(n1_ref[...], gq)
    flat[0:1, :] += jnp.sum(gq.astype(f32), 0, keepdims=True)

    @pl.when(step == pl.num_programs(0) - 1)
    def _():
        if not last:
            outs[0][...] = acc[...]
            outs[1][...] = flat[...]
            return
        send_ref, keep_ref, small_ref = outs
        w = wqkv_ref[...]
        ones = jnp.ones((8, 3 * d), bf16)
        hi, lo = split_bf16(acc[...] * w.astype(f32))
        spread = dot_nt(ones, hi) + dot_nt(ones, lo)
        hi, lo = split_bf16(flat[...])
        dshift = (dot_nt(hi, w) + dot_nt(lo, w))[0:1]
        dgain = (spread[0:1] - shifts_ref[0:1, :] * dshift) / gains_ref[0:1, :]
        small = [dgain, gain2_ref[0:1, :], dshift, gain2_ref[1:2, :]]
        small += [jnp.broadcast_to(sums_ref[i : i + 1, 0:1], (1, d)) for i in range(2)]
        small = jnp.concatenate(small + [jnp.zeros((2, d), f32)], 0)
        small_ref[...] = small
        first = rep_ref[0] == 0
        parts = [acc[:, b * d : (b + 1) * d].astype(bf16) for b in range(3)] + [dwo_ref[...]]
        for b in range(2):
            keep_ref[b * d : (b + 1) * d] = jnp.where(first, parts[b], parts[b + 2])
            send_ref[b * d : (b + 1) * d] = jnp.where(first, parts[b + 2], parts[b])
        put_small(send_ref, 2 * d, small)


def backward_attention(piece, pieces, held, rep, datt, qkv, probs, n1, dwo, gain2, sums, gains, shifts, wqkv, rows=512):
    tokens, d = n1.shape
    steps = tokens // pieces // rows
    first = piece * steps
    last = piece == pieces - 1
    block = lambda w: pl.BlockSpec((rows, w), lambda i: (i + first, 0))
    shape = jax.ShapeDtypeStruct
    if last:
        outs = [shape((2 * d + NOTE, d), bf16), shape((2 * d, d), bf16), shape((8, d), f32)]
    else:
        outs = [shape((d, 3 * d), f32), shape((8, 3 * d), f32)]
    args = (rep, datt, qkv, probs, n1, dwo, gain2, sums, gains, shifts, wqkv)
    return pl.pallas_call(
        functools.partial(backward_attention_kernel, len(held), last),
        grid=(steps,),
        in_specs=[
            pl.BlockSpec(memory_space=pltpu.SMEM), block(d), block(3 * d),
            pl.BlockSpec((rows // LANES * (d // LANES), LANES, 2 * LANES), lambda i: (i + first, 0, 0)),
            block(d),
        ]
        + [whole(x) for x in args[5:]]
        + ([pl.BlockSpec(memory_space=pl.ANY)] + [whole(x) for x in held[1:]] if held else []),
        out_specs=[block(3 * d)] + [whole(x) for x in outs],
        out_shape=[shape((tokens, 3 * d), bf16)] + outs,
        input_output_aliases={len(args): 0} if held else {},
        scratch_shapes=[
            pltpu.VMEM((d, 3 * d), f32),
            pltpu.VMEM((8, 3 * d), f32),
            pltpu.VMEM((rows // LANES * (d // LANES), LANES, 2 * LANES), f32),
            pltpu.VMEM((rows // LANES * (d // LANES), LANES, 2 * LANES), bf16),
        ],
        compiler_params=params(16 * 1024 * 1024),
        cost_estimate=cost(0.009 * tokens / pieces),
        name="backward_attention",
    )(*args, *held)


def backward_input_kernel(gq_ref, gmid_ref, n1_ref, stat_ref, gains_ref, shifts_ref, wqkv_ref, *refs):
    dx_ref = refs[-1]
    gn = dot_nt(gq_ref[...], wqkv_ref[...]) * gains_ref[0:1, :]
    xhat = (n1_ref[...].astype(f32) - shifts_ref[0:1, :]) / gains_ref[0:1, :]
    stat = stat_ref[...].astype(f32)
    dx_ref[...] = gmid_ref[...] + (stat[:, 0:1] + stat[:, 32:33]) * (
        gn - jnp.mean(gn, -1, keepdims=True) - xhat * jnp.mean(gn * xhat, -1, keepdims=True)
    )


def backward_input(piece, pieces, held, gq, gmid, n1, stat, gains, shifts, wqkv, rows=512):
    tokens, d = gmid.shape
    steps = tokens // pieces // rows
    block = lambda w: pl.BlockSpec((rows, w), lambda i: (i + piece * steps, 0))
    args = (gq, gmid, n1, stat, gains, shifts, wqkv)
    return pl.pallas_call(
        backward_input_kernel,
        grid=(steps,),
        in_specs=[block(3 * d), block(d), block(d), block(LANES), whole(gains), whole(shifts), whole(wqkv)]
        + [pl.BlockSpec(memory_space=pl.ANY)] * len(held),
        out_specs=block(d),
        out_shape=jax.ShapeDtypeStruct((tokens, d), f32),
        input_output_aliases={len(args): 0} if held else {},
        compiler_params=params(16 * 1024 * 1024),
        cost_estimate=cost(0.004 * tokens / pieces),
        name="backward_input",
    )(*args, *held)


def finish_kernel(places, rep_ref, own_ref, got_ref, *out_refs):
    first = rep_ref[0] == 0
    for out, top, left, begin, n, part in places:
        a = own_ref[begin : begin + n, :]
        b = got_ref[begin : begin + n, :]
        mine = first if part == 0 else jnp.logical_not(first)
        out_refs[out][top : top + n, left : left + a.shape[1]] = jnp.where(mine, a, b).astype(f32)


def finish(rep, own, got, shapes, segments):
    half = own.shape[0]
    places = []
    for row, count, out, top, left in segments:
        while count:
            part, begin = divmod(row, half)
            n = min(count, half - begin)
            places.append((out, top, left, begin, n, part))
            row, top, count = row + n, top + n, count - n
    outs = [jax.ShapeDtypeStruct(s, f32) for s in shapes]
    return pl.pallas_call(
        functools.partial(finish_kernel, places),
        grid=(1,),
        in_specs=[pl.BlockSpec(memory_space=pltpu.SMEM), whole(own), whole(got)],
        out_specs=[whole(x) for x in outs],
        out_shape=outs,
        compiler_params=params(16 * 1024 * 1024),
        cost_estimate=cost(3.0),
        name="finish",
    )(rep, own, got)


class Links:
    def __init__(self, mesh):
        self.dp, self.rep = mesh.shape["dp"], mesh.shape["rep"]
        self.bits = (self.dp - 1).bit_length()
        assert self.dp == 1 << self.bits and self.rep == 2
        near, far = list(range(min(2, self.bits))), list(range(2, self.bits))
        turn = lambda bits: list(zip(bits, bits[::-1]))
        self.near, self.far = turn(near), turn(far)
        self.gather_order = [(b, b) for b in far[::-1]] + self.near

    def bit(self, pair):
        place = lax.axis_index("dp")
        return jnp.where(lax.axis_index("rep") == 0, (place >> pair[0]) & 1, (place >> pair[1]) & 1)

    def across(self, x, pair):
        moves = [(2 * i + r, 2 * (i ^ (1 << pair[r])) + r) for i in range(self.dp) for r in range(2)]
        return lax.ppermute(x, ("dp", "rep"), moves)

    def core(self, x):
        return lax.ppermute(x, "rep", [(0, 1), (1, 0)])


def put_small(ref, at, small):
    hi, lo = split_bf16(small)
    ref[at : at + NOTE] = jnp.concatenate([hi, lo], 0)


def hop_kernel(kind, late, with_small, v_ref, x_ref, got_ref, *refs):
    n, d = x_ref.shape
    refs = list(refs)
    small_ref = refs.pop(0) if with_small else None
    low = v_ref[0] == 0
    if kind == "join":
        x, got = x_ref[...], got_ref[...]
        refs[0][:n] = jnp.where(low, x, got)
        refs[0][n:] = jnp.where(low, got, x)
        return
    add = lambda r: (x_ref[r].astype(f32) + got_ref[r].astype(f32)).astype(bf16)
    send_ref, keep_ref = refs[0], refs[1]
    if late == "half":
        m = n // 2
        a, b = add(slice(0, m)), add(slice(m, n))
        keep_ref[...] = jnp.where(low, a, b)
        send_ref[:m] = jnp.where(low, b, a)
    else:
        m = n
        x = add(slice(0, n))
        keep_ref[...] = x
        if late == "full":
            send_ref[:m] = x
    if with_small:
        hi, lo = got_ref[n : n + NOTE // 2], got_ref[n + NOTE // 2 :]
        small = small_ref[...] + (hi.astype(f32) + lo.astype(f32))
        refs[2][...] = small
        if send_ref.shape[0] > m:
            put_small(send_ref, m, small)


class Reduction:
    def __init__(self, links, send, keep, small=None):
        self.kind = None
        self.links, self.send, self.x, self.small = links, send, keep, small
        self.plan = (
            [("core", None)]
            + [("half", p) for p in links.near]
            + [("full", p) for p in links.far]
            + [("join", p) for p in links.near[::-1]]
            + [("last", None)]
        )

    def start(self, *after):
        links = self.links
        self.kind, self.pair = self.plan.pop(0)
        if after:
            self.send, *after = beside(self.send, *after)
        self.got = links.core(self.send) if self.pair is None else links.across(self.send, self.pair)
        return after

    def end(self):
        kind, x, links = self.kind, self.x, self.links
        if kind == "last":
            return
        n, d = x.shape
        shape = jax.ShapeDtypeStruct
        late, pair = self.plan[0]
        if kind == "join":
            v, outs = links.signs[self.pair], [shape((2 * n, d), bf16)]
        else:
            v = links.signs[pair] if late == "half" else links.any
            m = n // 2 if late == "half" else n
            more = NOTE if self.small is not None and late in ("half", "full") else 0
            outs = [shape((m + more if late in ("half", "full") else NOTE, d), bf16), shape((m, d), bf16)]
        args = [v, x, self.got]
        with_small = self.small is not None and kind != "join"
        if with_small:
            args.append(self.small)
            outs.append(shape(self.small.shape, f32))
        out = pl.pallas_call(
            functools.partial(hop_kernel, kind, late, with_small),
            in_specs=[pl.BlockSpec(memory_space=pltpu.SMEM)] + [pl.BlockSpec(memory_space=pltpu.VMEM)] * (len(args) - 1),
            out_specs=[pl.BlockSpec(memory_space=pltpu.VMEM)] * len(outs),
            out_shape=outs,
            compiler_params=params(HOP_VMEM),
            cost_estimate=cost(1.0),
            name="hop",
        )(*args)
        if kind == "join":
            self.send = self.x = out[0]
            return
        self.x = out[1]
        self.send = out[0] if late in ("half", "full") else self.x
        if with_small:
            self.small = out[2]


def beside(*values):
    return lax.optimization_barrier(values)


def body(
    links, image_in, img_gains, img_shifts, img_qkv, img_out, img_up, img_down, text_in, lengths, valid,
    txt_gains, txt_shifts, txt_qkv, txt_out, txt_up, txt_down, log_scale,
):
    dp, bits = links.dp, links.bits
    pairs, txt, d = text_in.shape
    ff = txt_up.shape[1]
    tokens = pairs * txt
    scale = jnp.exp(log_scale).reshape(1)
    rep = lax.axis_index("rep").astype(jnp.int32).reshape(1)
    order = links.gather_order

    own_valid = valid.astype(f32)[None, :]
    flen = lengths.astype(f32)[:, None]
    key_ok = (jnp.arange(txt)[None, :] < lengths[:, None]).astype(f32).reshape(tokens // LANES, LANES)

    xt = image_in.transpose(1, 0, 2)
    place = sum(links.bit(order[i]) << i for i in range(bits)).astype(jnp.int32).reshape(1)
    signs = [links.bit(pair).astype(jnp.int32).reshape(1) for pair in links.near]
    xt, flen, key_ok, own_valid, scale, rep, place, *signs = beside(
        xt, flen, key_ok, own_valid, scale, rep, place, *signs
    )
    links.signs = dict(zip(links.near, signs))
    links.any = rep
    other_valid = links.core(own_valid)
    image_args = (valid[None, :], img_gains, img_shifts, img_qkv, img_out, img_up, img_down)
    emb = image_embed(xt, *image_args, 0, pairs, True)
    text_args = (txt_gains, txt_shifts, txt_qkv, txt_out, txt_up, txt_down)
    text_x, emb = beside(text_in.reshape(tokens, d), emb)
    steps, pieces = list(order), 4
    a, held = emb[None], []
    for piece in range(pieces):
        if steps:
            got = links.across(a, steps.pop(0))
        held = list(text_forward(piece, pieces, held, text_x, key_ok, flen, *text_args, txt))
        if steps:
            text_x, got, held[-1] = beside(text_x, got, held[-1])
            a = jnp.concatenate([a, got], 0)
    while steps:
        got = links.across(a, steps.pop(0))
        if steps:
            a = jnp.concatenate([a, got], 0)
    n1, qkv, probs, att, n2, slope, stat, hpool, u, text_emb = held

    scores, images, col, okay, row = pair_scores(
        place, text_emb, links.core(text_emb), own_valid, other_valid, scale, a, got
    )
    swap = links.core(row)
    for pair in order[:-1]:
        col = col + links.across(col, pair)
    col_got = links.across(col, order[-1])
    part, other, sums = pair_gradients(dp, scale, scores, images, col, col_got, okay, row, swap, text_emb, emb)
    back = links.core(other)

    ffn_send, ffn_keep, gd, dh = backward_up(scale, rep, part, back, row, swap, emb, u, flen, hpool, n2, slope, txt_down, txt)
    first = Reduction(links, ffn_send, ffn_keep)
    first.start()
    gmid, datt, dwo, gain2 = backward_middle(
        gd, dh, flen, n2, slope, stat, att, txt_gains, txt_shifts, txt_up, txt_out, txt
    )
    held = []
    for piece in range(2):
        datt, first.got, *held = beside(datt, first.got, *held)
        first.end()
        first.start()
        held = list(backward_attention(
            piece, 2, held, rep, datt, qkv, probs, n1, dwo, gain2, sums, txt_gains, txt_shifts, txt_qkv
        ))
    gq, att_send, att_keep, small = held
    att_send, first.got = beside(att_send, first.got)
    second = Reduction(links, att_send, att_keep, small)
    dx, done = [], []

    def inputs(piece, stream):
        gq_now, stream.x = beside(gq, stream.x)
        dx[:] = [backward_input(piece, 2, dx, gq_now, gmid, n1, stat, txt_gains, txt_shifts, txt_qkv)]

    other = {first: second, second: first}
    far = len(links.far)
    for act, stream in (
        [("s", second), ("e", first), ("s", first), ("e", second), ("s", second), ("i", 0), ("e", second), ("s", second)]
        + [("e", first), ("s", first), ("e", second), ("s", second), ("i", 1), ("e", second), ("s", second)]
        + [("e", first), ("s", first), ("e", second), ("s", second), ("e", first), ("s", first)] * (far > 0)
    ):
        if act == "i":
            inputs(stream, second)
        elif act == "e":
            stream.end()
        elif stream.plan:
            if stream is second and second.kind is None:
                stream.start()
            else:
                other[stream].x, *dx[:] = stream.start(other[stream].x, *dx)
    while first.plan or second.plan:
        for stream in (second, first):
            if stream.plan:
                stream.end()
                stream.start()
    grad_down, grad_up = finish(
        rep, first.x, first.got, [(ff, d), (d, ff)], [(0, ff, 0, 0, 0)] + [(ff + i * d, d, 1, 0, i * d) for i in range(ff // d)]
    )
    grad_qkv, grad_out = finish(
        rep, second.x, second.got, [(d, 3 * d), (d, d)], [(i * d, d, 0, 0, i * d) for i in range(3)] + [(3 * d, d, 1, 0, 0)]
    )
    small, dx = second.small, dx[0]
    return (
        small[4, 0],
        small[0:2],
        small[2:4],
        grad_qkv,
        grad_out,
        grad_up,
        grad_down,
        small[5, 0],
        dx.reshape(pairs, txt, d),
    )


def solution(mesh):
    both = ("dp", "rep")
    deep = P(both, None, None)
    in_specs = (deep,) + (P(),) * 6 + (deep, P(both), P(both)) + (P(),) * 7
    out_specs = (P(),) * 8 + (deep,)
    return jax.shard_map(
        functools.partial(body, Links(mesh)), mesh=mesh, in_specs=in_specs, out_specs=out_specs, check_vma=False
    )
```

```python
import functools
import jax
import jax.numpy as jnp
from jax import lax
from jax.experimental import pallas as pl
from jax.experimental.pallas import tpu as pltpu
from jax.sharding import PartitionSpec as P

HEAD = 64
LANES = 128
f32 = jnp.float32
bf16 = jnp.bfloat16
GELU_C = 0.7978845608028654
GELU_A = 0.044715
SHIFT = 50.0
SAFE = 80.0
NOTE = 16
PITCH = 8
VMEM = 60 * 1024 * 1024
HOP_VMEM = 12 * 1024 * 1024


def dot(a, b):
    return jnp.dot(a, b, preferred_element_type=f32)


def dot_nt(a, b):
    return lax.dot_general(a, b, (((1,), (1,)), ((), ())), preferred_element_type=f32)


def dot_tn(a, b):
    return lax.dot_general(a, b, (((0,), (0,)), ((), ())), preferred_element_type=f32)


def norm_parts(x):
    mu = jnp.mean(x, -1, keepdims=True)
    c = x - mu
    rstd = lax.rsqrt(jnp.mean(c * c, -1, keepdims=True) + 1e-6)
    return c * rstd, rstd


def whole(a):
    return pl.BlockSpec(a.shape, lambda *_: (0,) * a.ndim)


def params(limit=VMEM):
    return pltpu.CompilerParams(vmem_limit_bytes=limit)


def cost(us):
    return pl.CostEstimate(flops=int(us * 1.1e9), bytes_accessed=0, transcendentals=0)


def split_bf16(v):
    hi = v.astype(bf16)
    return hi, (v - hi.astype(f32)).astype(bf16)


def count_rows(valid_ref, d):
    count = jnp.sum(valid_ref[...].astype(f32), 1, keepdims=True)
    return jnp.broadcast_to(count, (NOTE, d)).astype(bf16)


def stack_heads(a, low, zero):
    return jnp.concatenate([jnp.where(low, a, zero), jnp.where(low, zero, a)], 0)


def image_kernel(
    seqs, x_ref, old_ref, valid_ref, gains_ref, shifts_ref, wqkv_ref, wo_ref, wup_ref, wdown_ref, out_ref,
    qkv, att, sc, ec, hs, ms,
):
    tokens, _, d = x_ref.shape
    pad = -(-tokens // 8) * 8
    pitch = seqs + PITCH
    rows, pair = seqs * tokens, 2 * pad
    step, last = pl.program_id(0), pl.num_programs(0) - 1
    now, then = lax.rem(step, 2), lax.rem(step + 1, 2)
    ff = wup_ref.shape[1]
    hp = d // LANES

    @pl.when(step == 0)
    def _():
        qkv[:, tokens * pitch :] = jnp.zeros((3 * hp, (pad - tokens) * pitch, LANES), f32)

    low = lax.broadcasted_iota(jnp.int32, (pair, LANES), 1) < HEAD
    key_lane = lax.broadcasted_iota(jnp.int32, (pair, 2 * pair), 1)
    query_row = lax.broadcasted_iota(jnp.int32, (pair, 2 * pair), 0)
    first_head = key_lane < pair
    key_row = jnp.where(first_head, key_lane, key_lane - pair)
    second_image = key_row >= pad
    key_pos = jnp.where(second_image, key_row - pad, key_row)
    bias = jnp.where((key_pos < tokens) & (second_image == (query_row >= pad)), 0.0, -1e30)
    zero, one = jnp.zeros((pair, LANES), bf16), jnp.ones((pair, LANES), bf16)
    ones = stack_heads(one, low, zero)
    tiles = [(b, p) for b in range(seqs // 2) for p in range(hp)]

    def pick(j, b):
        return jnp.concatenate([qkv[j, pl.ds(2 * b + i, pad, stride=pitch), :] for i in range(2)], 0).astype(bf16)

    def attend(b, p, e):
        v = stack_heads(pick(2 * hp + p, b), low, zero)
        o = dot(e, jnp.concatenate([v, ones], 1))
        o = o[:, :LANES] / o[:, LANES:]
        for i in range(2):
            att[now, p, pl.ds(2 * b + i, pad, stride=pitch), :] = o[i * pad : (i + 1) * pad]

    def project(n1, c):
        r = dot(n1, wqkv_ref[:, c * d : (c + 1) * d])
        r = r * HEAD**-0.5 if c == 0 else r
        for p in range(hp):
            for t in range(tokens):
                qkv[c * hp + p, t * pitch : t * pitch + seqs] = r[t * seqs : (t + 1) * seqs, p * LANES : (p + 1) * LANES]

    def attention():
        x = x_ref[...].astype(f32).reshape(rows, d)
        n1 = (norm_parts(x)[0] * gains_ref[0:1, :] + shifts_ref[0:1, :]).astype(bf16)
        for c in range(3):
            project(n1, c)
            yield
        big = jnp.zeros((pair, 2 * pair), f32)
        for b, p in tiles:
            s = dot_nt(pick(p, b), stack_heads(pick(hp + p, b), low, zero))
            big = jnp.maximum(big, jnp.abs(s))
            sc[b * hp + p] = s
        yield
        for i in range(len(tiles)):
            ec[i] = jnp.exp(sc[i] + bias).astype(bf16)
        yield
        for b, p in tiles:
            attend(b, p, ec[b * hp + p])
        yield big

    def recheck(big):
        @pl.when(jnp.logical_not(jnp.max(big) < SAFE))
        def _():
            for b in range(seqs // 2):

                @pl.loop(0, hp)
                def _(p):
                    s = sc[b * hp + p] + bias
                    top0 = jnp.max(jnp.where(first_head, s, -2e30), -1, keepdims=True)
                    top1 = jnp.max(jnp.where(first_head, -2e30, s), -1, keepdims=True)
                    attend(b, p, jnp.exp(s - jnp.where(first_head, top0, top1)).astype(bf16))

    def forward():
        attended = jnp.concatenate(
            [jnp.concatenate([att[then, p, t * pitch : t * pitch + seqs] for p in range(hp)], 1) for t in range(tokens)], 0
        ).astype(bf16)
        mid = old_ref[...].astype(f32).reshape(rows, d) + dot(attended, wo_ref[...])
        at = pl.ds(pl.multiple_of((step - 1) * seqs, seqs), seqs)
        ms[at, :] = jnp.sum(mid.reshape(tokens, seqs, d), 0)
        n2 = (norm_parts(mid)[0] * gains_ref[1:2, :] + shifts_ref[1:2, :]).astype(bf16)
        yield
        chunk = ff // 2
        for c in range(0, ff, chunk):
            v = dot(n2, wup_ref[:, c : c + chunk])
            t = jnp.tanh(v * (GELU_C + (GELU_C * GELU_A) * (v * v)))
            h = (0.5 * v) * (1.0 + t)
            hs[at, c : c + chunk] = jnp.sum(h.reshape(tokens, seqs, chunk), 0)
            yield

    def run(*works):
        works, given = list(works), None
        while works:
            for w in list(works):
                try:
                    value = next(w)
                    given = given if value is None else value
                except StopIteration:
                    works.remove(w)
        return given

    @pl.when(step == 0)
    def _():
        recheck(run(attention()))

    @pl.when((step > 0) & (step < last))
    def _():
        recheck(run(attention(), forward()))

    @pl.when(step == last)
    def _():
        run(forward())
        hi, lo = split_bf16(hs[...] * (1.0 / tokens))
        u = ms[...] * (1.0 / tokens) + dot(hi, wdown_ref[...]) + dot(lo, wdown_ref[...])
        n = u.shape[0]
        out_ref[:n] = (u * lax.rsqrt(jnp.sum(u * u, -1, keepdims=True) + 1e-6)).astype(bf16)
        if out_ref.shape[0] > n:
            out_ref[n:] = count_rows(valid_ref, d)


def image_embed(xt, valid, gains, shifts, wqkv, wo, wup, wdown, start, count, note, seqs=16):
    tokens, _, d = xt.shape
    ff = wup.shape[1]
    pad = -(-tokens // 8) * 8
    pitch = seqs + PITCH
    tiles = seqs // 2 * (d // LANES)
    first, groups = start // seqs, count // seqs
    rows = count + (NOTE if note else 0)
    return pl.pallas_call(
        functools.partial(image_kernel, seqs),
        grid=(groups + 1,),
        in_specs=[
            pl.BlockSpec((tokens, seqs, d), lambda i: (0, jnp.minimum(i, groups - 1) + first, 0)),
            pl.BlockSpec((tokens, seqs, d), lambda i: (0, jnp.maximum(i - 1, 0) + first, 0)),
        ]
        + [whole(a) for a in (valid, gains, shifts, wqkv, wo, wup, wdown)],
        out_specs=pl.BlockSpec((rows, d), lambda i: (0, 0)),
        out_shape=jax.ShapeDtypeStruct((rows, d), bf16),
        scratch_shapes=[
            pltpu.VMEM((3 * d // LANES, pitch * pad, LANES), f32),
            pltpu.VMEM((2, d // LANES, pitch * pad, LANES), f32),
            pltpu.VMEM((tiles, 2 * pad, 4 * pad), f32),
            pltpu.VMEM((tiles, 2 * pad, 4 * pad), bf16),
            pltpu.VMEM((count, ff), f32),
            pltpu.VMEM((count, d), f32),
        ],
        compiler_params=params(56 * 1024 * 1024),
        cost_estimate=cost(0.45 * count),
        name="image_block",
    )(xt, xt, valid, gains, shifts, wqkv, wo, wup, wdown)


def real_tokens(length, txt):
    seqs = length.shape[0]
    spread = jnp.broadcast_to(length[:, None, :], (seqs, txt, 1)).reshape(seqs * txt, 1)
    pos = lax.broadcasted_iota(jnp.int32, (seqs * txt, 1), 0) % txt
    return jnp.where(pos.astype(f32) < spread, 1.0, 0.0)


def text_forward_kernel(
    txt, held, x_ref, flen_ref, gains_ref, shifts_ref, wqkv_ref, wo_ref, wup_ref, wdown_ref, *refs,
):
    (n1_ref, qkv_ref, probs_ref, att_ref, n2_ref, slope_ref, stat_ref, hpool_ref, u_ref, emb_ref, ms, sc, ec) = refs[held:]
    step = pl.program_id(0)
    rows, d = x_ref.shape
    ff = wup_ref.shape[1]
    seqs = rows // txt
    x = x_ref[...].astype(f32)
    xhat1, rstd1 = norm_parts(x)
    n1 = (xhat1 * gains_ref[0:1, :] + shifts_ref[0:1, :]).astype(bf16)
    n1_ref[...] = n1
    qkv_ref[:, :d] = (dot(n1, wqkv_ref[:, :d]) * HEAD**-0.5).astype(bf16)
    qkv_ref[:, d:] = dot(n1, wqkv_ref[:, d:]).astype(bf16)
    low = lax.broadcasted_iota(jnp.int32, (LANES, LANES), 1) < HEAD
    same = (
        lax.broadcasted_iota(jnp.int32, (LANES, LANES), 0) // txt
        == lax.broadcasted_iota(jnp.int32, (LANES, LANES), 1) // txt
    )
    zero = jnp.zeros((LANES, LANES), bf16)
    hp = d // LANES
    tiles = [(g, p) for g in range(rows // LANES) for p in range(hp)]
    group = LANES // txt
    key_lane = lax.broadcasted_iota(jnp.int32, (group, LANES), 1)
    owner = key_lane // txt == lax.broadcasted_iota(jnp.int32, (group, LANES), 0)
    key_pos = (key_lane[0:1] % txt).astype(f32)

    def attend(g, p, probs):
        r = slice(g * LANES, (g + 1) * LANES)
        probs_ref[g * hp + p] = probs
        v = qkv_ref[r, 2 * d + p * LANES : 2 * d + (p + 1) * LANES]
        att_ref[r, p * LANES : (p + 1) * LANES] = dot(probs, stack_heads(v, low, zero)).astype(bf16)

    def share(s, top):
        halves = []
        for h in range(2):
            sh = s[:, h * LANES : (h + 1) * LANES]
            e = jnp.exp(sh - jnp.max(sh, -1, keepdims=True)) if top else jnp.exp(sh)
            halves.append(e / jnp.sum(e, -1, keepdims=True))
        return jnp.concatenate(halves, 1).astype(bf16)

    big = jnp.zeros((LANES, 2 * LANES), f32)
    for g, p in tiles:
        r = slice(g * LANES, (g + 1) * LANES)
        near = pl.ds(pl.multiple_of(step * seqs + g * group, group), group)
        length = jnp.sum(jnp.where(owner, flen_ref[near, :], 0.0), 0, keepdims=True)
        bias = jnp.where(same & (key_pos < length), 0.0, -1e30)
        q = qkv_ref[r, p * LANES : (p + 1) * LANES]
        k = qkv_ref[r, d + p * LANES : d + (p + 1) * LANES]
        s = dot_nt(q, stack_heads(k, low, zero))
        big = jnp.maximum(big, jnp.abs(s))
        sc[g * hp + p] = s + jnp.concatenate([bias, bias], 1)
    for g, p in tiles:
        ec[g * hp + p] = share(sc[g * hp + p], False)
    for g, p in tiles:
        attend(g, p, ec[g * hp + p])

    @pl.when(jnp.logical_not(jnp.max(big) < SAFE))
    def _():
        for g, p in tiles:
            attend(g, p, share(sc[g * hp + p], True))

    mid = x + dot(att_ref[...], wo_ref[...])
    xhat2, rstd2 = norm_parts(mid)
    lane = lax.broadcasted_iota(jnp.int32, (rows, LANES), 1)
    hi1, hi2 = rstd1.astype(bf16).astype(f32), rstd2.astype(bf16).astype(f32)
    stat = jnp.where(lane < 64, jnp.where(lane < 32, hi1, rstd1 - hi1), jnp.where(lane < 96, hi2, rstd2 - hi2))
    stat_ref[...] = stat.astype(bf16)
    at = pl.ds(pl.multiple_of(step * seqs, seqs), seqs)
    keep = real_tokens(flen_ref[at, :], txt)
    n2 = ((xhat2 * gains_ref[1:2, :] + shifts_ref[1:2, :]) * keep).astype(bf16)
    n2_ref[...] = n2
    ms[at, :] = jnp.sum((mid * keep).reshape(seqs, txt, d), 1)
    chunk = 512
    for c in range(0, ff, chunk):
        v = dot(n2, wup_ref[:, c : c + chunk])
        v2 = v * v
        t = jnp.tanh(v * (GELU_C + (GELU_C * GELU_A) * v2))
        half = 0.5 + 0.5 * t
        h = v * half
        slope = half + h * (1.0 - t) * (GELU_C + (3.0 * GELU_C * GELU_A) * v2)
        slope_ref[:, c : c + chunk] = (slope * keep).astype(bf16)
        hpool_ref[at, c : c + chunk] = jnp.sum(h.reshape(seqs, txt, chunk), 1)

    @pl.when(step == pl.num_programs(0) - 1)
    def _():
        hi, lo = split_bf16(hpool_ref[...])
        pooled = ms[...] + dot(hi, wdown_ref[...]) + dot(lo, wdown_ref[...])
        u = pooled / flen_ref[...]
        u_ref[...] = u
        emb_ref[...] = (u * lax.rsqrt(jnp.sum(u * u, -1, keepdims=True) + 1e-6)).astype(bf16)


def text_forward(piece, pieces, held, x, flen, gains, shifts, wqkv, wo, wup, wdown, txt, rows=512):
    total, d = x.shape
    ff = wup.shape[1]
    pairs = total // txt
    hp = d // LANES
    part = pairs // pieces
    steps = total // pieces // rows
    first = piece * steps
    block = lambda *tail: pl.BlockSpec((rows,) + tail, lambda i: (i + first,) + (0,) * len(tail))
    still = lambda *shape: pl.BlockSpec(shape, lambda i: (piece, 0))
    shape = jax.ShapeDtypeStruct
    args = (x, flen, gains, shifts, wqkv, wo, wup, wdown)
    return pl.pallas_call(
        functools.partial(text_forward_kernel, txt, len(held)),
        grid=(steps,),
        in_specs=[
            block(d), still(part, 1)
        ]
        + [whole(a) for a in args[2:]]
        + [pl.BlockSpec(memory_space=pl.ANY)] * len(held),
        out_specs=[
            block(d), block(3 * d), pl.BlockSpec((rows // LANES * hp, LANES, 2 * LANES), lambda i: (i + first, 0, 0)),
            block(d), block(d), block(ff), block(LANES), still(part, ff), still(part, d), still(part, d),
        ],
        out_shape=[
            shape((total, d), bf16), shape((total, 3 * d), bf16), shape((total // LANES * hp, LANES, 2 * LANES), bf16),
            shape((total, d), bf16), shape((total, d), bf16), shape((total, ff), bf16), shape((total, LANES), bf16),
            shape((pairs, ff), f32), shape((pairs, d), f32), shape((pairs, d), bf16),
        ],
        input_output_aliases={len(args) + i: i for i in range(len(held))},
        scratch_shapes=[
            pltpu.VMEM((part, d), f32),
            pltpu.VMEM((rows // LANES * hp, LANES, 2 * LANES), f32),
            pltpu.VMEM((rows // LANES * hp, LANES, 2 * LANES), bf16),
        ],
        compiler_params=params(18 * 1024 * 1024),
        cost_estimate=cost(0.013 * total / pieces),
        name="text_forward",
    )(*args, *held)


def scores_kernel(
    group, place_ref, own_ref, other_ref, own_valid_ref, other_valid_ref, scale_ref, a0_ref, a1_ref,
    s_ref, all_ref, col_out, okay_out, row_out,
):
    step = pl.program_id(0)
    pairs = own_ref.shape[0]
    scale = scale_ref[0]
    row = lax.broadcasted_iota(jnp.int32, (pairs, 1), 0).astype(f32)
    mask = [jnp.where(row < jnp.sum(v[...], 1, keepdims=True), 1.0, 0.0) for v in (own_valid_ref, other_valid_ref)]
    mask = jnp.concatenate(mask, 0)
    inner = lax.rem(place_ref[0], group)
    late = lax.bitwise_xor(step, lax.div(place_ref[0], group)) >= pl.num_programs(0) // 2
    texts = jnp.concatenate([own_ref[...], other_ref[...]], 0)

    @pl.when(step == 0)
    def _():
        row_out[...] = jnp.zeros_like(row_out)
        row_out[:, 3:4] = mask

    lane = lax.broadcasted_iota(jnp.int32, (1, pairs), 1).astype(f32)
    for k in range(group):
        at = lax.bitwise_xor(k, inner)
        cols = slice(k * pairs, (k + 1) * pairs)
        a = jnp.where(late, a1_ref[at], a0_ref[at])
        images = a[:pairs]
        count = a[pairs : pairs + 1, 0:1].astype(f32)
        okay = jnp.where(lane < count, 1.0, 0.0)
        okay_out[0:1, cols] = okay
        all_ref[cols, :] = images
        s = scale * dot_nt(texts, images)
        s_ref[:, cols] = s
        up = jnp.exp(s - SHIFT)
        down = jnp.exp(jnp.minimum(s, 0.0) + SHIFT)
        col_out[0:1, cols] = jnp.sum(up * mask, 0, keepdims=True)
        col_out[1:2, cols] = jnp.sum(down * mask, 0, keepdims=True)
        row_out[:, 0:1] += jnp.sum(up * okay, 1, keepdims=True)
        row_out[:, 1:2] += jnp.sum(down * okay, 1, keepdims=True)
        row_out[:, 2:3] += jnp.broadcast_to(count, (2 * pairs, 1))


def pair_scores(place, own, other, own_valid, other_valid, scale, a0, a1):
    slots, _, d = a0.shape
    pairs = own.shape[0]
    group = min(8, slots)
    groups = slots // group
    cols = group * pairs
    keep = lambda *_: (0, 0)
    turn = lambda i, s: (lax.rem(lax.bitwise_xor(i, lax.div(s[0], group)), groups), 0, 0)
    still = lambda a: pl.BlockSpec(a.shape, keep)
    shape = jax.ShapeDtypeStruct
    return pl.pallas_call(
        functools.partial(scores_kernel, group),
        grid_spec=pltpu.PrefetchScalarGridSpec(
            num_scalar_prefetch=1,
            grid=(2 * groups,),
            in_specs=[still(own), still(other), still(own_valid), still(other_valid), pl.BlockSpec(memory_space=pltpu.SMEM)]
            + [pl.BlockSpec((group,) + a.shape[1:], turn) for a in (a0, a1)],
            out_specs=[
                pl.BlockSpec((2 * pairs, cols), lambda i, s: (0, i)),
                pl.BlockSpec((cols, d), lambda i, s: (i, 0)),
                pl.BlockSpec((2, cols), lambda i, s: (0, i)),
                pl.BlockSpec((1, cols), lambda i, s: (0, i)),
                pl.BlockSpec((2 * pairs, 4), keep),
            ],
        ),
        out_shape=[
            shape((2 * pairs, 2 * groups * cols), f32), shape((2 * groups * cols, d), bf16),
            shape((2, 2 * groups * cols), f32), shape((1, 2 * groups * cols), f32), shape((2 * pairs, 4), f32),
        ],
        compiler_params=params(12 * 1024 * 1024),
        cost_estimate=cost(4.0),
        name="pair_scores",
    )(place, own, other, own_valid, other_valid, scale, a0, a1)


def log_sum(up, down):
    fine = up >= 1.9287498479639178e-22
    return jnp.where(
        fine, jnp.log(jnp.where(fine, up, 1.0)) + SHIFT, jnp.log(jnp.where(fine, 1.0, down)) - SHIFT
    )


def gradient_kernel(
    dp, scale_ref, s_ref, all_ref, col_ref, got_ref, okay_ref, row_ref, swap_ref, text_ref, a_ref,
    grad_ref, back_ref, loss_ref,
):
    step = pl.program_id(0)
    pairs = text_ref.shape[0]
    row = row_ref[...] + jnp.concatenate([swap_ref[pairs:], swap_ref[:pairs]], 0)
    factor = 0.5 / row[0:1, 2:3]
    mask = row_ref[:, 3:4]
    okay = okay_ref[...]
    row_lse = log_sum(row[:, 0:1], row[:, 1:2])
    col = col_ref[...] + got_ref[...]
    col_lse = log_sum(col[0:1, :], col[1:2, :])

    @pl.when(step == 0)
    def _():
        grad_ref[...] = jnp.zeros_like(grad_ref)
        back_ref[...] = jnp.zeros_like(back_ref)
        loss_ref[...] = jnp.zeros_like(loss_ref)
        t = text_ref[...].astype(f32) * a_ref[:pairs].astype(f32)
        diag = scale_ref[0] * jnp.sum(t, -1, keepdims=True)
        m = mask[:pairs]
        loss_ref[0:1, 0:1] = factor * jnp.sum(m * (row_lse[:pairs] - 2.0 * diag), 0, keepdims=True)
        loss_ref[1:2, 0:1] = -2.0 * factor * jnp.sum(m * diag, 0, keepdims=True)

    s = s_ref[...]
    g = jnp.exp(jnp.minimum(s - row_lse, 1.0)) + jnp.exp(jnp.minimum(s - col_lse, 1.0))
    g = g * ((factor * mask) * okay)
    grad = dot(g.astype(bf16), all_ref[...])
    grad_ref[...] += grad[:pairs]
    back_ref[...] += grad[pairs:]
    cols = jnp.sum(jnp.where(okay > 0, col_lse, 0.0), 1, keepdims=True)
    loss_ref[0:1, 0:1] += factor * (cols * (1.0 / dp))
    loss_ref[1:2, 0:1] += jnp.sum(jnp.sum(g * s, 0, keepdims=True), 1, keepdims=True)


def pair_gradients(dp, scale, scores, images, col, got, okay, row, swap, texts, a):
    pairs, d = texts.shape
    cols = min(8, dp) * pairs
    still = lambda *shape: pl.BlockSpec(shape, lambda i: (0, 0))
    shape = jax.ShapeDtypeStruct
    return pl.pallas_call(
        functools.partial(gradient_kernel, dp),
        grid=(dp * pairs // cols,),
        in_specs=[
            pl.BlockSpec(memory_space=pltpu.SMEM),
            pl.BlockSpec((2 * pairs, cols), lambda i: (0, i)),
            pl.BlockSpec((cols, d), lambda i: (i, 0)),
            pl.BlockSpec((2, cols), lambda i: (0, i)),
            pl.BlockSpec((2, cols), lambda i: (0, i)),
            pl.BlockSpec((1, cols), lambda i: (0, i)),
        ]
        + [whole(x) for x in (row, swap, texts, a)],
        out_specs=[still(pairs, d), still(pairs, d), still(8, LANES)],
        out_shape=[shape((pairs, d), f32), shape((pairs, d), f32), shape((8, LANES), f32)],
        compiler_params=params(12 * 1024 * 1024),
        cost_estimate=cost(3.0),
        name="pair_gradients",
    )(scale, scores, images, col, got, okay, row, swap, texts, a)


def spread_rows(a, txt):
    seqs, width = a.shape
    return jnp.broadcast_to(a[:, None, :], (seqs, txt, width)).reshape(seqs * txt, width)


def backward_up_kernel(
    txt, scale_ref, rep_ref, part_ref, back_ref, row_ref, swap_ref, a_ref, u_ref, len_ref, hpool_ref, n2_ref, slope_ref,
    wdown_ref, send_ref, keep_ref, gd_ref, dh_ref, down, acc,
):
    step = pl.program_id(0)
    rows, d = n2_ref.shape
    ff = slope_ref.shape[1]
    seqs = rows // txt

    @pl.when(step == 0)
    def _():
        pairs = part_ref.shape[0]
        scale = scale_ref[0]
        factor = 0.5 / (row_ref[0:1, 2:3] + swap_ref[0:1, 2:3])
        images = a_ref[:pairs].astype(f32)
        u = u_ref[...]
        r = lax.rsqrt(jnp.sum(u * u, -1, keepdims=True) + 1e-6)
        g = scale * (part_ref[...] + back_ref[...]) - (2.0 * scale) * (factor * row_ref[:pairs, 3:4]) * images
        du = (r * g - (r * r * r) * u * jnp.sum(u * g, -1, keepdims=True)) / len_ref[...]
        gd_ref[...] = du
        low = du.astype(bf16)
        dh_ref[...] = dot_nt(low, wdown_ref[...])
        hi, lo = split_bf16(hpool_ref[...])
        down[...] = (dot_tn(hi, low) + dot_tn(lo, low)).astype(bf16)
        acc[...] = jnp.zeros_like(acc)

    at = pl.ds(pl.multiple_of(step * seqs, seqs), seqs)
    chunk = 512
    for c in range(0, ff, chunk):
        cs = slice(c, c + chunk)
        grad_before = (spread_rows(dh_ref[at, cs], txt) * slope_ref[:, cs].astype(f32)).astype(bf16)
        acc[:, cs] += dot_tn(n2_ref[...], grad_before)

    @pl.when(step == pl.num_programs(0) - 1)
    def _():
        first = rep_ref[0] == 0
        for b in range(ff // d):
            r = slice(b * d, (b + 1) * d)
            up = acc[:, r].astype(bf16)
            keep_ref[r] = jnp.where(first, down[r], up)
            send_ref[r] = jnp.where(first, up, down[r])


def backward_up(scale, rep, part, back, row, swap, a, u, flen, hpool, n2, slope, wdown, txt, rows=512):
    tokens, d = n2.shape
    pairs, ff = hpool.shape
    block = lambda w: pl.BlockSpec((rows, w), lambda i: (i, 0))
    shape = jax.ShapeDtypeStruct
    smem = pl.BlockSpec(memory_space=pltpu.SMEM)
    outs = [shape((ff, d), bf16), shape((ff, d), bf16), shape((pairs, d), f32), shape((pairs, ff), f32)]
    return pl.pallas_call(
        functools.partial(backward_up_kernel, txt),
        grid=(tokens // rows,),
        in_specs=[smem, smem]
        + [whole(x) for x in (part, back, row, swap, a, u, flen, hpool)]
        + [block(d), block(ff), whole(wdown)],
        out_specs=[whole(x) for x in outs],
        out_shape=outs,
        scratch_shapes=[pltpu.VMEM((ff, d), bf16), pltpu.VMEM((d, ff), f32)],
        compiler_params=params(16 * 1024 * 1024),
        cost_estimate=cost(0.006 * tokens),
        name="backward_up",
    )(scale, rep, part, back, row, swap, a, u, flen, hpool, n2, slope, wdown)


def backward_middle_kernel(
    txt, gd_ref, dh_ref, len_ref, n2_ref, slope_ref, stat_ref, att_ref, gains_ref, shifts_ref, wup_ref, wo_ref,
    gmid_ref, datt_ref, dwo_ref, gain_ref, acc,
):
    step = pl.program_id(0)
    rows, d = n2_ref.shape
    ff = wup_ref.shape[1]

    @pl.when(step == 0)
    def _():
        acc[...] = jnp.zeros_like(acc)
        gain_ref[...] = jnp.zeros_like(gain_ref)

    dn2 = jnp.zeros((rows, d), f32)
    chunk = 512
    for c in range(0, ff, chunk):
        cs = slice(c, c + chunk)
        grad_before = (spread_rows(dh_ref[:, cs], txt) * slope_ref[:, cs].astype(f32)).astype(bf16)
        dn2 += dot_nt(grad_before, wup_ref[:, cs])
    xhat = (n2_ref[...].astype(f32) - shifts_ref[1:2, :]) / gains_ref[1:2, :]
    stat = stat_ref[...].astype(f32)
    gain_ref[0:1, :] += jnp.sum(dn2 * xhat, 0, keepdims=True)
    gain_ref[1:2, :] += jnp.sum(dn2, 0, keepdims=True)
    gn = dn2 * gains_ref[1:2, :]
    dmid = (stat[:, 64:65] + stat[:, 96:97]) * (
        gn - jnp.mean(gn, -1, keepdims=True) - xhat * jnp.mean(gn * xhat, -1, keepdims=True)
    )
    gmid = spread_rows(gd_ref[...], txt) * real_tokens(len_ref[...], txt) + dmid
    gmid_ref[...] = gmid
    branch = gmid.astype(bf16)
    acc[...] += dot_tn(att_ref[...], branch)
    datt_ref[...] = dot_nt(branch, wo_ref[...]).astype(bf16)

    @pl.when(step == pl.num_programs(0) - 1)
    def _():
        dwo_ref[...] = acc[...].astype(bf16)


def backward_middle(gd, dh, flen, n2, slope, stat, att, gains, shifts, wup, wo, txt, rows=512):
    tokens, d = n2.shape
    ff = wup.shape[1]
    block = lambda w: pl.BlockSpec((rows, w), lambda i: (i, 0))
    lead = lambda w: pl.BlockSpec((rows // txt, w), lambda i: (i, 0))
    shape = jax.ShapeDtypeStruct
    sums = [shape((d, d), bf16), shape((8, d), f32)]
    return pl.pallas_call(
        functools.partial(backward_middle_kernel, txt),
        grid=(tokens // rows,),
        in_specs=[lead(d), lead(ff), lead(1), block(d), block(ff), block(LANES), block(d)]
        + [whole(x) for x in (gains, shifts, wup, wo)],
        out_specs=[block(d), block(d)] + [whole(x) for x in sums],
        out_shape=[shape((tokens, d), f32), shape((tokens, d), bf16)] + sums,
        scratch_shapes=[pltpu.VMEM((d, d), f32)],
        compiler_params=params(16 * 1024 * 1024),
        cost_estimate=cost(0.006 * tokens),
        name="backward_middle",
    )(gd, dh, flen, n2, slope, stat, att, gains, shifts, wup, wo)


def backward_attention_kernel(
    held, last, rep_ref, datt_ref, qkv_ref, probs_ref, n1_ref, dwo_ref, gain2_ref, sums_ref, gains_ref, shifts_ref, wqkv_ref,
    *refs
):
    old_acc, old_flat = refs[1:3] if held else (None, None)
    gq_ref, *outs = refs[held:-4]
    acc, flat, sc, ec = refs[-4:]
    step = pl.program_id(0)
    rows, d = n1_ref.shape
    low = lax.broadcasted_iota(jnp.int32, (LANES, LANES), 1) < HEAD
    zero = jnp.zeros((LANES, LANES), bf16)

    @pl.when(step == 0)
    def _():
        acc[...] = old_acc[...] if held else jnp.zeros_like(acc)
        flat[...] = old_flat[...] if held else jnp.zeros_like(flat)

    hp = d // LANES
    tiles = [(g, p) for g in range(rows // LANES) for p in range(hp)]
    at = lambda g, p, part: (slice(g * LANES, (g + 1) * LANES), slice(part * d + p * LANES, part * d + (p + 1) * LANES))
    for g, p in tiles:
        sc[g * hp + p] = dot_nt(datt_ref[at(g, p, 0)], stack_heads(qkv_ref[at(g, p, 2)], low, zero))
    for g, p in tiles:
        i = g * hp + p
        probs = probs_ref[i].astype(f32)
        halves = []
        for h in range(2):
            hs = slice(h * LANES, (h + 1) * LANES)
            ph, dh = probs[:, hs], sc[i, :, hs]
            halves.append(ph * (dh - jnp.sum(ph * dh, -1, keepdims=True)))
        ec[i] = jnp.concatenate(halves, 1).astype(bf16)
    for g, p in tiles:
        dv = dot_tn(probs_ref[g * hp + p], datt_ref[at(g, p, 0)])
        gq_ref[at(g, p, 2)] = jnp.where(low, dv[:LANES], dv[LANES:]).astype(bf16)
    for g, p in tiles:
        keys = stack_heads(qkv_ref[at(g, p, 1)], low, zero)
        gq_ref[at(g, p, 0)] = (dot(ec[g * hp + p], keys) * HEAD**-0.5).astype(bf16)
    for g, p in tiles:
        dk = dot_tn(ec[g * hp + p], qkv_ref[at(g, p, 0)])
        gq_ref[at(g, p, 1)] = jnp.where(low, dk[:LANES], dk[LANES:]).astype(bf16)
    gq = gq_ref[...]
    acc[...] += dot_tn(n1_ref[...], gq)
    flat[0:1, :] += jnp.sum(gq.astype(f32), 0, keepdims=True)

    @pl.when(step == pl.num_programs(0) - 1)
    def _():
        if not last:
            outs[0][...] = acc[...]
            outs[1][...] = flat[...]
            return
        send_ref, keep_ref, small_ref = outs
        w = wqkv_ref[...]
        ones = jnp.ones((8, 3 * d), bf16)
        hi, lo = split_bf16(acc[...] * w.astype(f32))
        spread = dot_nt(ones, hi) + dot_nt(ones, lo)
        hi, lo = split_bf16(flat[...])
        dshift = (dot_nt(hi, w) + dot_nt(lo, w))[0:1]
        dgain = (spread[0:1] - shifts_ref[0:1, :] * dshift) / gains_ref[0:1, :]
        small = [dgain, gain2_ref[0:1, :], dshift, gain2_ref[1:2, :]]
        small += [jnp.broadcast_to(sums_ref[i : i + 1, 0:1], (1, d)) for i in range(2)]
        small = jnp.concatenate(small + [jnp.zeros((2, d), f32)], 0)
        small_ref[...] = small
        first = rep_ref[0] == 0
        parts = [acc[:, b * d : (b + 1) * d].astype(bf16) for b in range(3)] + [dwo_ref[...]]
        for b in range(2):
            keep_ref[b * d : (b + 1) * d] = jnp.where(first, parts[b], parts[b + 2])
            send_ref[b * d : (b + 1) * d] = jnp.where(first, parts[b + 2], parts[b])
        put_small(send_ref, 2 * d, small)


def backward_attention(piece, pieces, held, rep, datt, qkv, probs, n1, dwo, gain2, sums, gains, shifts, wqkv, rows=512):
    tokens, d = n1.shape
    steps = tokens // pieces // rows
    first = piece * steps
    last = piece == pieces - 1
    block = lambda w: pl.BlockSpec((rows, w), lambda i: (i + first, 0))
    shape = jax.ShapeDtypeStruct
    if last:
        outs = [shape((2 * d + NOTE, d), bf16), shape((2 * d, d), bf16), shape((8, d), f32)]
    else:
        outs = [shape((d, 3 * d), f32), shape((8, 3 * d), f32)]
    args = (rep, datt, qkv, probs, n1, dwo, gain2, sums, gains, shifts, wqkv)
    return pl.pallas_call(
        functools.partial(backward_attention_kernel, len(held), last),
        grid=(steps,),
        in_specs=[
            pl.BlockSpec(memory_space=pltpu.SMEM), block(d), block(3 * d),
            pl.BlockSpec((rows // LANES * (d // LANES), LANES, 2 * LANES), lambda i: (i + first, 0, 0)),
            block(d),
        ]
        + [whole(x) for x in args[5:]]
        + ([pl.BlockSpec(memory_space=pl.ANY)] + [whole(x) for x in held[1:]] if held else []),
        out_specs=[block(3 * d)] + [whole(x) for x in outs],
        out_shape=[shape((tokens, 3 * d), bf16)] + outs,
        input_output_aliases={len(args): 0} if held else {},
        scratch_shapes=[
            pltpu.VMEM((d, 3 * d), f32),
            pltpu.VMEM((8, 3 * d), f32),
            pltpu.VMEM((rows // LANES * (d // LANES), LANES, 2 * LANES), f32),
            pltpu.VMEM((rows // LANES * (d // LANES), LANES, 2 * LANES), bf16),
        ],
        compiler_params=params(16 * 1024 * 1024),
        cost_estimate=cost(0.009 * tokens / pieces),
        name="backward_attention",
    )(*args, *held)


def backward_input_kernel(gq_ref, gmid_ref, n1_ref, stat_ref, gains_ref, shifts_ref, wqkv_ref, *refs):
    dx_ref = refs[-1]
    gn = dot_nt(gq_ref[...], wqkv_ref[...]) * gains_ref[0:1, :]
    xhat = (n1_ref[...].astype(f32) - shifts_ref[0:1, :]) / gains_ref[0:1, :]
    stat = stat_ref[...].astype(f32)
    dx_ref[...] = gmid_ref[...] + (stat[:, 0:1] + stat[:, 32:33]) * (
        gn - jnp.mean(gn, -1, keepdims=True) - xhat * jnp.mean(gn * xhat, -1, keepdims=True)
    )


def backward_input(piece, pieces, held, gq, gmid, n1, stat, gains, shifts, wqkv, rows=512):
    tokens, d = gmid.shape
    steps = tokens // pieces // rows
    block = lambda w: pl.BlockSpec((rows, w), lambda i: (i + piece * steps, 0))
    args = (gq, gmid, n1, stat, gains, shifts, wqkv)
    return pl.pallas_call(
        backward_input_kernel,
        grid=(steps,),
        in_specs=[block(3 * d), block(d), block(d), block(LANES), whole(gains), whole(shifts), whole(wqkv)]
        + [pl.BlockSpec(memory_space=pl.ANY)] * len(held),
        out_specs=block(d),
        out_shape=jax.ShapeDtypeStruct((tokens, d), f32),
        input_output_aliases={len(args): 0} if held else {},
        compiler_params=params(16 * 1024 * 1024),
        cost_estimate=cost(0.004 * tokens / pieces),
        name="backward_input",
    )(*args, *held)


def finish_kernel(places, rep_ref, own_ref, got_ref, *out_refs):
    first = rep_ref[0] == 0
    for out, top, left, begin, n, part in places:
        a = own_ref[begin : begin + n, :]
        b = got_ref[begin : begin + n, :]
        mine = first if part == 0 else jnp.logical_not(first)
        out_refs[out][top : top + n, left : left + a.shape[1]] = jnp.where(mine, a, b).astype(f32)


def finish(rep, own, got, shapes, segments):
    half = own.shape[0]
    places = []
    for row, count, out, top, left in segments:
        while count:
            part, begin = divmod(row, half)
            n = min(count, half - begin)
            places.append((out, top, left, begin, n, part))
            row, top, count = row + n, top + n, count - n
    outs = [jax.ShapeDtypeStruct(s, f32) for s in shapes]
    return pl.pallas_call(
        functools.partial(finish_kernel, places),
        grid=(1,),
        in_specs=[pl.BlockSpec(memory_space=pltpu.SMEM), whole(own), whole(got)],
        out_specs=[whole(x) for x in outs],
        out_shape=outs,
        compiler_params=params(16 * 1024 * 1024),
        cost_estimate=cost(3.0),
        name="finish",
    )(rep, own, got)


class Links:
    def __init__(self, mesh):
        self.dp, self.rep = mesh.shape["dp"], mesh.shape["rep"]
        self.bits = (self.dp - 1).bit_length()
        assert self.dp == 1 << self.bits and self.rep == 2
        near, far = list(range(min(2, self.bits))), list(range(2, self.bits))
        turn = lambda bits: list(zip(bits, bits[::-1]))
        self.near, self.far = turn(near), turn(far)
        self.gather_order = [(b, b) for b in far[::-1]] + self.near

    def bit(self, pair):
        place = lax.axis_index("dp")
        return jnp.where(lax.axis_index("rep") == 0, (place >> pair[0]) & 1, (place >> pair[1]) & 1)

    def across(self, x, pair):
        moves = [(2 * i + r, 2 * (i ^ (1 << pair[r])) + r) for i in range(self.dp) for r in range(2)]
        return lax.ppermute(x, ("dp", "rep"), moves)

    def core(self, x):
        return lax.ppermute(x, "rep", [(0, 1), (1, 0)])


def put_small(ref, at, small):
    hi, lo = split_bf16(small)
    ref[at : at + NOTE] = jnp.concatenate([hi, lo], 0)


def hop_kernel(kind, late, with_small, v_ref, x_ref, got_ref, *refs):
    n, d = x_ref.shape
    refs = list(refs)
    small_ref = refs.pop(0) if with_small else None
    low = v_ref[0] == 0
    if kind == "join":
        x, got = x_ref[...], got_ref[...]
        refs[0][:n] = jnp.where(low, x, got)
        refs[0][n:] = jnp.where(low, got, x)
        return
    add = lambda r: (x_ref[r].astype(f32) + got_ref[r].astype(f32)).astype(bf16)
    send_ref, keep_ref = refs[0], refs[1]
    if late == "half":
        m = n // 2
        a, b = add(slice(0, m)), add(slice(m, n))
        keep_ref[...] = jnp.where(low, a, b)
        send_ref[:m] = jnp.where(low, b, a)
    else:
        m = n
        x = add(slice(0, n))
        keep_ref[...] = x
        if late == "full":
            send_ref[:m] = x
    if with_small:
        hi, lo = got_ref[n : n + NOTE // 2], got_ref[n + NOTE // 2 :]
        small = small_ref[...] + (hi.astype(f32) + lo.astype(f32))
        refs[2][...] = small
        if send_ref.shape[0] > m:
            put_small(send_ref, m, small)


class Reduction:
    def __init__(self, links, send, keep, small=None):
        self.kind = None
        self.links, self.send, self.x, self.small = links, send, keep, small
        self.plan = (
            [("core", None)]
            + [("half", p) for p in links.near]
            + [("full", p) for p in links.far]
            + [("join", p) for p in links.near[::-1]]
            + [("last", None)]
        )

    def start(self, *after):
        links = self.links
        self.kind, self.pair = self.plan.pop(0)
        if after:
            self.send, *after = beside(self.send, *after)
        self.got = links.core(self.send) if self.pair is None else links.across(self.send, self.pair)
        return after

    def end(self):
        kind, x, links = self.kind, self.x, self.links
        if kind == "last":
            return
        n, d = x.shape
        shape = jax.ShapeDtypeStruct
        late, pair = self.plan[0]
        if kind == "join":
            v, outs = links.signs[self.pair], [shape((2 * n, d), bf16)]
        else:
            v = links.signs[pair] if late == "half" else links.any
            m = n // 2 if late == "half" else n
            more = NOTE if self.small is not None and late in ("half", "full") else 0
            outs = [shape((m + more if late in ("half", "full") else NOTE, d), bf16), shape((m, d), bf16)]
        args = [v, x, self.got]
        with_small = self.small is not None and kind != "join"
        if with_small:
            args.append(self.small)
            outs.append(shape(self.small.shape, f32))
        out = pl.pallas_call(
            functools.partial(hop_kernel, kind, late, with_small),
            in_specs=[pl.BlockSpec(memory_space=pltpu.SMEM)] + [pl.BlockSpec(memory_space=pltpu.VMEM)] * (len(args) - 1),
            out_specs=[pl.BlockSpec(memory_space=pltpu.VMEM)] * len(outs),
            out_shape=outs,
            compiler_params=params(HOP_VMEM),
            cost_estimate=cost(1.0),
            name="hop",
        )(*args)
        if kind == "join":
            self.send = self.x = out[0]
            return
        self.x = out[1]
        self.send = out[0] if late in ("half", "full") else self.x
        if with_small:
            self.small = out[2]


def beside(*values):
    return lax.optimization_barrier(values)


def body(
    links, image_in, img_gains, img_shifts, img_qkv, img_out, img_up, img_down, text_in, lengths, valid,
    txt_gains, txt_shifts, txt_qkv, txt_out, txt_up, txt_down, log_scale,
):
    dp, bits = links.dp, links.bits
    pairs, txt, d = text_in.shape
    ff = txt_up.shape[1]
    tokens = pairs * txt
    scale = jnp.exp(log_scale).reshape(1)
    rep = lax.axis_index("rep").astype(jnp.int32).reshape(1)
    order = links.gather_order

    own_valid = valid.astype(f32)[None, :]
    flen = lengths.astype(f32)[:, None]

    xt = image_in.transpose(1, 0, 2)
    place = sum(links.bit(order[i]) << i for i in range(bits)).astype(jnp.int32).reshape(1)
    signs = [links.bit(pair).astype(jnp.int32).reshape(1) for pair in links.near]
    xt, flen, own_valid, scale, rep, place, *signs = beside(
        xt, flen, own_valid, scale, rep, place, *signs
    )
    links.signs = dict(zip(links.near, signs))
    links.any = rep
    other_valid = links.core(own_valid)
    image_args = (valid[None, :], img_gains, img_shifts, img_qkv, img_out, img_up, img_down)
    emb = image_embed(xt, *image_args, 0, pairs, True)
    text_args = (txt_gains, txt_shifts, txt_qkv, txt_out, txt_up, txt_down)
    text_x, emb = beside(text_in.reshape(tokens, d), emb)
    steps, pieces = list(order), 4
    a, held = emb[None], []
    for piece in range(pieces):
        if steps:
            got = links.across(a, steps.pop(0))
        held = list(text_forward(piece, pieces, held, text_x, flen, *text_args, txt))
        if steps:
            text_x, got, held[-1] = beside(text_x, got, held[-1])
            a = jnp.concatenate([a, got], 0)
    while steps:
        got = links.across(a, steps.pop(0))
        if steps:
            a = jnp.concatenate([a, got], 0)
    n1, qkv, probs, att, n2, slope, stat, hpool, u, text_emb = held

    scores, images, col, okay, row = pair_scores(
        place, text_emb, links.core(text_emb), own_valid, other_valid, scale, a, got
    )
    swap = links.core(row)
    for pair in order[:-1]:
        col = col + links.across(col, pair)
    col_got = links.across(col, order[-1])
    part, other, sums = pair_gradients(dp, scale, scores, images, col, col_got, okay, row, swap, text_emb, emb)
    back = links.core(other)

    ffn_send, ffn_keep, gd, dh = backward_up(scale, rep, part, back, row, swap, emb, u, flen, hpool, n2, slope, txt_down, txt)
    first = Reduction(links, ffn_send, ffn_keep)
    first.start()
    gmid, datt, dwo, gain2 = backward_middle(
        gd, dh, flen, n2, slope, stat, att, txt_gains, txt_shifts, txt_up, txt_out, txt
    )
    held = []
    for piece in range(2):
        datt, first.got, *held = beside(datt, first.got, *held)
        first.end()
        first.start()
        held = list(backward_attention(
            piece, 2, held, rep, datt, qkv, probs, n1, dwo, gain2, sums, txt_gains, txt_shifts, txt_qkv
        ))
    gq, att_send, att_keep, small = held
    att_send, first.got = beside(att_send, first.got)
    second = Reduction(links, att_send, att_keep, small)
    dx, done = [], []

    def inputs(piece, stream):
        gq_now, stream.x = beside(gq, stream.x)
        dx[:] = [backward_input(piece, 2, dx, gq_now, gmid, n1, stat, txt_gains, txt_shifts, txt_qkv)]

    other = {first: second, second: first}
    far = len(links.far)
    for act, stream in (
        [("s", second), ("e", first), ("s", first), ("e", second), ("s", second), ("i", 0), ("e", second), ("s", second)]
        + [("e", first), ("s", first), ("e", second), ("s", second), ("i", 1), ("e", second), ("s", second)]
        + [("e", first), ("s", first), ("e", second), ("s", second), ("e", first), ("s", first)] * (far > 0)
    ):
        if act == "i":
            inputs(stream, second)
        elif act == "e":
            stream.end()
        elif stream.plan:
            if stream is second and second.kind is None:
                stream.start()
            else:
                other[stream].x, *dx[:] = stream.start(other[stream].x, *dx)
    while first.plan or second.plan:
        for stream in (second, first):
            if stream.plan:
                stream.end()
                stream.start()
    grad_down, grad_up = finish(
        rep, first.x, first.got, [(ff, d), (d, ff)], [(0, ff, 0, 0, 0)] + [(ff + i * d, d, 1, 0, i * d) for i in range(ff // d)]
    )
    grad_qkv, grad_out = finish(
        rep, second.x, second.got, [(d, 3 * d), (d, d)], [(i * d, d, 0, 0, i * d) for i in range(3)] + [(3 * d, d, 1, 0, 0)]
    )
    small, dx = second.small, dx[0]
    return (
        small[4, 0],
        small[0:2],
        small[2:4],
        grad_qkv,
        grad_out,
        grad_up,
        grad_down,
        small[5, 0],
        dx.reshape(pairs, txt, d),
    )


def solution(mesh):
    both = ("dp", "rep")
    deep = P(both, None, None)
    in_specs = (deep,) + (P(),) * 6 + (deep, P(both), P(both)) + (P(),) * 7
    out_specs = (P(),) * 8 + (deep,)
    return jax.shard_map(
        functools.partial(body, Links(mesh)), mesh=mesh, in_specs=in_specs, out_specs=out_specs, check_vma=False
    )
```
